32 devices in a mesh: grp: 4 (over y, x), mem: 8 (over z, core).
Axes of the slice: x: 2, y: 2, z: 4, core: 2. Of those that a mesh axis runs over, the one named last changes fastest.
Arguments:
- activations: bfloat16 [1024, 32, 4096], P(('grp', 'mem')), may hold values from -6 to 6
- out_grads: bfloat16 [1024, 32, 4096], P(('grp', 'mem')), may hold values from -6 to 6
- proj_in: bfloat16 [4096, 64], replicated, may hold values from -1 to 1
- proj_out: bfloat16 [4096, 64], replicated, may hold values from -1 to 1
- basis_in: float32 [64, 64], replicated, may hold values from -1 to 1
- basis_out: float32 [64, 64], replicated, may hold values from -1 to 1
- eigen: float32 [64, 64], replicated, may hold values from 0.05 to 12
- doc_ids: int32 [1024], P(('grp', 'mem')), may hold values from 0 to 255
Outputs:
- scores: float32 [1024, 1024], P(('grp', 'mem'))
The draws below stay inside these ranges and needn't reach their ends.
All inputs are finite; a program needn't handle non-finite values.
Results may differ from the reference program's by a relative error of at most 0.0077.
Values may be sent and summed in bfloat16 or wider, within the bound.
No kernel may reach another device: no remote copies, remote signals or barrier semaphores. Data moves between devices by JAX's collectives and lax.ppermute only.
A program may use at most 192 MiB of HBM per device.

```python
import math
import jax
import jax.numpy as jnp
from jax import lax

D = 4096
R = 64
TOK_EX = 32
E_DEV = 32
EXAMPLES = 1024


def ekfac_common(key):
    key_list = [jax.random.fold_in(key, 7001 + offset) for offset in range(8)]
    basis_in = jnp.linalg.qr(jax.random.normal(key_list[0], (R, R), jnp.float32))[0]
    basis_out = jnp.linalg.qr(jax.random.normal(key_list[1], (R, R), jnp.float32))[0]
    proj_in = jnp.clip(jax.random.normal(key_list[2], (D, R), jnp.float32), -5.0, 5.0) / math.sqrt(D)
    proj_out = jnp.clip(jax.random.normal(key_list[3], (D, R), jnp.float32), -5.0, 5.0) / math.sqrt(D)
    proj_in = proj_in.astype(jnp.bfloat16).astype(jnp.float32)
    proj_out = proj_out.astype(jnp.bfloat16).astype(jnp.float32)
    target_in = jnp.exp(jax.random.uniform(key_list[4], (R,), jnp.float32, math.log(0.3), math.log(3.0)))
    target_out = jnp.exp(jax.random.uniform(key_list[5], (R,), jnp.float32, math.log(0.3), math.log(3.0)))
    correction = jnp.exp(jax.random.uniform(key_list[6], (R, R), jnp.float32, math.log(0.8), math.log(1.25)))
    return (basis_in, basis_out, proj_in, proj_out, target_in, target_out, correction)


def side_map(projection, eigenbasis):
    high = lax.Precision.HIGHEST
    mapped = jnp.dot(projection, eigenbasis, precision=high)
    gram_matrix = jnp.dot(mapped.T, mapped, precision=high)
    lift_map = jnp.linalg.solve(gram_matrix, mapped.T)
    return (lift_map, jnp.diagonal(gram_matrix))


def side_variance(projection, eigenbasis, target):
    lift_map, gram_diag = side_map(projection, eigenbasis)
    return 0.25 * gram_diag + target - 0.25


def logged_rows(key, projection, eigenbasis, target, salt_value):
    lift_map, gram_diag = side_map(projection, eigenbasis)
    spread = jnp.sqrt(target - 0.25)
    base_key = jax.random.fold_in(key, salt_value)

    def block_rows(position):
        block_key = jax.random.fold_in(base_key, position)
        noise_key, coeff_key = jax.random.split(block_key)
        noise_part = jax.random.normal(noise_key, (E_DEV, TOK_EX, D), jnp.float32)
        coeffs = jax.random.normal(coeff_key, (E_DEV, TOK_EX, R), jnp.float32)
        row_block = 0.5 * noise_part + jnp.einsum('etk,kd->etd', coeffs * spread, lift_map)
        return jnp.clip(row_block, -6.0, 6.0).astype(jnp.bfloat16)
    stacked = lax.map(block_rows, jnp.arange(EXAMPLES // E_DEV, dtype=jnp.int32))
    return stacked.reshape(EXAMPLES, TOK_EX, D)


def draw_activations(key, part):
    basis_in, basis_out, proj_in, proj_out, target_in, target_out, correction = ekfac_common(key)
    return logged_rows(key, proj_in, basis_in, target_in, 8101)


def draw_out_grads(key, part):
    basis_in, basis_out, proj_in, proj_out, target_in, target_out, correction = ekfac_common(key)
    return logged_rows(key, proj_out, basis_out, target_out, 8202)


def draw_proj_in(key, part):
    common = ekfac_common(key)
    return common[2].astype(jnp.bfloat16)


def draw_proj_out(key, part):
    common = ekfac_common(key)
    return common[3].astype(jnp.bfloat16)


def draw_basis_in(key, part):
    common = ekfac_common(key)
    return common[0]


def draw_basis_out(key, part):
    common = ekfac_common(key)
    return common[1]


def draw_eigen(key, part):
    basis_in, basis_out, proj_in, proj_out, target_in, target_out, correction = ekfac_common(key)
    input_var = side_variance(proj_in, basis_in, target_in)
    output_var = side_variance(proj_out, basis_out, target_out)
    measured = output_var[:, None] * input_var[None, :] * correction
    return jnp.clip(measured, 0.05, 12.0)


def plant(values, own_key, least, top_value):
    spot = [jax.random.randint(jax.random.fold_in(own_key, axis), (), 0, length) for axis, length in enumerate(values.shape)]
    longest = values.shape.index(max(values.shape))
    neighbour = spot[:longest] + [(spot[longest] + 1) % values.shape[longest]] + spot[longest + 1:]
    return values.at[tuple(spot)].set(least).at[tuple(neighbour)].set(top_value)


def setup_inputs(seed: int = 0) -> dict:
    splits = jax.random.split(jax.random.key(seed), 9)
    return {
        "activations": draw_activations(jax.random.fold_in(splits[8], 71), 0),
        "out_grads": draw_out_grads(jax.random.fold_in(splits[8], 71), 0),
        "proj_in": draw_proj_in(jax.random.fold_in(splits[8], 71), 0),
        "proj_out": draw_proj_out(jax.random.fold_in(splits[8], 71), 0),
        "basis_in": draw_basis_in(jax.random.fold_in(splits[8], 71), 0),
        "basis_out": draw_basis_out(jax.random.fold_in(splits[8], 71), 0),
        "eigen": draw_eigen(jax.random.fold_in(splits[8], 71), 0),
        "doc_ids": plant(jax.random.randint(splits[7], (EXAMPLES,), 0, EXAMPLES // 4), jax.random.fold_in(splits[7], 1), 0, (EXAMPLES // 4) - 1).astype(jnp.int32),
    }


damping = 0.1

def reference(activations, out_grads, proj_in, proj_out, basis_in, basis_out, eigen, doc_ids):
    high = lax.Precision.HIGHEST
    blocks = EXAMPLES // E_DEV

    def features(pair):
        act_block, grad_block = pair
        act_proj = jnp.dot(act_block.reshape(-1, D).astype(jnp.float32), proj_in.astype(jnp.float32), preferred_element_type=jnp.float32).astype(jnp.bfloat16)
        grad_proj = jnp.dot(grad_block.reshape(-1, D).astype(jnp.float32), proj_out.astype(jnp.float32), preferred_element_type=jnp.float32).astype(jnp.bfloat16)
        act_proj = act_proj.reshape(E_DEV, TOK_EX, R).astype(jnp.float32)
        grad_proj = grad_proj.reshape(E_DEV, TOK_EX, R).astype(jnp.float32)
        grad_feat = jnp.einsum('etr,ets->ers', grad_proj, act_proj, precision=high)
        rotated = jnp.einsum('ers,ru->eus', grad_feat, basis_out, precision=high)
        rotated = jnp.einsum('eus,sv->euv', rotated, basis_in, precision=high)
        return (rotated / jnp.sqrt(eigen + damping)).astype(jnp.bfloat16).reshape(E_DEV, R * R)
    scaled = lax.map(features, (activations.reshape(blocks, E_DEV, TOK_EX, D), out_grads.reshape(blocks, E_DEV, TOK_EX, D)))
    scaled = scaled.reshape(EXAMPLES, R * R).astype(jnp.float32)
    products = jnp.dot(scaled, scaled.T, precision=high)
    products = products * (1.0 / (TOK_EX * R))
    same_doc = doc_ids[:, None] == doc_ids[None, :]
    return jnp.where(same_doc, jnp.float32(0.0), products)
```

```python
import functools
import jax
import jax.numpy as jnp
from jax import lax
from jax.experimental import pallas as pl
from jax.experimental.pallas import tpu as pltpu
from jax.sharding import PartitionSpec as P

damping = 0.1
batch = 8


def dot_nn(a, b):
    return lax.dot_general(a, b, (((1,), (0,)), ((), ())), preferred_element_type=jnp.float32)


def dot_nt(a, b):
    return lax.dot_general(a, b, (((1,), (1,)), ((), ())), preferred_element_type=jnp.float32)


def split_two(value):
    high = value.astype(jnp.bfloat16)
    low = (value - high.astype(jnp.float32)).astype(jnp.bfloat16)
    return high, low


def feature_kernel(
    tokens, act_hbm, grad_hbm, pin_hbm, pout_hbm, bin_ref, bout_ref, eigen_ref, out_ref,
    act, grad, pin, pout, gt_ref, feat, act_sem, grad_sem, w_sem,
):
    rows = act.shape[0]
    rank = bin_ref.shape[0]
    half = rank // 2
    step_rows = batch * tokens
    steps = rows // step_rows

    copies = []
    weights = []
    for slot, (src, dst) in enumerate(((pin_hbm, pin), (pout_hbm, pout))):
        for part in range(2):
            weights.append(pltpu.make_async_copy(
                src, dst.at[pl.ds(part * rank, rank)], w_sem.at[2 * slot + part]))
    for step in range(steps):
        rng = pl.ds(step * step_rows, step_rows)
        copies.append((
            pltpu.make_async_copy(act_hbm.at[rng], act.at[rng], act_sem.at[step]),
            pltpu.make_async_copy(grad_hbm.at[rng], grad.at[rng], grad_sem.at[step]),
        ))
    weights[0].start()
    weights[1].start()
    copies[0][0].start()
    weights[2].start()
    weights[3].start()
    copies[0][1].start()
    for pair in copies[1:]:
        pair[0].start()
        pair[1].start()

    bin_hi, bin_lo = split_two(bin_ref[...])
    bin_stack = jnp.concatenate([bin_hi, bin_lo], axis=0)
    bin_stack = jnp.concatenate([bin_stack, bin_stack], axis=1)
    bout_hi, bout_lo = split_two(bout_ref[...].T)
    bout_stack = jnp.concatenate([bout_hi, bout_lo], axis=1)
    inverse = 1.0 / jnp.sqrt(eigen_ref[...] + damping)
    inverse = jnp.concatenate([inverse[:half], inverse[half:]], axis=1)
    own_token = (
        lax.broadcasted_iota(jnp.int32, (batch, step_rows), 1) // tokens
        == lax.broadcasted_iota(jnp.int32, (batch, step_rows), 0)
    )
    first_lanes = lax.broadcasted_iota(jnp.int32, (batch, 2 * rank), 1) < rank

    for step in range(steps):
        rng = pl.ds(step * step_rows, step_rows)
        if step == 0:
            weights[0].wait()
            weights[1].wait()
        copies[step][0].wait()
        act_proj = dot_nt(act[rng], pin[...]).astype(jnp.bfloat16)
        if step == 0:
            weights[2].wait()
            weights[3].wait()
        copies[step][1].wait()
        grad_proj = dot_nt(grad[rng], pout[...]).astype(jnp.bfloat16)
        act_hi, act_lo = split_two(dot_nn(act_proj, bin_stack))
        gt_ref[...] = dot_nt(bout_stack, grad_proj)
        spread_hi, spread_lo = [], []
        for u in range(rank):
            row = jnp.broadcast_to(gt_ref[pl.ds(u, 1)], (batch, step_rows))
            hi, lo = split_two(jnp.where(own_token, row, 0.0))
            spread_hi.append(hi)
            spread_lo.append(lo)
        spread_hi = jnp.concatenate(spread_hi, axis=0)
        spread_lo = jnp.concatenate(spread_lo, axis=0)
        rotated = dot_nn(spread_hi, act_hi) + dot_nn(spread_hi, act_lo) + dot_nn(spread_lo, act_hi)
        for u in range(half):
            value = jnp.where(
                first_lanes,
                rotated[u * batch:(u + 1) * batch],
                rotated[(u + half) * batch:(u + half + 1) * batch],
            ) * inverse[u:u + 1]
            feat[u, pl.ds(step * batch, batch)] = value
    out_ref[...] = feat[...].astype(jnp.bfloat16)


def features(activations, out_grads, proj_in, proj_out, basis_in, basis_out, eigen):
    examples, tokens, width = activations.shape
    rank = proj_in.shape[1]
    rows = examples * tokens
    steps = examples // batch
    hbm = pl.BlockSpec(memory_space=pl.ANY)
    vmem = pl.BlockSpec(memory_space=pltpu.VMEM)
    return pl.pallas_call(
        functools.partial(feature_kernel, tokens),
        out_shape=jax.ShapeDtypeStruct((rank // 2, examples, 2 * rank), jnp.bfloat16),
        in_specs=[hbm] * 4 + [vmem] * 3,
        out_specs=vmem,
        scratch_shapes=[
            pltpu.VMEM((rows, width), jnp.bfloat16),
            pltpu.VMEM((rows, width), jnp.bfloat16),
            pltpu.VMEM((2 * rank, width), jnp.bfloat16),
            pltpu.VMEM((2 * rank, width), jnp.bfloat16),
            pltpu.VMEM((rank, batch * tokens), jnp.float32),
            pltpu.VMEM((rank // 2, examples, 2 * rank), jnp.float32),
            pltpu.SemaphoreType.DMA((steps,)),
            pltpu.SemaphoreType.DMA((steps,)),
            pltpu.SemaphoreType.DMA((4,)),
        ],
        compiler_params=pltpu.CompilerParams(vmem_limit_bytes=60 * 2**20),
        cost_estimate=pl.CostEstimate(
            flops=4 * rows * width * rank, bytes_accessed=4 * rows * width, transcendentals=0),
        name="features",
    )(
        activations.reshape(rows, width), out_grads.reshape(rows, width),
        proj_in.T, proj_out.T, basis_in, basis_out, eigen,
    )


def product_kernel(groups, members, grp_axis, *refs):
    blocks, out_ref, stack = refs[:groups], refs[groups], refs[groups + 1]
    total, examples, lanes = blocks[0].shape
    depth = total // members
    me = lax.axis_index(grp_axis)
    for block in range(groups):
        for member in range(members):
            for part in range(depth):
                stack[pl.ds(member * examples, examples), pl.ds(part * lanes, lanes)] = (
                    blocks[block][member * depth + part])
        if block == 0:
            own = stack[...]
        value = dot_nt(own, stack[...]).astype(jnp.bfloat16)
        value = value.reshape(members, examples, members * examples)
        start = pl.multiple_of((me ^ block) * (members * examples), members * examples)
        out_ref[:, :, pl.ds(start, members * examples)] = value


def products(blocks, members, grp_axis):
    groups = len(blocks)
    total, examples, lanes = blocks[0].shape
    depth = total // members
    vmem = pl.BlockSpec(memory_space=pltpu.VMEM)
    count = members * examples
    return pl.pallas_call(
        functools.partial(product_kernel, groups, members, grp_axis),
        out_shape=jax.ShapeDtypeStruct((members, examples, groups * count), jnp.bfloat16),
        in_specs=[vmem] * groups,
        out_specs=vmem,
        scratch_shapes=[pltpu.VMEM((count, depth * lanes), jnp.bfloat16)],
        compiler_params=pltpu.CompilerParams(vmem_limit_bytes=40 * 2**20),
        cost_estimate=pl.CostEstimate(
            flops=2 * count * count * groups * depth * lanes,
            bytes_accessed=4 * count * count * groups, transcendentals=0),
        name="products",
    )(*blocks)


def on_device(members, groups, activations, out_grads, proj_in, proj_out, basis_in, basis_out, eigen, doc_ids):
    examples, tokens, width = activations.shape
    rank = proj_in.shape[1]
    factor = 1.0 / (tokens * rank)
    devices = members * groups
    all_ids = lax.all_to_all(
        jnp.broadcast_to(doc_ids[None, :], (devices, examples)), ("grp", "mem"), 0, 0, tiled=True
    ).reshape(1, -1)
    feat = features(activations, out_grads, proj_in, proj_out, basis_in, basis_out, eigen)
    slab = lax.all_to_all(feat, "mem", 0, 0, tiled=True)
    blocks = [slab] + [
        lax.ppermute(slab, "grp", [(g, g ^ step) for g in range(groups)]) for step in range(1, groups)
    ]
    partial = products(blocks, members, "grp")
    parts = lax.all_to_all(partial, "mem", 0, 0, tiled=True)
    scores = jnp.sum(parts.astype(jnp.float32), axis=0) * factor
    return jnp.where(doc_ids[:, None] == all_ids, jnp.float32(0.0), scores)


def solution(mesh):
    return jax.shard_map(
        functools.partial(on_device, mesh.shape["mem"], mesh.shape["grp"]),
        mesh=mesh,
        in_specs=(
            P(("grp", "mem"), None, None),
            P(("grp", "mem"), None, None),
            P(),
            P(),
            P(),
            P(),
            P(),
            P(("grp", "mem")),
        ),
        out_specs=P(("grp", "mem"), None),
        check_vma=False,
    )
```

```python
import functools
import jax
import jax.numpy as jnp
from jax import lax
from jax.experimental import pallas as pl
from jax.experimental.pallas import tpu as pltpu
from jax.sharding import PartitionSpec as P

damping = 0.1
batch = 8
cores = 2


def dot_nn(a, b):
    return lax.dot_general(a, b, (((1,), (0,)), ((), ())), preferred_element_type=jnp.float32)


def dot_nt(a, b):
    return lax.dot_general(a, b, (((1,), (1,)), ((), ())), preferred_element_type=jnp.float32)


def split_two(value):
    high = value.astype(jnp.bfloat16)
    low = (value - high.astype(jnp.float32)).astype(jnp.bfloat16)
    return high, low


def feature_kernel(
    tokens, slices, act_hbm, grad_hbm, pin_hbm, pout_hbm, bin_ref, bout_ref, eigen_ref, *refs
):
    out_refs = refs[:slices]
    act, grad, pin, pout, act_proj, grad_proj, gt_ref, feat, act_sem, grad_sem, w_sem = refs[slices:]
    rows = act.shape[0]
    rank = bin_ref.shape[0]
    half = rank // 2
    step_rows = batch * tokens
    steps = rows // step_rows

    def step_copies(step):
        rng = pl.ds(pl.multiple_of(step * step_rows, step_rows), step_rows)
        return (
            pltpu.make_async_copy(act_hbm.at[rng], act.at[rng], act_sem.at[step]),
            pltpu.make_async_copy(grad_hbm.at[rng], grad.at[rng], grad_sem.at[step]),
        )

    weights = [
        pltpu.make_async_copy(pin_hbm, pin, w_sem.at[0]),
        pltpu.make_async_copy(pout_hbm, pout, w_sem.at[1]),
    ]
    for copy in weights:
        copy.start()
    for step in range(steps):
        for copy in step_copies(step):
            copy.start()

    bin_hi, bin_lo = split_two(jnp.concatenate([bin_ref[...], bin_ref[...]], axis=1))
    bout_hi, bout_lo = split_two(bout_ref[...].T)
    inverse = 1.0 / jnp.sqrt(eigen_ref[...] + damping)
    inverse = jnp.concatenate([inverse[:half], inverse[half:]], axis=1)
    own_token = (
        lax.broadcasted_iota(jnp.int32, (batch, step_rows), 1) // tokens
        == lax.broadcasted_iota(jnp.int32, (batch, step_rows), 0)
    )
    first_lanes = lax.broadcasted_iota(jnp.int32, (batch, 2 * rank), 1) < rank
    for copy in weights:
        copy.wait()

    def project(step):
        for copy in step_copies(step):
            copy.wait()
        rng = pl.ds(pl.multiple_of(step * step_rows, step_rows), step_rows)
        return (
            dot_nt(act[rng], pin[...]).astype(jnp.bfloat16),
            dot_nt(grad[rng], pout[...]).astype(jnp.bfloat16),
        )

    def rotate(step, act_part, grad_part):
        act_hi, act_lo = split_two(dot_nn(act_part, bin_hi) + dot_nn(act_part, bin_lo))
        gt_ref[...] = dot_nt(bout_hi, grad_part) + dot_nt(bout_lo, grad_part)
        spread_hi, spread_lo = [], []
        for u in range(rank):
            row = jnp.broadcast_to(gt_ref[pl.ds(u, 1)], (batch, step_rows))
            hi, lo = split_two(jnp.where(own_token, row, 0.0))
            spread_hi.append(hi)
            spread_lo.append(lo)
        spread_hi = jnp.concatenate(spread_hi, axis=0)
        spread_lo = jnp.concatenate(spread_lo, axis=0)
        wide = dot_nn(spread_hi, jnp.concatenate([act_hi, act_lo], axis=1))
        rotated = wide[:, :2 * rank] + wide[:, 2 * rank:] + dot_nn(spread_lo, act_hi)
        start = pl.multiple_of(step * batch, batch)
        for u in range(half):
            value = jnp.where(
                first_lanes,
                rotated[u * batch:(u + 1) * batch],
                rotated[(u + half) * batch:(u + half + 1) * batch],
            ) * inverse[u:u + 1]
            feat[u, pl.ds(start, batch)] = value

    act_proj[...], grad_proj[...] = project(0)

    def body(step, carry):
        act_part, grad_part = act_proj[...], grad_proj[...]
        act_next, grad_next = project(step)
        rotate(step - 1, act_part, grad_part)
        act_proj[...] = act_next
        grad_proj[...] = grad_next
        return carry

    lax.fori_loop(1, steps, body, 0)
    rotate(steps - 1, act_proj[...], grad_proj[...])
    depth = half // slices
    me = lax.axis_index("mem") // cores
    for index in range(slices):
        start = (me ^ index) * depth
        out_refs[index][...] = feat[pl.ds(start, depth)].astype(jnp.bfloat16)


def features(slices, activations, out_grads, proj_in, proj_out, basis_in, basis_out, eigen):
    examples, tokens, width = activations.shape
    rank = proj_in.shape[1]
    rows = examples * tokens
    steps = examples // batch
    half = rank // 2
    hbm = pl.BlockSpec(memory_space=pl.ANY)
    vmem = pl.BlockSpec(memory_space=pltpu.VMEM)
    return pl.pallas_call(
        functools.partial(feature_kernel, tokens, slices),
        out_shape=[
            jax.ShapeDtypeStruct((half // slices, examples, 2 * rank), jnp.bfloat16)
        ] * slices,
        in_specs=[hbm] * 4 + [vmem] * 3,
        out_specs=[vmem] * slices,
        scratch_shapes=[
            pltpu.VMEM((rows, width), jnp.bfloat16),
            pltpu.VMEM((rows, width), jnp.bfloat16),
            pltpu.VMEM((rank, width), jnp.bfloat16),
            pltpu.VMEM((rank, width), jnp.bfloat16),
            pltpu.VMEM((batch * tokens, rank), jnp.bfloat16),
            pltpu.VMEM((batch * tokens, rank), jnp.bfloat16),
            pltpu.VMEM((rank, batch * tokens), jnp.float32),
            pltpu.VMEM((half, examples, 2 * rank), jnp.float32),
            pltpu.SemaphoreType.DMA((steps,)),
            pltpu.SemaphoreType.DMA((steps,)),
            pltpu.SemaphoreType.DMA((2,)),
        ],
        compiler_params=pltpu.CompilerParams(vmem_limit_bytes=60 * 2**20),
        cost_estimate=pl.CostEstimate(
            flops=4 * rows * width * rank, bytes_accessed=4 * rows * width, transcendentals=0),
        name="features",
    )(
        activations.reshape(rows, width), out_grads.reshape(rows, width),
        proj_in.T, proj_out.T, basis_in, basis_out, eigen,
    )


def product_kernel(groups, slices, pieces, *refs):
    runs = slices // pieces
    columns = refs[:groups * runs]
    others = refs[groups * runs:(groups + 1) * runs]
    outs = refs[(groups + 1) * runs:(groups + 1) * runs + slices * cores]
    column_stack, row_stack, result = refs[(groups + 1) * runs + slices * cores:]
    depth = columns[0].shape[0] // pieces
    _, examples, lanes = columns[0].shape
    grp = lax.axis_index("grp")
    mem = lax.axis_index("mem")
    pair, core = mem // cores, mem % cores

    def place(stack, row, ref, piece):
        start = pl.multiple_of(row * examples, examples)
        for part in range(depth):
            stack[pl.ds(start, examples), pl.ds(part * lanes, lanes)] = ref[piece * depth + part]

    for run in range(runs):
        for piece in range(pieces):
            place_of = pair ^ (run * pieces + piece)
            for group in range(groups):
                place(column_stack, (grp ^ group) * slices + place_of, columns[group * runs + run], piece)
            place(row_stack, place_of * cores + core, columns[run], piece)
            place(row_stack, place_of * cores + (core ^ 1), others[run], piece)
    result[...] = dot_nt(row_stack[...], column_stack[...]).astype(jnp.bfloat16)
    for index in range(slices * cores):
        start = pl.multiple_of((mem ^ index) * examples, examples)
        outs[index][...] = result[pl.ds(start, examples)]


def products(columns, others, groups, slices, pieces):
    depth = columns[0].shape[0] // pieces
    _, examples, lanes = columns[0].shape
    vmem = pl.BlockSpec(memory_space=pltpu.VMEM)
    rows, cols = slices * cores * examples, groups * slices * examples
    return pl.pallas_call(
        functools.partial(product_kernel, groups, slices, pieces),
        out_shape=[jax.ShapeDtypeStruct((examples, cols), jnp.bfloat16)] * (slices * cores),
        in_specs=[vmem] * (len(columns) + len(others)),
        out_specs=[vmem] * (slices * cores),
        scratch_shapes=[
            pltpu.VMEM((cols, depth * lanes), jnp.bfloat16),
            pltpu.VMEM((rows, depth * lanes), jnp.bfloat16),
            pltpu.VMEM((rows, cols), jnp.bfloat16),
        ],
        compiler_params=pltpu.CompilerParams(vmem_limit_bytes=40 * 2**20),
        cost_estimate=pl.CostEstimate(
            flops=2 * rows * cols * depth * lanes, bytes_accessed=4 * rows * cols, transcendentals=0),
        name="products",
    )(*columns, *others)


def finish_kernel(slices, factor, own_ids_ref, all_ids_ref, *refs):
    parts, out_ref = refs[:-1], refs[-1]
    examples, cols = parts[0].shape
    core = lax.axis_index("mem") % cores
    lane = lax.broadcasted_iota(jnp.int32, (examples, 128), 1)
    own = lane // examples % cores
    own_ids = own_ids_ref[...]
    for tile in range(cols // 128):
        rng = pl.ds(tile * 128, 128)
        same = sum(parts[cores * index][:, rng].astype(jnp.float32) for index in range(slices))
        other = sum(parts[cores * index + 1][:, rng].astype(jnp.float32) for index in range(slices))
        first = jnp.where(core == 0, same, other)
        second = jnp.where(core == 0, other, same)
        for side in range(cores):
            value = jnp.zeros((examples, 128), jnp.float32)
            for quarter in range(128 // examples):
                source = side * (64 // examples) + quarter // cores
                moved = second if quarter % cores else first
                shift = (quarter - source) * examples % 128
                if shift:
                    moved = pltpu.roll(moved, shift, 1)
                value = jnp.where(lane // examples == quarter, moved, value)
            out_rng = pl.ds(tile * 256 + side * 128, 128)
            keep = own_ids != all_ids_ref[:, out_rng]
            out_ref[:, out_rng] = jnp.where(keep, value * factor, 0.0)


def finish(parts, own_ids, all_ids, slices, factor):
    examples, cols = parts[0].shape
    vmem = pl.BlockSpec(memory_space=pltpu.VMEM)
    return pl.pallas_call(
        functools.partial(finish_kernel, slices, factor),
        out_shape=jax.ShapeDtypeStruct((examples, cores * cols), jnp.float32),
        in_specs=[vmem] * (2 + len(parts)),
        out_specs=vmem,
        compiler_params=pltpu.CompilerParams(vmem_limit_bytes=40 * 2**20),
        cost_estimate=pl.CostEstimate(
            flops=examples * cols * len(parts), bytes_accessed=8 * examples * cols, transcendentals=0),
        name="finish",
    )(own_ids, all_ids, *parts)


def swap(value, axis, size, distance):
    return lax.ppermute(value, axis, [(place, place ^ distance) for place in range(size)])


def gather_groups(piece, groups, low_first):
    held = [piece]
    for distance in range(1, groups):
        low = distance & -distance
        high = 1 << (distance.bit_length() - 1)
        bit = low if low_first else high
        held.append(swap(held[distance ^ bit], "grp", groups, bit))
    return held


def on_device(members, groups, activations, out_grads, proj_in, proj_out, basis_in, basis_out, eigen, doc_ids):
    examples, tokens, width = activations.shape
    rank = proj_in.shape[1]
    factor = 1.0 / (tokens * rank)
    devices = members * groups
    slices = members // cores
    runs = 2
    pieces = slices // runs
    all_ids = lax.all_to_all(
        jnp.broadcast_to(doc_ids[None, :], (devices, examples)), ("grp", "mem"), 0, 0, tiled=True
    ).reshape(1, -1)
    feat = features(slices, activations, out_grads, proj_in, proj_out, basis_in, basis_out, eigen)
    got = [feat[0]] + [swap(feat[index], "mem", members, cores * index) for index in range(1, slices)]
    columns = [[None] * runs for _ in range(groups)]
    others = []
    for run in range(runs):
        slab = jnp.concatenate(got[run * pieces:(run + 1) * pieces], axis=0)
        for group, held in enumerate(gather_groups(slab, groups, run % 2 == 0)):
            columns[group][run] = held
        others.append(swap(slab, "mem", members, 1))
    flat = [columns[group][run] for group in range(groups) for run in range(runs)]
    partial = products(flat, others, groups, slices, pieces)
    parts = [partial[0]] + [swap(partial[index], "mem", members, index) for index in range(1, members)]
    return finish(parts, doc_ids[:, None], all_ids, slices, factor)


def solution(mesh):
    return jax.shard_map(
        functools.partial(on_device, mesh.shape["mem"], mesh.shape["grp"]),
        mesh=mesh,
        in_specs=(
            P(("grp", "mem"), None, None),
            P(("grp", "mem"), None, None),
            P(),
            P(),
            P(),
            P(),
            P(),
            P(("grp", "mem")),
        ),
        out_specs=P(("grp", "mem"), None),
        check_vma=False,
    )
```

```python
import functools
import jax
import jax.numpy as jnp
from jax import lax
from jax.experimental import pallas as pl
from jax.experimental.pallas import tpu as pltpu
from jax.sharding import PartitionSpec as P

damping = 0.1
batch = 8
id_rows = 16
cores = 2


def dot_nn(a, b):
    return lax.dot_general(a, b, (((1,), (0,)), ((), ())), preferred_element_type=jnp.float32)


def dot_nt(a, b):
    return lax.dot_general(a, b, (((1,), (1,)), ((), ())), preferred_element_type=jnp.float32)


def split_two(value):
    high = value.astype(jnp.bfloat16)
    low = (value - high.astype(jnp.float32)).astype(jnp.bfloat16)
    return high, low


def feature_kernel(
    tokens, slices, act_hbm, grad_hbm, pin_hbm, pout_hbm, bin_ref, bout_ref, eigen_ref, ids_ref, *refs
):
    out_refs = refs[:slices]
    act, grad, pin, pout, act_proj, grad_proj, gt_ref, feat, act_sem, grad_sem, w_sem = refs[slices:]
    rows, width = act.shape
    rank = bin_ref.shape[0]
    half = rank // 2
    step_rows = batch * tokens
    steps = rows // step_rows
    examples = feat.shape[1]

    def step_copies(step):
        rng = pl.ds(pl.multiple_of(step * step_rows, step_rows), step_rows)
        return (
            pltpu.make_async_copy(act_hbm.at[rng], act.at[rng], act_sem.at[step]),
            pltpu.make_async_copy(grad_hbm.at[rng], grad.at[rng], grad_sem.at[step]),
        )

    weights = [
        pltpu.make_async_copy(pin_hbm, pin, w_sem.at[0]),
        pltpu.make_async_copy(pout_hbm, pout, w_sem.at[1]),
    ]
    for copy in weights:
        copy.start()
    for step in range(steps):
        for copy in step_copies(step):
            copy.start()

    bin_hi, bin_lo = split_two(jnp.concatenate([bin_ref[...], bin_ref[...]], axis=1))
    bout_hi, bout_lo = split_two(bout_ref[...].T)
    inverse = 1.0 / jnp.sqrt(eigen_ref[...] + damping)
    inverse = jnp.concatenate([inverse[:half], inverse[half:]], axis=1)
    own_token = (
        lax.broadcasted_iota(jnp.int32, (batch, step_rows), 1) // tokens
        == lax.broadcasted_iota(jnp.int32, (batch, step_rows), 0)
    )
    first_lanes = lax.broadcasted_iota(jnp.int32, (batch, 2 * rank), 1) < rank
    ids = jnp.concatenate([ids_ref[...]] * (2 * rank // examples), axis=1)
    place = lax.broadcasted_iota(jnp.int32, (id_rows, 2 * rank), 0) % 4
    digits = (jnp.broadcast_to(ids, (id_rows, 2 * rank)) >> (place * 8)) & 255
    digits = digits.astype(jnp.float32).astype(jnp.bfloat16)
    for copy in weights:
        copy.wait()

    def project(step):
        for copy in step_copies(step):
            copy.wait()
        rng = pl.ds(pl.multiple_of(step * step_rows, step_rows), step_rows)
        first, second = pl.ds(0, width // 2), pl.ds(width // 2, width // 2)
        return (
            (dot_nt(act[rng, first], pin[:, first]) + dot_nt(act[rng, second], pin[:, second])
             ).astype(jnp.bfloat16),
            (dot_nt(grad[rng, first], pout[:, first]) + dot_nt(grad[rng, second], pout[:, second])
             ).astype(jnp.bfloat16),
        )

    def rotate(step, act_part, grad_part):
        act_hi, act_lo = split_two(dot_nn(act_part, bin_hi) + dot_nn(act_part, bin_lo))
        gt_ref[...] = dot_nt(bout_hi, grad_part) + dot_nt(bout_lo, grad_part)
        spread_hi, spread_lo = [], []
        for u in range(rank):
            row = jnp.broadcast_to(gt_ref[pl.ds(u, 1)], (batch, step_rows))
            hi, lo = split_two(jnp.where(own_token, row, 0.0))
            spread_hi.append(hi)
            spread_lo.append(lo)
        spread_hi = jnp.concatenate(spread_hi, axis=0)
        spread_lo = jnp.concatenate(spread_lo, axis=0)
        wide = dot_nn(spread_hi, jnp.concatenate([act_hi, act_lo], axis=1))
        rotated = wide[:, :2 * rank] + wide[:, 2 * rank:] + dot_nn(spread_lo, act_hi)
        start = pl.multiple_of(step * batch, batch)
        for u in range(half):
            value = jnp.where(
                first_lanes,
                rotated[u * batch:(u + 1) * batch],
                rotated[(u + half) * batch:(u + half + 1) * batch],
            ) * inverse[u:u + 1]
            feat[u, pl.ds(start, batch)] = value

    act_proj[...], grad_proj[...] = project(0)

    def body(step, carry):
        act_part, grad_part = act_proj[...], grad_proj[...]
        act_next, grad_next = project(step)
        rotate(step - 1, act_part, grad_part)
        act_proj[...] = act_next
        grad_proj[...] = grad_next
        return carry

    lax.fori_loop(1, steps, body, 0)
    rotate(steps - 1, act_proj[...], grad_proj[...])
    depth = half // slices
    me = lax.axis_index("mem") // cores
    for index in range(slices):
        start = (me ^ index) * depth
        piece = feat[pl.ds(start, depth)].astype(jnp.bfloat16)
        out_refs[index][pl.ds(0, depth * examples)] = piece.reshape(depth * examples, 2 * rank)
        out_refs[index][pl.ds(depth * examples, id_rows)] = digits


def features(slices, activations, out_grads, proj_in, proj_out, basis_in, basis_out, eigen, doc_ids):
    examples, tokens, width = activations.shape
    rank = proj_in.shape[1]
    rows = examples * tokens
    steps = examples // batch
    half = rank // 2
    hbm = pl.BlockSpec(memory_space=pl.ANY)
    vmem = pl.BlockSpec(memory_space=pltpu.VMEM)
    return pl.pallas_call(
        functools.partial(feature_kernel, tokens, slices),
        out_shape=[
            jax.ShapeDtypeStruct((half // slices * examples + id_rows, 2 * rank), jnp.bfloat16)
        ] * slices,
        in_specs=[hbm] * 4 + [vmem] * 4,
        out_specs=[vmem] * slices,
        scratch_shapes=[
            pltpu.VMEM((rows, width), jnp.bfloat16),
            pltpu.VMEM((rows, width), jnp.bfloat16),
            pltpu.VMEM((rank, width), jnp.bfloat16),
            pltpu.VMEM((rank, width), jnp.bfloat16),
            pltpu.VMEM((batch * tokens, rank), jnp.bfloat16),
            pltpu.VMEM((batch * tokens, rank), jnp.bfloat16),
            pltpu.VMEM((rank, batch * tokens), jnp.float32),
            pltpu.VMEM((half, examples, 2 * rank), jnp.float32),
            pltpu.SemaphoreType.DMA((steps,)),
            pltpu.SemaphoreType.DMA((steps,)),
            pltpu.SemaphoreType.DMA((2,)),
        ],
        compiler_params=pltpu.CompilerParams(vmem_limit_bytes=60 * 2**20),
        cost_estimate=pl.CostEstimate(
            flops=4 * rows * width * rank, bytes_accessed=4 * rows * width, transcendentals=0),
        name="features",
    )(
        activations.reshape(rows, width), out_grads.reshape(rows, width),
        proj_in.T, proj_out.T, basis_in, basis_out, eigen, doc_ids.reshape(1, examples),
    )


def reverse_bits(value, count):
    return sum(((value >> bit) & 1) << (count - 1 - bit) for bit in range(count))


def product_kernel(groups, slices, pieces, examples, *refs):
    runs = slices // pieces
    columns = refs[:groups * runs]
    others = refs[groups * runs:(groups + 1) * runs]
    outs = refs[(groups + 1) * runs:(groups + 1) * runs + slices]
    ids_ref, column_stack, row_stack, result = refs[(groups + 1) * runs + slices:]
    piece_rows, lanes = columns[0].shape
    piece_rows = piece_rows // pieces
    depth = (piece_rows - id_rows) // examples
    cols = column_stack.shape[0]
    grp = lax.axis_index("grp")
    mem = lax.axis_index("mem")
    pair, core = mem // cores, mem % cores

    def place(stack, row, ref, piece):
        start = pl.multiple_of(row * examples, examples)
        for part in range(depth):
            stack[pl.ds(start, examples), pl.ds(part * lanes, lanes)] = (
                ref[pl.ds(piece * piece_rows + part * examples, examples)])

    block = lax.broadcasted_iota(jnp.int32, (id_rows, cols), 1) // examples
    digits = jnp.zeros((id_rows, cols), jnp.float32)
    for run in range(runs):
        for piece in range(pieces):
            place_of = pair ^ (run * pieces + piece)
            for slot in range(groups):
                distance = jnp.where(
                    core == 0, slot, reverse_bits(slot, groups.bit_length() - 1))
                column = (grp ^ distance) * slices + place_of
                ref = columns[slot * runs + run]
                place(column_stack, column, ref, piece)
                some = ref[pl.ds((piece + 1) * piece_rows - id_rows, id_rows)].astype(jnp.float32)
                some = jnp.concatenate([some] * (cols // lanes), axis=1)
                digits = jnp.where(block == column, some, digits)
            place(row_stack, place_of * cores + core, columns[run], piece)
            place(row_stack, place_of * cores + (core ^ 1), others[run], piece)
    result[...] = dot_nt(row_stack[...], column_stack[...]).astype(jnp.bfloat16)
    for index in range(slices):
        start = pl.multiple_of((pair ^ index) * (cores * examples), cores * examples)
        outs[index][...] = result[pl.ds(start, cores * examples)]
    ids_ref[pl.ds(0, 1)] = digits[0:1] + digits[1:2] * 256.0
    ids_ref[pl.ds(1, 1)] = digits[2:3] + digits[3:4] * 256.0


def products(columns, others, groups, slices, pieces, examples):
    piece_rows, lanes = columns[0].shape
    depth = (piece_rows // pieces - id_rows) // examples
    vmem = pl.BlockSpec(memory_space=pltpu.VMEM)
    rows, cols = slices * cores * examples, groups * slices * examples
    return pl.pallas_call(
        functools.partial(product_kernel, groups, slices, pieces, examples),
        out_shape=[jax.ShapeDtypeStruct((cores * examples, cols), jnp.bfloat16)] * slices
        + [jax.ShapeDtypeStruct((2, cols), jnp.float32)],
        in_specs=[vmem] * (len(columns) + len(others)),
        out_specs=[vmem] * (slices + 1),
        scratch_shapes=[
            pltpu.VMEM((cols, depth * lanes), jnp.bfloat16),
            pltpu.VMEM((rows, depth * lanes), jnp.bfloat16),
            pltpu.VMEM((rows, cols), jnp.bfloat16),
        ],
        compiler_params=pltpu.CompilerParams(vmem_limit_bytes=40 * 2**20),
        cost_estimate=pl.CostEstimate(
            flops=2 * rows * cols * depth * lanes, bytes_accessed=4 * rows * cols, transcendentals=0),
        name="products",
    )(*columns, *others)


def total_kernel(slices, ids_ref, *refs):
    parts, (keep_ref, send_ref) = refs[:slices], refs[slices:]
    examples = keep_ref.shape[0]
    core = lax.axis_index("mem") % cores
    keep = pl.ds(pl.multiple_of(core * examples, examples), examples)
    send = pl.ds(pl.multiple_of((core ^ 1) * examples, examples), examples)
    keep_ref[...] = sum(part[keep].astype(jnp.float32) for part in parts)
    send_ref[pl.ds(0, examples)] = sum(part[send].astype(jnp.float32) for part in parts)
    send_ref[pl.ds(examples, 2)] = ids_ref[...]


def totals(parts, ids, examples):
    cols = parts[0].shape[1]
    vmem = pl.BlockSpec(memory_space=pltpu.VMEM)
    return pl.pallas_call(
        functools.partial(total_kernel, len(parts)),
        out_shape=[
            jax.ShapeDtypeStruct((examples, cols), jnp.float32),
            jax.ShapeDtypeStruct((examples + 8, cols), jnp.float32),
        ],
        in_specs=[vmem] * (1 + len(parts)),
        out_specs=[vmem] * 2,
        compiler_params=pltpu.CompilerParams(vmem_limit_bytes=40 * 2**20),
        cost_estimate=pl.CostEstimate(
            flops=2 * examples * cols * len(parts), bytes_accessed=8 * examples * cols, transcendentals=0),
        name="totals",
    )(ids, *parts)


def finish_kernel(factor, own_ids_ref, ids_ref, keep_ref, got_ref, out_ref):
    examples, cols = keep_ref.shape
    core = lax.axis_index("mem") % cores
    block = lax.broadcasted_iota(jnp.int32, (examples, 128), 1) // examples
    id_block = lax.broadcasted_iota(jnp.int32, (8, 128), 1) // examples
    own_low = (own_ids_ref[...] & 0xFFFF).astype(jnp.float32)
    own_high = ((own_ids_ref[...] >> 16) & 0xFFFF).astype(jnp.float32)

    def take_turns(first, second, side, block):
        value = jnp.zeros_like(first)
        for quarter in range(128 // examples):
            moved = second if quarter % cores else first
            source = side * (64 // examples) + quarter // cores
            shift = (quarter - source) * examples % 128
            if shift:
                moved = pltpu.roll(moved, shift, 1)
            value = jnp.where(block == quarter, moved, value)
        return value

    for tile in range(cols // 128):
        rng = pl.ds(tile * 128, 128)
        same, other = keep_ref[:, rng], got_ref[pl.ds(0, examples), rng]
        first, second = jnp.where(core == 0, same, other), jnp.where(core == 0, other, same)
        same_ids = [jnp.broadcast_to(ids_ref[pl.ds(row, 1), rng], (8, 128)) for row in range(2)]
        other_ids = [jnp.broadcast_to(got_ref[pl.ds(examples + row, 1), rng], (8, 128)) for row in range(2)]
        for side in range(cores):
            value = take_turns(first, second, side, block)
            low, high = [
                take_turns(
                    jnp.where(core == 0, a, b), jnp.where(core == 0, b, a), side, id_block)[0:1]
                for a, b in zip(same_ids, other_ids)
            ]
            same_doc = (own_low == low) & (own_high == high)
            out_ref[:, pl.ds(tile * 256 + side * 128, 128)] = jnp.where(same_doc, 0.0, value * factor)


def finish(own_ids, ids, keep, got, factor):
    examples, cols = keep.shape
    vmem = pl.BlockSpec(memory_space=pltpu.VMEM)
    return pl.pallas_call(
        functools.partial(finish_kernel, factor),
        out_shape=jax.ShapeDtypeStruct((examples, cores * cols), jnp.float32),
        in_specs=[vmem] * 4,
        out_specs=vmem,
        compiler_params=pltpu.CompilerParams(vmem_limit_bytes=40 * 2**20),
        cost_estimate=pl.CostEstimate(
            flops=8 * examples * cols, bytes_accessed=16 * examples * cols, transcendentals=0),
        name="finish",
    )(own_ids, ids, keep, got)


def swap(value, axis, size, distance):
    return lax.ppermute(value, axis, [(place, place ^ distance) for place in range(size)])


def gather_groups(piece, groups, members):
    bits = groups.bit_length() - 1
    held = [piece]
    for slot in range(1, groups):
        bit = 1 << (slot.bit_length() - 1)
        pairs = []
        for group in range(groups):
            for member in range(members):
                step = reverse_bits(bit, bits) if member % cores else bit
                pairs.append((group * members + member, (group ^ step) * members + member))
        held.append(lax.ppermute(held[slot ^ bit], ("grp", "mem"), pairs))
    return held


def on_device(members, groups, activations, out_grads, proj_in, proj_out, basis_in, basis_out, eigen, doc_ids):
    examples, tokens, width = activations.shape
    rank = proj_in.shape[1]
    factor = 1.0 / (tokens * rank)
    slices = members // cores
    runs = 2
    pieces = slices // runs
    feat = features(slices, activations, out_grads, proj_in, proj_out, basis_in, basis_out, eigen, doc_ids)
    got = [feat[0]] + [swap(feat[index], "mem", members, cores * index) for index in range(1, slices)]
    columns = [[None] * runs for _ in range(groups)]
    others = []
    for run in range(runs):
        slab = jnp.concatenate(got[run * pieces:(run + 1) * pieces], axis=0)
        for slot, held in enumerate(gather_groups(slab, groups, members)):
            columns[slot][run] = held
        others.append(swap(slab, "mem", members, 1))
    flat = [columns[slot][run] for slot in range(groups) for run in range(runs)]
    *partial, ids = products(flat, others, groups, slices, pieces, examples)
    parts = [partial[0]] + [swap(partial[index], "mem", members, cores * index) for index in range(1, slices)]
    keep, send = totals(parts, ids, examples)
    return finish(doc_ids[:, None], ids, keep, swap(send, "mem", members, 1), factor)


def solution(mesh):
    return jax.shard_map(
        functools.partial(on_device, mesh.shape["mem"], mesh.shape["grp"]),
        mesh=mesh,
        in_specs=(
            P(("grp", "mem"), None, None),
            P(("grp", "mem"), None, None),
            P(),
            P(),
            P(),
            P(),
            P(),
            P(("grp", "mem")),
        ),
        out_specs=P(("grp", "mem"), None),
        check_vma=False,
    )
```

```python
import functools
import jax
import jax.numpy as jnp
from jax import lax
from jax.experimental import pallas as pl
from jax.experimental.pallas import tpu as pltpu
from jax.sharding import PartitionSpec as P

damping = 0.1
batch = 8
id_rows = 16
cores = 2


def dot_nn(a, b):
    return lax.dot_general(a, b, (((1,), (0,)), ((), ())), preferred_element_type=jnp.float32)


def dot_nt(a, b):
    return lax.dot_general(a, b, (((1,), (1,)), ((), ())), preferred_element_type=jnp.float32)


def split_two(value):
    high = value.astype(jnp.bfloat16)
    low = (value - high.astype(jnp.float32)).astype(jnp.bfloat16)
    return high, low


def feature_kernel(
    tokens, slices, act_hbm, grad_hbm, pin_hbm, pout_hbm, bin_ref, bout_ref, eigen_ref, ids_ref, *refs
):
    out_refs = refs[:slices]
    act, grad, pin, pout, act_proj, grad_proj, gt_ref, feat, act_sem, grad_sem, w_sem = refs[slices:]
    rows, width = act.shape
    rank = bin_ref.shape[0]
    half = rank // 2
    step_rows = batch * tokens
    steps = rows // step_rows
    examples = feat.shape[1]

    def step_copies(step):
        rng = pl.ds(pl.multiple_of(step * step_rows, step_rows), step_rows)
        return (
            pltpu.make_async_copy(act_hbm.at[rng], act.at[rng], act_sem.at[step]),
            pltpu.make_async_copy(grad_hbm.at[rng], grad.at[rng], grad_sem.at[step]),
        )

    weights = [
        pltpu.make_async_copy(pin_hbm, pin, w_sem.at[0]),
        pltpu.make_async_copy(pout_hbm, pout, w_sem.at[1]),
    ]
    for copy in weights:
        copy.start()
    for step in range(steps):
        for priority, copy in enumerate(step_copies(step)):
            copy.start(priority=priority)

    bin_hi, bin_lo = split_two(jnp.concatenate([bin_ref[...], bin_ref[...]], axis=1))
    bout_hi, bout_lo = split_two(bout_ref[...].T)
    inverse = 1.0 / jnp.sqrt(eigen_ref[...] + damping)
    inverse = jnp.concatenate([inverse[:half], inverse[half:]], axis=1)
    own_token = (
        lax.broadcasted_iota(jnp.int32, (batch, step_rows), 1) // tokens
        == lax.broadcasted_iota(jnp.int32, (batch, step_rows), 0)
    )
    first_lanes = lax.broadcasted_iota(jnp.int32, (batch, 2 * rank), 1) < rank
    ids = jnp.concatenate([ids_ref[...]] * (2 * rank // examples), axis=1)
    place = lax.broadcasted_iota(jnp.int32, (id_rows, 2 * rank), 0) % 4
    digits = (jnp.broadcast_to(ids, (id_rows, 2 * rank)) >> (place * 8)) & 255
    digits = digits.astype(jnp.float32).astype(jnp.bfloat16)
    for copy in weights:
        copy.wait()

    def project(step):
        for copy in step_copies(step):
            copy.wait()
        rng = pl.ds(pl.multiple_of(step * step_rows, step_rows), step_rows)
        first, second = pl.ds(0, width // 2), pl.ds(width // 2, width // 2)
        return (
            (dot_nt(act[rng, first], pin[:, first]) + dot_nt(act[rng, second], pin[:, second])
             ).astype(jnp.bfloat16),
            (dot_nt(grad[rng, first], pout[:, first]) + dot_nt(grad[rng, second], pout[:, second])
             ).astype(jnp.bfloat16),
        )

    def rotate(step, act_part, grad_part):
        act_hi, act_lo = split_two(dot_nn(act_part, bin_hi) + dot_nn(act_part, bin_lo))
        gt_ref[...] = dot_nt(bout_hi, grad_part) + dot_nt(bout_lo, grad_part)
        spread_hi, spread_lo = [], []
        for u in range(rank):
            row = jnp.broadcast_to(gt_ref[pl.ds(u, 1)], (batch, step_rows))
            hi, lo = split_two(jnp.where(own_token, row, 0.0))
            spread_hi.append(hi)
            spread_lo.append(lo)
        spread_hi = jnp.concatenate(spread_hi, axis=0)
        spread_lo = jnp.concatenate(spread_lo, axis=0)
        wide = dot_nn(spread_hi, jnp.concatenate([act_hi, act_lo], axis=1))
        rotated = wide[:, :2 * rank] + wide[:, 2 * rank:] + dot_nn(spread_lo, act_hi)
        start = pl.multiple_of(step * batch, batch)
        for u in range(half):
            value = jnp.where(
                first_lanes,
                rotated[u * batch:(u + 1) * batch],
                rotated[(u + half) * batch:(u + half + 1) * batch],
            ) * inverse[u:u + 1]
            feat[u, pl.ds(start, batch)] = value

    act_proj[...], grad_proj[...] = project(0)

    def body(step, carry):
        act_part, grad_part = act_proj[...], grad_proj[...]
        act_next, grad_next = project(step)
        rotate(step - 1, act_part, grad_part)
        act_proj[...] = act_next
        grad_proj[...] = grad_next
        return carry

    lax.fori_loop(1, steps, body, 0)
    rotate(steps - 1, act_proj[...], grad_proj[...])
    depth = half // slices
    me = lax.axis_index("mem") // cores
    for index in range(slices):
        start = (me ^ index) * depth
        piece = feat[pl.ds(start, depth)].astype(jnp.bfloat16)
        out_refs[index][pl.ds(0, depth * examples)] = piece.reshape(depth * examples, 2 * rank)
        out_refs[index][pl.ds(depth * examples, id_rows)] = digits


def features(slices, activations, out_grads, proj_in, proj_out, basis_in, basis_out, eigen, doc_ids):
    examples, tokens, width = activations.shape
    rank = proj_in.shape[1]
    rows = examples * tokens
    steps = examples // batch
    half = rank // 2
    hbm = pl.BlockSpec(memory_space=pl.ANY)
    vmem = pl.BlockSpec(memory_space=pltpu.VMEM)
    return pl.pallas_call(
        functools.partial(feature_kernel, tokens, slices),
        out_shape=[
            jax.ShapeDtypeStruct((half // slices * examples + id_rows, 2 * rank), jnp.bfloat16)
        ] * slices,
        in_specs=[hbm] * 4 + [vmem] * 4,
        out_specs=[vmem] * slices,
        scratch_shapes=[
            pltpu.VMEM((rows, width), jnp.bfloat16),
            pltpu.VMEM((rows, width), jnp.bfloat16),
            pltpu.VMEM((rank, width), jnp.bfloat16),
            pltpu.VMEM((rank, width), jnp.bfloat16),
            pltpu.VMEM((batch * tokens, rank), jnp.bfloat16),
            pltpu.VMEM((batch * tokens, rank), jnp.bfloat16),
            pltpu.VMEM((rank, batch * tokens), jnp.float32),
            pltpu.VMEM((half, examples, 2 * rank), jnp.float32),
            pltpu.SemaphoreType.DMA((steps,)),
            pltpu.SemaphoreType.DMA((steps,)),
            pltpu.SemaphoreType.DMA((2,)),
        ],
        compiler_params=pltpu.CompilerParams(vmem_limit_bytes=60 * 2**20),
        cost_estimate=pl.CostEstimate(
            flops=4 * rows * width * rank, bytes_accessed=4 * rows * width, transcendentals=0),
        name="features",
    )(
        activations.reshape(rows, width), out_grads.reshape(rows, width),
        proj_in.T, proj_out.T, basis_in, basis_out, eigen, doc_ids.reshape(1, examples),
    )


def reverse_bits(value, count):
    return sum(((value >> bit) & 1) << (count - 1 - bit) for bit in range(count))


def product_kernel(groups, slices, pieces, examples, *refs):
    runs = slices // pieces
    columns = refs[:groups * runs]
    others = refs[groups * runs:(groups + 1) * runs]
    outs = refs[(groups + 1) * runs:(groups + 1) * runs + slices]
    ids_ref, column_stack, row_stack, result = refs[(groups + 1) * runs + slices:]
    piece_rows, lanes = columns[0].shape
    piece_rows = piece_rows // pieces
    depth = (piece_rows - id_rows) // examples
    cols = column_stack.shape[0]
    grp = lax.axis_index("grp")
    mem = lax.axis_index("mem")
    pair, core = mem // cores, mem % cores

    def place(stack, row, ref, piece):
        start = pl.multiple_of(row * examples, examples)
        for part in range(depth):
            stack[pl.ds(start, examples), pl.ds(part * lanes, lanes)] = (
                ref[pl.ds(piece * piece_rows + part * examples, examples)])

    block = lax.broadcasted_iota(jnp.int32, (id_rows, cols), 1) // examples
    digits = jnp.zeros((id_rows, cols), jnp.float32)
    for run in range(runs):
        for piece in range(pieces):
            place_of = pair ^ (run * pieces + piece)
            for slot in range(groups):
                distance = jnp.where(
                    core == 0, slot, reverse_bits(slot, groups.bit_length() - 1))
                column = (grp ^ distance) * slices + place_of
                ref = columns[slot * runs + run]
                place(column_stack, column, ref, piece)
                some = ref[pl.ds((piece + 1) * piece_rows - id_rows, id_rows)].astype(jnp.float32)
                some = jnp.concatenate([some] * (cols // lanes), axis=1)
                digits = jnp.where(block == column, some, digits)
            place(row_stack, place_of * cores + core, columns[run], piece)
            place(row_stack, place_of * cores + (core ^ 1), others[run], piece)
    result[...] = dot_nt(row_stack[...], column_stack[...]).astype(jnp.bfloat16)
    for index in range(slices):
        start = pl.multiple_of((pair ^ index) * (cores * examples), cores * examples)
        outs[index][...] = result[pl.ds(start, cores * examples)]
    ids_ref[pl.ds(0, 1)] = digits[0:1] + digits[1:2] * 256.0
    ids_ref[pl.ds(1, 1)] = digits[2:3] + digits[3:4] * 256.0


def products(columns, others, groups, slices, pieces, examples):
    piece_rows, lanes = columns[0].shape
    depth = (piece_rows // pieces - id_rows) // examples
    vmem = pl.BlockSpec(memory_space=pltpu.VMEM)
    rows, cols = slices * cores * examples, groups * slices * examples
    return pl.pallas_call(
        functools.partial(product_kernel, groups, slices, pieces, examples),
        out_shape=[jax.ShapeDtypeStruct((cores * examples, cols), jnp.bfloat16)] * slices
        + [jax.ShapeDtypeStruct((2, cols), jnp.float32)],
        in_specs=[vmem] * (len(columns) + len(others)),
        out_specs=[vmem] * (slices + 1),
        scratch_shapes=[
            pltpu.VMEM((cols, depth * lanes), jnp.bfloat16),
            pltpu.VMEM((rows, depth * lanes), jnp.bfloat16),
            pltpu.VMEM((rows, cols), jnp.bfloat16),
        ],
        compiler_params=pltpu.CompilerParams(vmem_limit_bytes=40 * 2**20),
        cost_estimate=pl.CostEstimate(
            flops=2 * rows * cols * depth * lanes, bytes_accessed=4 * rows * cols, transcendentals=0),
        name="products",
    )(*columns, *others)


def total_kernel(slices, ids_ref, *refs):
    parts, (keep_ref, send_ref) = refs[:slices], refs[slices:]
    examples = keep_ref.shape[0]
    core = lax.axis_index("mem") % cores
    keep = pl.ds(pl.multiple_of(core * examples, examples), examples)
    send = pl.ds(pl.multiple_of((core ^ 1) * examples, examples), examples)
    keep_ref[...] = sum(part[keep].astype(jnp.float32) for part in parts)
    send_ref[pl.ds(0, examples)] = sum(part[send].astype(jnp.float32) for part in parts)
    send_ref[pl.ds(examples, 2)] = ids_ref[...]


def totals(parts, ids, examples):
    cols = parts[0].shape[1]
    vmem = pl.BlockSpec(memory_space=pltpu.VMEM)
    return pl.pallas_call(
        functools.partial(total_kernel, len(parts)),
        out_shape=[
            jax.ShapeDtypeStruct((examples, cols), jnp.float32),
            jax.ShapeDtypeStruct((examples + 8, cols), jnp.float32),
        ],
        in_specs=[vmem] * (1 + len(parts)),
        out_specs=[vmem] * 2,
        compiler_params=pltpu.CompilerParams(vmem_limit_bytes=40 * 2**20),
        cost_estimate=pl.CostEstimate(
            flops=2 * examples * cols * len(parts), bytes_accessed=8 * examples * cols, transcendentals=0),
        name="totals",
    )(ids, *parts)


def finish_kernel(factor, own_ids_ref, ids_ref, keep_ref, got_ref, out_ref):
    examples, cols = keep_ref.shape
    core = lax.axis_index("mem") % cores
    block = lax.broadcasted_iota(jnp.int32, (examples, 128), 1) // examples
    id_block = lax.broadcasted_iota(jnp.int32, (8, 128), 1) // examples
    own_low = (own_ids_ref[...] & 0xFFFF).astype(jnp.float32)
    own_high = ((own_ids_ref[...] >> 16) & 0xFFFF).astype(jnp.float32)

    def take_turns(first, second, side, block):
        value = jnp.zeros_like(first)
        for quarter in range(128 // examples):
            moved = second if quarter % cores else first
            source = side * (64 // examples) + quarter // cores
            shift = (quarter - source) * examples % 128
            if shift:
                moved = pltpu.roll(moved, shift, 1)
            value = jnp.where(block == quarter, moved, value)
        return value

    for tile in range(cols // 128):
        rng = pl.ds(tile * 128, 128)
        same, other = keep_ref[:, rng], got_ref[pl.ds(0, examples), rng]
        first, second = jnp.where(core == 0, same, other), jnp.where(core == 0, other, same)
        same_ids = [jnp.broadcast_to(ids_ref[pl.ds(row, 1), rng], (8, 128)) for row in range(2)]
        other_ids = [jnp.broadcast_to(got_ref[pl.ds(examples + row, 1), rng], (8, 128)) for row in range(2)]
        for side in range(cores):
            value = take_turns(first, second, side, block)
            low, high = [
                take_turns(
                    jnp.where(core == 0, a, b), jnp.where(core == 0, b, a), side, id_block)[0:1]
                for a, b in zip(same_ids, other_ids)
            ]
            same_doc = (own_low == low) & (own_high == high)
            out_ref[:, pl.ds(tile * 256 + side * 128, 128)] = jnp.where(same_doc, 0.0, value * factor)


def finish(own_ids, ids, keep, got, factor):
    examples, cols = keep.shape
    vmem = pl.BlockSpec(memory_space=pltpu.VMEM)
    return pl.pallas_call(
        functools.partial(finish_kernel, factor),
        out_shape=jax.ShapeDtypeStruct((examples, cores * cols), jnp.float32),
        in_specs=[vmem] * 4,
        out_specs=vmem,
        compiler_params=pltpu.CompilerParams(vmem_limit_bytes=40 * 2**20),
        cost_estimate=pl.CostEstimate(
            flops=8 * examples * cols, bytes_accessed=16 * examples * cols, transcendentals=0),
        name="finish",
    )(own_ids, ids, keep, got)


def swap(value, axis, size, distance):
    return lax.ppermute(value, axis, [(place, place ^ distance) for place in range(size)])


def gather_groups(piece, groups, members):
    bits = groups.bit_length() - 1
    held = [piece]
    for slot in range(1, groups):
        bit = 1 << (slot.bit_length() - 1)
        pairs = []
        for group in range(groups):
            for member in range(members):
                step = reverse_bits(bit, bits) if member % cores else bit
                pairs.append((group * members + member, (group ^ step) * members + member))
        held.append(lax.ppermute(held[slot ^ bit], ("grp", "mem"), pairs))
    return held


def on_device(members, groups, activations, out_grads, proj_in, proj_out, basis_in, basis_out, eigen, doc_ids):
    examples, tokens, width = activations.shape
    rank = proj_in.shape[1]
    factor = 1.0 / (tokens * rank)
    slices = members // cores
    runs = 2
    pieces = slices // runs
    feat = features(slices, activations, out_grads, proj_in, proj_out, basis_in, basis_out, eigen, doc_ids)
    got = [feat[0]] + [swap(feat[index], "mem", members, cores * index) for index in range(1, slices)]
    columns = [[None] * runs for _ in range(groups)]
    others = []
    for run in range(runs):
        slab = jnp.concatenate(got[run * pieces:(run + 1) * pieces], axis=0)
        if run:
            slab, columns[1][run - 1] = lax.optimization_barrier((slab, columns[1][run - 1]))
        for slot, held in enumerate(gather_groups(slab, groups, members)):
            columns[slot][run] = held
        others.append(swap(slab, "mem", members, 1))
    flat = [columns[slot][run] for slot in range(groups) for run in range(runs)]
    *partial, ids = products(flat, others, groups, slices, pieces, examples)
    parts = [partial[0]] + [swap(partial[index], "mem", members, cores * index) for index in range(1, slices)]
    keep, send = totals(parts, ids, examples)
    return finish(doc_ids[:, None], ids, keep, swap(send, "mem", members, 1), factor)


def solution(mesh):
    return jax.shard_map(
        functools.partial(on_device, mesh.shape["mem"], mesh.shape["grp"]),
        mesh=mesh,
        in_specs=(
            P(("grp", "mem"), None, None),
            P(("grp", "mem"), None, None),
            P(),
            P(),
            P(),
            P(),
            P(),
            P(("grp", "mem")),
        ),
        out_specs=P(("grp", "mem"), None),
        check_vma=False,
    )
```

```python
import functools
import jax
import jax.numpy as jnp
from jax import lax
from jax.experimental import pallas as pl
from jax.experimental.pallas import tpu as pltpu
from jax.sharding import PartitionSpec as P

damping = 0.1
batch = 8
chunks = 4
id_rows = 16
cores = 2


def dot_nn(a, b):
    return lax.dot_general(a, b, (((1,), (0,)), ((), ())), preferred_element_type=jnp.float32)


def dot_nt(a, b):
    return lax.dot_general(a, b, (((1,), (1,)), ((), ())), preferred_element_type=jnp.float32)


def split_two(value):
    high = value.astype(jnp.bfloat16)
    low = (value - high.astype(jnp.float32)).astype(jnp.bfloat16)
    return high, low


def feature_kernel(
    tokens, slices, act_hbm, grad_hbm, pin_hbm, pout_hbm, bin_ref, bout_ref, eigen_ref, ids_ref, out_ref,
    act, grad, pin, pout, act_sum, grad_sum, gt_ref, feat, act_sem, grad_sem, w_sem,
):
    rows, width = act.shape
    rank = bin_ref.shape[0]
    half = rank // 2
    step_rows = batch * tokens
    steps = rows // step_rows
    examples = feat.shape[1]
    chunk = width // chunks

    def chunk_copies(index):
        rng = pl.ds(pl.multiple_of(index * chunk, chunk), chunk)
        return (
            pltpu.make_async_copy(act_hbm.at[:, rng], act.at[:, rng], act_sem.at[index]),
            pltpu.make_async_copy(grad_hbm.at[:, rng], grad.at[:, rng], grad_sem.at[index]),
        )

    weights = [
        pltpu.make_async_copy(pin_hbm, pin, w_sem.at[0]),
        pltpu.make_async_copy(pout_hbm, pout, w_sem.at[1]),
    ]
    for copy in weights:
        copy.start()
    for index in range(chunks):
        for priority, copy in enumerate(chunk_copies(index)):
            copy.start(priority=priority)

    bin_hi, bin_lo = split_two(jnp.concatenate([bin_ref[...], bin_ref[...]], axis=1))
    bout_hi, bout_lo = split_two(bout_ref[...].T)
    inverse = 1.0 / jnp.sqrt(eigen_ref[...] + damping)
    inverse = jnp.concatenate([inverse[:half], inverse[half:]], axis=1)
    own_token = (
        lax.broadcasted_iota(jnp.int32, (batch, step_rows), 1) // tokens
        == lax.broadcasted_iota(jnp.int32, (batch, step_rows), 0)
    )
    first_lanes = lax.broadcasted_iota(jnp.int32, (batch, 2 * rank), 1) < rank
    ids = jnp.concatenate([ids_ref[...]] * (2 * rank // examples), axis=1)
    place = lax.broadcasted_iota(jnp.int32, (id_rows, 2 * rank), 0) % 4
    digits = (jnp.broadcast_to(ids, (id_rows, 2 * rank)) >> (place * 8)) & 255
    digits = digits.astype(jnp.float32).astype(jnp.bfloat16)
    for copy in weights:
        copy.wait()

    def project(index, first):
        for copy in chunk_copies(index):
            copy.wait()
        rng = pl.ds(pl.multiple_of(index * chunk, chunk), chunk)
        act_part = dot_nt(act[:, rng], pin[:, rng])
        grad_part = dot_nt(grad[:, rng], pout[:, rng])
        act_sum[...] = act_part if first else act_sum[...] + act_part
        grad_sum[...] = grad_part if first else grad_sum[...] + grad_part

    def rotate(step):
        rng = pl.ds(pl.multiple_of(step * step_rows, step_rows), step_rows)
        act_part = act_sum[rng].astype(jnp.bfloat16)
        grad_part = grad_sum[rng].astype(jnp.bfloat16)
        act_hi, act_lo = split_two(dot_nn(act_part, bin_hi) + dot_nn(act_part, bin_lo))
        gt_ref[...] = dot_nt(bout_hi, grad_part) + dot_nt(bout_lo, grad_part)
        spread_hi, spread_lo = [], []
        for u in range(rank):
            row = jnp.broadcast_to(gt_ref[pl.ds(u, 1)], (batch, step_rows))
            hi, lo = split_two(jnp.where(own_token, row, 0.0))
            spread_hi.append(hi)
            spread_lo.append(lo)
        spread_hi = jnp.concatenate(spread_hi, axis=0)
        spread_lo = jnp.concatenate(spread_lo, axis=0)
        wide = dot_nn(spread_hi, jnp.concatenate([act_hi, act_lo], axis=1))
        rotated = wide[:, :2 * rank] + wide[:, 2 * rank:] + dot_nn(spread_lo, act_hi)
        start = pl.multiple_of(step * batch, batch)
        for u in range(half):
            value = jnp.where(
                first_lanes,
                rotated[u * batch:(u + 1) * batch],
                rotated[(u + half) * batch:(u + half + 1) * batch],
            ) * inverse[u:u + 1]
            feat[u, pl.ds(start, batch)] = value

    project(0, True)
    lax.fori_loop(1, chunks, lambda index, carry: (project(index, False), carry)[1], 0)
    lax.fori_loop(0, steps, lambda step, carry: (rotate(step), carry)[1], 0)
    depth = half // slices
    for index in range(slices):
        piece = feat[pl.ds(index * depth, depth)].astype(jnp.bfloat16)
        out_ref[index, pl.ds(0, depth * examples)] = piece.reshape(depth * examples, 2 * rank)
        out_ref[index, pl.ds(depth * examples, id_rows)] = digits


def features(slices, activations, out_grads, proj_in, proj_out, basis_in, basis_out, eigen, doc_ids):
    examples, tokens, width = activations.shape
    rank = proj_in.shape[1]
    rows = examples * tokens
    half = rank // 2
    hbm = pl.BlockSpec(memory_space=pl.ANY)
    vmem = pl.BlockSpec(memory_space=pltpu.VMEM)
    return pl.pallas_call(
        functools.partial(feature_kernel, tokens, slices),
        out_shape=jax.ShapeDtypeStruct(
            (slices, half // slices * examples + id_rows, 2 * rank), jnp.bfloat16),
        in_specs=[hbm] * 4 + [vmem] * 4,
        out_specs=vmem,
        scratch_shapes=[
            pltpu.VMEM((rows, width), jnp.bfloat16),
            pltpu.VMEM((rows, width), jnp.bfloat16),
            pltpu.VMEM((rank, width), jnp.bfloat16),
            pltpu.VMEM((rank, width), jnp.bfloat16),
            pltpu.VMEM((rows, rank), jnp.float32),
            pltpu.VMEM((rows, rank), jnp.float32),
            pltpu.VMEM((rank, batch * tokens), jnp.float32),
            pltpu.VMEM((half, examples, 2 * rank), jnp.float32),
            pltpu.SemaphoreType.DMA((chunks,)),
            pltpu.SemaphoreType.DMA((chunks,)),
            pltpu.SemaphoreType.DMA((2,)),
        ],
        compiler_params=pltpu.CompilerParams(vmem_limit_bytes=60 * 2**20),
        cost_estimate=pl.CostEstimate(
            flops=4 * rows * width * rank, bytes_accessed=4 * rows * width, transcendentals=0),
        name="features",
    )(
        activations.reshape(rows, width), out_grads.reshape(rows, width),
        proj_in.T, proj_out.T, basis_in, basis_out, eigen, doc_ids.reshape(1, examples),
    )


def reverse_bits(value, count):
    return sum(((value >> bit) & 1) << (count - 1 - bit) for bit in range(count))


def product_kernel(groups, examples, *refs):
    columns, (other, out_ref, ids_ref, column_stack, row_stack) = refs[:groups], refs[groups:]
    slices, piece_rows, lanes = columns[0].shape
    depth = (piece_rows - id_rows) // examples
    cols = column_stack.shape[0]
    grp = lax.axis_index("grp")
    core = lax.axis_index("mem") % cores

    def place(stack, row, ref, piece):
        start = pl.multiple_of(row * examples, examples)
        for part in range(depth):
            stack[pl.ds(start, examples), pl.ds(part * lanes, lanes)] = (
                ref[piece, pl.ds(part * examples, examples)])

    block = lax.broadcasted_iota(jnp.int32, (id_rows, cols), 1) // examples
    digits = jnp.zeros((id_rows, cols), jnp.float32)
    for piece in range(slices):
        for slot in range(groups):
            distance = jnp.where(core == 0, slot, reverse_bits(slot, groups.bit_length() - 1))
            column = (grp ^ distance) * slices + piece
            ref = columns[slot]
            place(column_stack, column, ref, piece)
            some = ref[piece, pl.ds(piece_rows - id_rows, id_rows)].astype(jnp.float32)
            some = jnp.concatenate([some] * (cols // lanes), axis=1)
            digits = jnp.where(block == column, some, digits)
        place(row_stack, piece * cores + core, columns[0], piece)
        place(row_stack, piece * cores + (core ^ 1), other, piece)
    result = dot_nt(row_stack[...], column_stack[...]).astype(jnp.bfloat16)
    out_ref[...] = result.reshape(out_ref.shape)
    ids_ref[pl.ds(0, 1)] = digits[0:1] + digits[1:2] * 256.0
    ids_ref[pl.ds(1, 1)] = digits[2:3] + digits[3:4] * 256.0


def products(columns, other, groups, examples):
    slices, piece_rows, lanes = columns[0].shape
    depth = (piece_rows - id_rows) // examples
    vmem = pl.BlockSpec(memory_space=pltpu.VMEM)
    rows, cols = slices * cores * examples, groups * slices * examples
    return pl.pallas_call(
        functools.partial(product_kernel, groups, examples),
        out_shape=[
            jax.ShapeDtypeStruct((slices, cores * examples, cols), jnp.bfloat16),
            jax.ShapeDtypeStruct((2, cols), jnp.float32),
        ],
        in_specs=[vmem] * (groups + 1),
        out_specs=[vmem] * 2,
        scratch_shapes=[
            pltpu.VMEM((cols, depth * lanes), jnp.bfloat16),
            pltpu.VMEM((rows, depth * lanes), jnp.bfloat16),
        ],
        compiler_params=pltpu.CompilerParams(vmem_limit_bytes=40 * 2**20),
        cost_estimate=pl.CostEstimate(
            flops=2 * rows * cols * depth * lanes, bytes_accessed=4 * rows * cols, transcendentals=0),
        name="products",
    )(*columns, other)


def total_kernel(ids_ref, parts_ref, keep_ref, send_ref):
    examples = keep_ref.shape[0]
    core = lax.axis_index("mem") % cores
    keep = pl.ds(pl.multiple_of(core * examples, examples), examples)
    send = pl.ds(pl.multiple_of((core ^ 1) * examples, examples), examples)
    parts = range(parts_ref.shape[0])
    keep_ref[...] = sum(parts_ref[part, keep].astype(jnp.float32) for part in parts)
    send_ref[pl.ds(0, examples)] = sum(parts_ref[part, send].astype(jnp.float32) for part in parts)
    send_ref[pl.ds(examples, 2)] = ids_ref[...]


def totals(parts, ids, examples):
    slices, _, cols = parts.shape
    vmem = pl.BlockSpec(memory_space=pltpu.VMEM)
    return pl.pallas_call(
        total_kernel,
        out_shape=[
            jax.ShapeDtypeStruct((examples, cols), jnp.float32),
            jax.ShapeDtypeStruct((examples + 8, cols), jnp.float32),
        ],
        in_specs=[vmem] * 2,
        out_specs=[vmem] * 2,
        compiler_params=pltpu.CompilerParams(vmem_limit_bytes=40 * 2**20),
        cost_estimate=pl.CostEstimate(
            flops=2 * examples * cols * slices, bytes_accessed=8 * examples * cols, transcendentals=0),
        name="totals",
    )(ids, parts)


def finish_kernel(factor, own_ids_ref, ids_ref, keep_ref, got_ref, out_ref):
    examples, cols = keep_ref.shape
    core = lax.axis_index("mem") % cores
    block = lax.broadcasted_iota(jnp.int32, (examples, 128), 1) // examples
    id_block = lax.broadcasted_iota(jnp.int32, (8, 128), 1) // examples
    own_low = (own_ids_ref[...] & 0xFFFF).astype(jnp.float32)
    own_high = ((own_ids_ref[...] >> 16) & 0xFFFF).astype(jnp.float32)

    def take_turns(first, second, side, block):
        value = jnp.zeros_like(first)
        for quarter in range(128 // examples):
            moved = second if quarter % cores else first
            source = side * (64 // examples) + quarter // cores
            shift = (quarter - source) * examples % 128
            if shift:
                moved = pltpu.roll(moved, shift, 1)
            value = jnp.where(block == quarter, moved, value)
        return value

    for tile in range(cols // 128):
        rng = pl.ds(tile * 128, 128)
        same, other = keep_ref[:, rng], got_ref[pl.ds(0, examples), rng]
        first, second = jnp.where(core == 0, same, other), jnp.where(core == 0, other, same)
        same_ids = [jnp.broadcast_to(ids_ref[pl.ds(row, 1), rng], (8, 128)) for row in range(2)]
        other_ids = [jnp.broadcast_to(got_ref[pl.ds(examples + row, 1), rng], (8, 128)) for row in range(2)]
        for side in range(cores):
            value = take_turns(first, second, side, block)
            low, high = [
                take_turns(
                    jnp.where(core == 0, a, b), jnp.where(core == 0, b, a), side, id_block)[0:1]
                for a, b in zip(same_ids, other_ids)
            ]
            same_doc = (own_low == low) & (own_high == high)
            out_ref[:, pl.ds(tile * 256 + side * 128, 128)] = jnp.where(same_doc, 0.0, value * factor)


def finish(own_ids, ids, keep, got, factor):
    examples, cols = keep.shape
    vmem = pl.BlockSpec(memory_space=pltpu.VMEM)
    return pl.pallas_call(
        functools.partial(finish_kernel, factor),
        out_shape=jax.ShapeDtypeStruct((examples, cores * cols), jnp.float32),
        in_specs=[vmem] * 4,
        out_specs=vmem,
        compiler_params=pltpu.CompilerParams(vmem_limit_bytes=40 * 2**20),
        cost_estimate=pl.CostEstimate(
            flops=8 * examples * cols, bytes_accessed=16 * examples * cols, transcendentals=0),
        name="finish",
    )(own_ids, ids, keep, got)


def swap(value, axis, size, distance):
    return lax.ppermute(value, axis, [(place, place ^ distance) for place in range(size)])


def gather_groups(piece, groups, members):
    bits = groups.bit_length() - 1
    held = [piece]
    for slot in range(1, groups):
        bit = 1 << (slot.bit_length() - 1)
        pairs = []
        for group in range(groups):
            for member in range(members):
                step = reverse_bits(bit, bits) if member % cores else bit
                pairs.append((group * members + member, (group ^ step) * members + member))
        held.append(lax.ppermute(held[slot ^ bit], ("grp", "mem"), pairs))
    return held


def exchange(value, members):
    lines = [list(range(core, members, cores)) for core in range(cores)]
    return lax.all_to_all(value, "mem", 0, 0, axis_index_groups=lines, tiled=True)


def on_device(members, groups, activations, out_grads, proj_in, proj_out, basis_in, basis_out, eigen, doc_ids):
    examples, tokens, width = activations.shape
    rank = proj_in.shape[1]
    factor = 1.0 / (tokens * rank)
    slices = members // cores
    feat = features(slices, activations, out_grads, proj_in, proj_out, basis_in, basis_out, eigen, doc_ids)
    slab = exchange(feat, members)
    columns = gather_groups(slab, groups, members)
    partial, ids = products(columns, swap(slab, "mem", members, 1), groups, examples)
    keep, send = totals(exchange(partial, members), ids, examples)
    return finish(doc_ids[:, None], ids, keep, swap(send, "mem", members, 1), factor)


def solution(mesh):
    return jax.shard_map(
        functools.partial(on_device, mesh.shape["mem"], mesh.shape["grp"]),
        mesh=mesh,
        in_specs=(
            P(("grp", "mem"), None, None),
            P(("grp", "mem"), None, None),
            P(),
            P(),
            P(),
            P(),
            P(),
            P(("grp", "mem")),
        ),
        out_specs=P(("grp", "mem"), None),
        check_vma=False,
    )
```

```python
import functools
import jax
import jax.numpy as jnp
from jax import lax
from jax.experimental import pallas as pl
from jax.experimental.pallas import tpu as pltpu
from jax.sharding import PartitionSpec as P

damping = 0.1
batch = 8
id_rows = 16
cores = 2


def dot_nn(a, b):
    return lax.dot_general(a, b, (((1,), (0,)), ((), ())), preferred_element_type=jnp.float32)


def dot_nt(a, b):
    return lax.dot_general(a, b, (((1,), (1,)), ((), ())), preferred_element_type=jnp.float32)


def split_two(value):
    high = value.astype(jnp.bfloat16)
    low = (value - high.astype(jnp.float32)).astype(jnp.bfloat16)
    return high, low


def feature_kernel(
    tokens, slices, act_hbm, grad_hbm, pin_hbm, pout_hbm, bin_ref, bout_ref, eigen_ref, ids_ref, *refs
):
    out_refs = refs[:slices]
    act, grad, pin, pout, act_proj, grad_proj, gt_ref, feat, act_sem, grad_sem, w_sem = refs[slices:]
    rows, width = act.shape
    rank = bin_ref.shape[0]
    half = rank // 2
    step_rows = batch * tokens
    steps = rows // step_rows
    examples = feat.shape[1]

    def step_copies(step):
        rng = pl.ds(pl.multiple_of(step * step_rows, step_rows), step_rows)
        return (
            pltpu.make_async_copy(act_hbm.at[rng], act.at[rng], act_sem.at[step]),
            pltpu.make_async_copy(grad_hbm.at[rng], grad.at[rng], grad_sem.at[step]),
        )

    weights = [
        pltpu.make_async_copy(pin_hbm, pin, w_sem.at[0]),
        pltpu.make_async_copy(pout_hbm, pout, w_sem.at[1]),
    ]
    for copy in weights:
        copy.start()
    for step in range(steps):
        for priority, copy in enumerate(step_copies(step)):
            copy.start(priority=priority)

    bin_hi, bin_lo = split_two(jnp.concatenate([bin_ref[...], bin_ref[...]], axis=1))
    bout_hi, bout_lo = split_two(bout_ref[...].T)
    inverse = 1.0 / jnp.sqrt(eigen_ref[...] + damping)
    inverse = jnp.concatenate([inverse[:half], inverse[half:]], axis=1)
    own_token = (
        lax.broadcasted_iota(jnp.int32, (batch, step_rows), 1) // tokens
        == lax.broadcasted_iota(jnp.int32, (batch, step_rows), 0)
    )
    first_lanes = lax.broadcasted_iota(jnp.int32, (batch, 2 * rank), 1) < rank
    ids = jnp.concatenate([ids_ref[...]] * (2 * rank // examples), axis=1)
    place = lax.broadcasted_iota(jnp.int32, (id_rows, 2 * rank), 0) % 4
    digits = (jnp.broadcast_to(ids, (id_rows, 2 * rank)) >> (place * 8)) & 255
    digits = digits.astype(jnp.float32).astype(jnp.bfloat16)
    for copy in weights:
        copy.wait()

    def project(step):
        for copy in step_copies(step):
            copy.wait()
        rng = pl.ds(pl.multiple_of(step * step_rows, step_rows), step_rows)
        first, second = pl.ds(0, width // 2), pl.ds(width // 2, width // 2)
        return (
            (dot_nt(act[rng, first], pin[:, first]) + dot_nt(act[rng, second], pin[:, second])
             ).astype(jnp.bfloat16),
            (dot_nt(grad[rng, first], pout[:, first]) + dot_nt(grad[rng, second], pout[:, second])
             ).astype(jnp.bfloat16),
        )

    def rotate(step, act_part, grad_part):
        act_hi, act_lo = split_two(dot_nn(act_part, bin_hi) + dot_nn(act_part, bin_lo))
        grad_hi, grad_lo = split_two(dot_nt(bout_hi, grad_part) + dot_nt(bout_lo, grad_part))
        gt_ref[0] = grad_hi.astype(jnp.float32)
        gt_ref[1] = grad_lo.astype(jnp.float32)
        spread_hi, spread_lo = [
            jnp.concatenate([
                jnp.where(own_token, jnp.broadcast_to(gt_ref[part, pl.ds(u, 1)], (batch, step_rows)), 0.0)
                for u in range(rank)
            ], axis=0).astype(jnp.bfloat16)
            for part in range(2)
        ]
        wide = dot_nn(spread_hi, jnp.concatenate([act_hi, act_lo], axis=1))
        rotated = wide[:, :2 * rank] + wide[:, 2 * rank:] + dot_nn(spread_lo, act_hi)
        start = pl.multiple_of(step * batch, batch)
        for u in range(half):
            value = jnp.where(
                first_lanes,
                rotated[u * batch:(u + 1) * batch],
                rotated[(u + half) * batch:(u + half + 1) * batch],
            ) * inverse[u:u + 1]
            feat[u, pl.ds(start, batch)] = value

    act_proj[...], grad_proj[...] = project(0)

    def body(step, carry):
        act_part, grad_part = act_proj[...], grad_proj[...]
        act_next, grad_next = project(step)
        rotate(step - 1, act_part, grad_part)
        act_proj[...] = act_next
        grad_proj[...] = grad_next
        return carry

    lax.fori_loop(1, steps, body, 0)
    rotate(steps - 1, act_proj[...], grad_proj[...])
    depth = half // slices
    me = lax.axis_index("mem") // cores
    for index in range(slices):
        start = (me ^ index) * depth
        piece = feat[pl.ds(start, depth)].astype(jnp.bfloat16)
        out_refs[index][pl.ds(0, depth * examples)] = piece.reshape(depth * examples, 2 * rank)
        out_refs[index][pl.ds(depth * examples, id_rows)] = digits


def features(slices, activations, out_grads, proj_in, proj_out, basis_in, basis_out, eigen, doc_ids):
    examples, tokens, width = activations.shape
    rank = proj_in.shape[1]
    rows = examples * tokens
    steps = examples // batch
    half = rank // 2
    hbm = pl.BlockSpec(memory_space=pl.ANY)
    vmem = pl.BlockSpec(memory_space=pltpu.VMEM)
    return pl.pallas_call(
        functools.partial(feature_kernel, tokens, slices),
        out_shape=[
            jax.ShapeDtypeStruct((half // slices * examples + id_rows, 2 * rank), jnp.bfloat16)
        ] * slices,
        in_specs=[hbm] * 4 + [vmem] * 4,
        out_specs=[vmem] * slices,
        scratch_shapes=[
            pltpu.VMEM((rows, width), jnp.bfloat16),
            pltpu.VMEM((rows, width), jnp.bfloat16),
            pltpu.VMEM((rank, width), jnp.bfloat16),
            pltpu.VMEM((rank, width), jnp.bfloat16),
            pltpu.VMEM((batch * tokens, rank), jnp.bfloat16),
            pltpu.VMEM((batch * tokens, rank), jnp.bfloat16),
            pltpu.VMEM((2, rank, batch * tokens), jnp.float32),
            pltpu.VMEM((half, examples, 2 * rank), jnp.float32),
            pltpu.SemaphoreType.DMA((steps,)),
            pltpu.SemaphoreType.DMA((steps,)),
            pltpu.SemaphoreType.DMA((2,)),
        ],
        compiler_params=pltpu.CompilerParams(vmem_limit_bytes=60 * 2**20),
        cost_estimate=pl.CostEstimate(
            flops=4 * rows * width * rank, bytes_accessed=4 * rows * width, transcendentals=0),
        name="features",
    )(
        activations.reshape(rows, width), out_grads.reshape(rows, width),
        proj_in.T, proj_out.T, basis_in, basis_out, eigen, doc_ids.reshape(1, examples),
    )


def slice_order(slices):
    return [0] + list(range(slices - 1, 0, -1))


def product_kernel(groups, slices, pieces, examples, *refs):
    runs = slices // pieces
    columns = refs[:groups * runs]
    others = refs[groups * runs:(groups + 1) * runs]
    outs = refs[(groups + 1) * runs:(groups + 1) * runs + slices]
    ids_ref, column_stack, row_stack, result = refs[(groups + 1) * runs + slices:]
    piece_rows, lanes = columns[0].shape
    piece_rows = piece_rows // pieces
    depth = (piece_rows - id_rows) // examples
    cols = column_stack.shape[0]
    grp = lax.axis_index("grp")
    mem = lax.axis_index("mem")
    pair, core = mem // cores, mem % cores

    def place(stack, row, ref, piece):
        start = pl.multiple_of(row * examples, examples)
        for part in range(depth):
            stack[pl.ds(start, examples), pl.ds(part * lanes, lanes)] = (
                ref[pl.ds(piece * piece_rows + part * examples, examples)])

    block = lax.broadcasted_iota(jnp.int32, (id_rows, cols), 1) // examples
    digits = jnp.zeros((id_rows, cols), jnp.float32)
    for run in range(runs):
        for piece in range(pieces):
            place_of = pair ^ slice_order(slices)[run * pieces + piece]
            for slot in range(groups):
                column = (grp ^ slot) * slices + place_of
                ref = columns[slot * runs + run]
                place(column_stack, column, ref, piece)
                some = ref[pl.ds((piece + 1) * piece_rows - id_rows, id_rows)].astype(jnp.float32)
                some = jnp.concatenate([some] * (cols // lanes), axis=1)
                digits = jnp.where(block == column, some, digits)
            place(row_stack, place_of * cores + core, columns[run], piece)
            place(row_stack, place_of * cores + (core ^ 1), others[run], piece)
    result[...] = dot_nt(row_stack[...], column_stack[...]).astype(jnp.bfloat16)
    for index in range(slices):
        start = pl.multiple_of((pair ^ index) * (cores * examples), cores * examples)
        outs[index][...] = result[pl.ds(start, cores * examples)]
    ids_ref[pl.ds(0, 1)] = digits[0:1] + digits[1:2] * 256.0
    ids_ref[pl.ds(1, 1)] = digits[2:3] + digits[3:4] * 256.0


def products(columns, others, groups, slices, pieces, examples):
    piece_rows, lanes = columns[0].shape
    depth = (piece_rows // pieces - id_rows) // examples
    vmem = pl.BlockSpec(memory_space=pltpu.VMEM)
    rows, cols = slices * cores * examples, groups * slices * examples
    return pl.pallas_call(
        functools.partial(product_kernel, groups, slices, pieces, examples),
        out_shape=[jax.ShapeDtypeStruct((cores * examples, cols), jnp.bfloat16)] * slices
        + [jax.ShapeDtypeStruct((2, cols), jnp.float32)],
        in_specs=[vmem] * (len(columns) + len(others)),
        out_specs=[vmem] * (slices + 1),
        scratch_shapes=[
            pltpu.VMEM((cols, depth * lanes), jnp.bfloat16),
            pltpu.VMEM((rows, depth * lanes), jnp.bfloat16),
            pltpu.VMEM((rows, cols), jnp.bfloat16),
        ],
        compiler_params=pltpu.CompilerParams(vmem_limit_bytes=40 * 2**20),
        cost_estimate=pl.CostEstimate(
            flops=2 * rows * cols * depth * lanes, bytes_accessed=4 * rows * cols, transcendentals=0),
        name="products",
    )(*columns, *others)


def total_kernel(slices, ids_ref, *refs):
    parts, (keep_ref, send_ref) = refs[:slices], refs[slices:]
    examples = keep_ref.shape[0]
    core = lax.axis_index("mem") % cores
    keep = pl.ds(pl.multiple_of(core * examples, examples), examples)
    send = pl.ds(pl.multiple_of((core ^ 1) * examples, examples), examples)
    keep_ref[...] = sum(part[keep].astype(jnp.float32) for part in parts)
    send_ref[pl.ds(0, examples)] = sum(part[send].astype(jnp.float32) for part in parts)
    send_ref[pl.ds(examples, 2)] = ids_ref[...]


def totals(parts, ids, examples):
    cols = parts[0].shape[1]
    vmem = pl.BlockSpec(memory_space=pltpu.VMEM)
    return pl.pallas_call(
        functools.partial(total_kernel, len(parts)),
        out_shape=[
            jax.ShapeDtypeStruct((examples, cols), jnp.float32),
            jax.ShapeDtypeStruct((examples + 8, cols), jnp.float32),
        ],
        in_specs=[vmem] * (1 + len(parts)),
        out_specs=[vmem] * 2,
        compiler_params=pltpu.CompilerParams(vmem_limit_bytes=40 * 2**20),
        cost_estimate=pl.CostEstimate(
            flops=2 * examples * cols * len(parts), bytes_accessed=8 * examples * cols, transcendentals=0),
        name="totals",
    )(ids, *parts)


def finish_kernel(factor, own_ids_ref, ids_ref, keep_ref, got_ref, out_ref):
    examples, cols = keep_ref.shape
    core = lax.axis_index("mem") % cores
    block = lax.broadcasted_iota(jnp.int32, (examples, 128), 1) // examples
    id_block = lax.broadcasted_iota(jnp.int32, (8, 128), 1) // examples
    own_low = (own_ids_ref[...] & 0xFFFF).astype(jnp.float32)
    own_high = ((own_ids_ref[...] >> 16) & 0xFFFF).astype(jnp.float32)

    def take_turns(first, second, side, block):
        value = jnp.zeros_like(first)
        for quarter in range(128 // examples):
            moved = second if quarter % cores else first
            source = side * (64 // examples) + quarter // cores
            shift = (quarter - source) * examples % 128
            if shift:
                moved = pltpu.roll(moved, shift, 1)
            value = jnp.where(block == quarter, moved, value)
        return value

    for tile in range(cols // 128):
        rng = pl.ds(tile * 128, 128)
        same, other = keep_ref[:, rng], got_ref[pl.ds(0, examples), rng]
        first, second = jnp.where(core == 0, same, other), jnp.where(core == 0, other, same)
        same_ids = [jnp.broadcast_to(ids_ref[pl.ds(row, 1), rng], (8, 128)) for row in range(2)]
        other_ids = [jnp.broadcast_to(got_ref[pl.ds(examples + row, 1), rng], (8, 128)) for row in range(2)]
        for side in range(cores):
            value = take_turns(first, second, side, block)
            low, high = [
                take_turns(
                    jnp.where(core == 0, a, b), jnp.where(core == 0, b, a), side, id_block)[0:1]
                for a, b in zip(same_ids, other_ids)
            ]
            same_doc = (own_low == low) & (own_high == high)
            out_ref[:, pl.ds(tile * 256 + side * 128, 128)] = jnp.where(same_doc, 0.0, value * factor)


def finish(own_ids, ids, keep, got, factor):
    examples, cols = keep.shape
    vmem = pl.BlockSpec(memory_space=pltpu.VMEM)
    return pl.pallas_call(
        functools.partial(finish_kernel, factor),
        out_shape=jax.ShapeDtypeStruct((examples, cores * cols), jnp.float32),
        in_specs=[vmem] * 4,
        out_specs=vmem,
        compiler_params=pltpu.CompilerParams(vmem_limit_bytes=40 * 2**20),
        cost_estimate=pl.CostEstimate(
            flops=8 * examples * cols, bytes_accessed=16 * examples * cols, transcendentals=0),
        name="finish",
    )(own_ids, ids, keep, got)


def swap(value, axis, size, distance):
    return lax.ppermute(value, axis, [(place, place ^ distance) for place in range(size)])


def gather_groups(piece, groups, low_first):
    held = [piece]
    for distance in range(1, groups):
        low = distance & -distance
        high = 1 << (distance.bit_length() - 1)
        bit = low if low_first else high
        held.append(swap(held[distance ^ bit], "grp", groups, bit))
    return held


def on_device(members, groups, activations, out_grads, proj_in, proj_out, basis_in, basis_out, eigen, doc_ids):
    examples, tokens, width = activations.shape
    rank = proj_in.shape[1]
    factor = 1.0 / (tokens * rank)
    slices = members // cores
    runs = 2
    pieces = slices // runs
    feat = features(slices, activations, out_grads, proj_in, proj_out, basis_in, basis_out, eigen, doc_ids)
    got = [feat[index] if index == 0 else swap(feat[index], "mem", members, cores * index)
           for index in slice_order(slices)]
    columns = [[None] * runs for _ in range(groups)]
    others = []
    for run in range(runs):
        slab = jnp.concatenate(got[run * pieces:(run + 1) * pieces], axis=0)
        if run:
            slab, columns[1][run - 1] = lax.optimization_barrier((slab, columns[1][run - 1]))
        for slot, held in enumerate(gather_groups(slab, groups, run % 2 == 1)):
            columns[slot][run] = held
        others.append(swap(slab, "mem", members, 1))
    flat = [columns[slot][run] for slot in range(groups) for run in range(runs)]
    *partial, ids = products(flat, others, groups, slices, pieces, examples)
    parts = [partial[index] if index == 0 else swap(partial[index], "mem", members, cores * index)
             for index in slice_order(slices)]
    keep, send = totals(parts, ids, examples)
    return finish(doc_ids[:, None], ids, keep, swap(send, "mem", members, 1), factor)


def solution(mesh):
    return jax.shard_map(
        functools.partial(on_device, mesh.shape["mem"], mesh.shape["grp"]),
        mesh=mesh,
        in_specs=(
            P(("grp", "mem"), None, None),
            P(("grp", "mem"), None, None),
            P(),
            P(),
            P(),
            P(),
            P(),
            P(("grp", "mem")),
        ),
        out_specs=P(("grp", "mem"), None),
        check_vma=False,
    )
```

```python
import functools
import jax
import jax.numpy as jnp
from jax import lax
from jax.experimental import pallas as pl
from jax.experimental.pallas import tpu as pltpu
from jax.sharding import PartitionSpec as P

damping = 0.1
batch = 8
id_rows = 16
cores = 2


def dot_nn(a, b):
    return lax.dot_general(a, b, (((1,), (0,)), ((), ())), preferred_element_type=jnp.float32)


def dot_nt(a, b):
    return lax.dot_general(a, b, (((1,), (1,)), ((), ())), preferred_element_type=jnp.float32)


def split_two(value):
    high = value.astype(jnp.bfloat16)
    low = (value - high.astype(jnp.float32)).astype(jnp.bfloat16)
    return high, low


def feature_kernel(
    tokens, slices, act_hbm, grad_hbm, pin_hbm, pout_hbm, bin_ref, bout_ref, eigen_ref, ids_ref, *refs
):
    out_refs = refs[:slices]
    act, grad, pin, pout, act_proj, grad_proj, gt_ref, feat, act_sem, grad_sem, w_sem = refs[slices:]
    rows, width = act.shape
    rank = bin_ref.shape[0]
    half = rank // 2
    step_rows = batch * tokens
    steps = rows // step_rows
    examples = feat.shape[1]

    def step_copies(step):
        rng = pl.ds(pl.multiple_of(step * step_rows, step_rows), step_rows)
        return (
            pltpu.make_async_copy(act_hbm.at[rng], act.at[rng], act_sem.at[step]),
            pltpu.make_async_copy(grad_hbm.at[rng], grad.at[rng], grad_sem.at[step]),
        )

    weights = [
        pltpu.make_async_copy(pin_hbm, pin, w_sem.at[0]),
        pltpu.make_async_copy(pout_hbm, pout, w_sem.at[1]),
    ]
    def start_step(step):
        for priority, copy in enumerate(step_copies(step)):
            copy.start(priority=priority)

    for copy in weights:
        copy.start()
    start_step(0)

    bin_hi, bin_lo = split_two(jnp.concatenate([bin_ref[...], bin_ref[...]], axis=1))
    bout_hi, bout_lo = split_two(bout_ref[...].T)
    inverse = 1.0 / jnp.sqrt(eigen_ref[...] + damping)
    inverse = jnp.concatenate([inverse[:half], inverse[half:]], axis=1)
    own_token = (
        lax.broadcasted_iota(jnp.int32, (batch, step_rows), 1) // tokens
        == lax.broadcasted_iota(jnp.int32, (batch, step_rows), 0)
    )
    first_lanes = lax.broadcasted_iota(jnp.int32, (batch, 2 * rank), 1) < rank
    ids = jnp.concatenate([ids_ref[...]] * (2 * rank // examples), axis=1)
    place = lax.broadcasted_iota(jnp.int32, (id_rows, 2 * rank), 0) % 4
    digits = (jnp.broadcast_to(ids, (id_rows, 2 * rank)) >> (place * 8)) & 255
    digits = digits.astype(jnp.float32).astype(jnp.bfloat16)
    for copy in weights:
        copy.wait()

    def project(step):
        for copy in step_copies(step):
            copy.wait()
        pl.when(step + 1 < steps)(lambda: start_step(step + 1))
        rng = pl.ds(pl.multiple_of(step * step_rows, step_rows), step_rows)
        first, second = pl.ds(0, width // 2), pl.ds(width // 2, width // 2)
        return (
            (dot_nt(act[rng, first], pin[:, first]) + dot_nt(act[rng, second], pin[:, second])
             ).astype(jnp.bfloat16),
            (dot_nt(grad[rng, first], pout[:, first]) + dot_nt(grad[rng, second], pout[:, second])
             ).astype(jnp.bfloat16),
        )

    def rotate(step, act_part, grad_part):
        act_hi, act_lo = split_two(dot_nn(act_part, bin_hi) + dot_nn(act_part, bin_lo))
        grad_hi, grad_lo = split_two(dot_nt(bout_hi, grad_part) + dot_nt(bout_lo, grad_part))
        gt_ref[0] = grad_hi.astype(jnp.float32)
        gt_ref[1] = grad_lo.astype(jnp.float32)
        spread_hi, spread_lo = [
            jnp.concatenate([
                jnp.where(own_token, jnp.broadcast_to(gt_ref[part, pl.ds(u, 1)], (batch, step_rows)), 0.0)
                for u in range(rank)
            ], axis=0).astype(jnp.bfloat16)
            for part in range(2)
        ]
        wide = dot_nn(spread_hi, jnp.concatenate([act_hi, act_lo], axis=1))
        rotated = wide[:, :2 * rank] + wide[:, 2 * rank:] + dot_nn(spread_lo, act_hi)
        start = pl.multiple_of(step * batch, batch)
        for u in range(half):
            value = jnp.where(
                first_lanes,
                rotated[u * batch:(u + 1) * batch],
                rotated[(u + half) * batch:(u + half + 1) * batch],
            ) * inverse[u:u + 1]
            feat[u, pl.ds(start, batch)] = value

    act_proj[...], grad_proj[...] = project(0)

    def body(step, carry):
        act_part, grad_part = act_proj[...], grad_proj[...]
        act_next, grad_next = project(step)
        rotate(step - 1, act_part, grad_part)
        act_proj[...] = act_next
        grad_proj[...] = grad_next
        return carry

    lax.fori_loop(1, steps, body, 0)
    rotate(steps - 1, act_proj[...], grad_proj[...])
    depth = half // slices
    me = lax.axis_index("mem") // cores
    for index in range(slices):
        start = (me ^ index) * depth
        piece = feat[pl.ds(start, depth)].astype(jnp.bfloat16)
        out_refs[index][pl.ds(0, depth * examples)] = piece.reshape(depth * examples, 2 * rank)
        out_refs[index][pl.ds(depth * examples, id_rows)] = digits


def features(slices, activations, out_grads, proj_in, proj_out, basis_in, basis_out, eigen, doc_ids):
    examples, tokens, width = activations.shape
    rank = proj_in.shape[1]
    rows = examples * tokens
    steps = examples // batch
    half = rank // 2
    hbm = pl.BlockSpec(memory_space=pl.ANY)
    vmem = pl.BlockSpec(memory_space=pltpu.VMEM)
    return pl.pallas_call(
        functools.partial(feature_kernel, tokens, slices),
        out_shape=[
            jax.ShapeDtypeStruct((half // slices * examples + id_rows, 2 * rank), jnp.bfloat16)
        ] * slices,
        in_specs=[hbm] * 4 + [vmem] * 4,
        out_specs=[vmem] * slices,
        scratch_shapes=[
            pltpu.VMEM((rows, width), jnp.bfloat16),
            pltpu.VMEM((rows, width), jnp.bfloat16),
            pltpu.VMEM((rank, width), jnp.bfloat16),
            pltpu.VMEM((rank, width), jnp.bfloat16),
            pltpu.VMEM((batch * tokens, rank), jnp.bfloat16),
            pltpu.VMEM((batch * tokens, rank), jnp.bfloat16),
            pltpu.VMEM((2, rank, batch * tokens), jnp.float32),
            pltpu.VMEM((half, examples, 2 * rank), jnp.float32),
            pltpu.SemaphoreType.DMA((steps,)),
            pltpu.SemaphoreType.DMA((steps,)),
            pltpu.SemaphoreType.DMA((2,)),
        ],
        compiler_params=pltpu.CompilerParams(vmem_limit_bytes=60 * 2**20),
        cost_estimate=pl.CostEstimate(
            flops=4 * rows * width * rank, bytes_accessed=4 * rows * width, transcendentals=0),
        name="features",
    )(
        activations.reshape(rows, width), out_grads.reshape(rows, width),
        proj_in.T, proj_out.T, basis_in, basis_out, eigen, doc_ids.reshape(1, examples),
    )


def slice_order(slices):
    return [0] + list(range(slices - 1, 0, -1))


def product_kernel(slices, pieces, examples, row_groups, column_groups, *refs):
    runs = slices // pieces
    slabs = row_groups - 1 + 2 * column_groups
    ins, outs = refs[:runs * slabs], refs[runs * slabs:runs * slabs + slices]
    ids_ref, column_stack, row_stack, result = refs[runs * slabs + slices:]
    piece_rows, lanes = ins[0].shape
    piece_rows = piece_rows // pieces
    depth = (piece_rows - id_rows) // examples
    cols = column_stack.shape[0]
    mem = lax.axis_index("mem")
    pair, core = mem // cores, mem % cores

    def place(stack, row, ref, piece):
        start = pl.multiple_of(row * examples, examples)
        for part in range(depth):
            stack[pl.ds(start, examples), pl.ds(part * lanes, lanes)] = (
                ref[pl.ds(piece * piece_rows + part * examples, examples)])

    block = lax.broadcasted_iota(jnp.int32, (id_rows, cols), 1) // examples
    digits = jnp.zeros((id_rows, cols), jnp.float32)
    for run in range(runs):
        part = ins[run * slabs:(run + 1) * slabs]
        columns, others = part[:column_groups], part[column_groups:2 * column_groups]
        rows = (columns[0],) + tuple(part[2 * column_groups:])
        for piece in range(pieces):
            place_of = pair ^ slice_order(slices)[run * pieces + piece]
            for group in range(column_groups):
                for ref, side in ((columns[group], core), (others[group], core ^ 1)):
                    column = (group * slices + place_of) * cores + side
                    place(column_stack, column, ref, piece)
                    some = ref[pl.ds((piece + 1) * piece_rows - id_rows, id_rows)].astype(jnp.float32)
                    some = jnp.concatenate([some] * (cols // lanes), axis=1)
                    digits = jnp.where(block == column, some, digits)
            for group in range(row_groups):
                place(row_stack, place_of * row_groups + group, rows[group], piece)
    result[...] = dot_nt(row_stack[...], column_stack[...]).astype(jnp.bfloat16)
    count = row_groups * examples
    for index in range(slices):
        start = pl.multiple_of((pair ^ index) * count, count)
        outs[index][...] = result[pl.ds(start, count)]
    ids_ref[pl.ds(0, 1)] = digits[0:1] + digits[1:2] * 256.0
    ids_ref[pl.ds(1, 1)] = digits[2:3] + digits[3:4] * 256.0


def products(slabs, slices, pieces, examples, row_groups, column_groups):
    piece_rows, lanes = slabs[0].shape
    depth = (piece_rows // pieces - id_rows) // examples
    vmem = pl.BlockSpec(memory_space=pltpu.VMEM)
    rows, cols = row_groups * slices * examples, column_groups * slices * cores * examples
    return pl.pallas_call(
        functools.partial(product_kernel, slices, pieces, examples, row_groups, column_groups),
        out_shape=[jax.ShapeDtypeStruct((row_groups * examples, cols), jnp.bfloat16)] * slices
        + [jax.ShapeDtypeStruct((2, cols), jnp.float32)],
        in_specs=[vmem] * len(slabs),
        out_specs=[vmem] * (slices + 1),
        scratch_shapes=[
            pltpu.VMEM((cols, depth * lanes), jnp.bfloat16),
            pltpu.VMEM((rows, depth * lanes), jnp.bfloat16),
            pltpu.VMEM((rows, cols), jnp.bfloat16),
        ],
        compiler_params=pltpu.CompilerParams(vmem_limit_bytes=40 * 2**20),
        cost_estimate=pl.CostEstimate(
            flops=2 * rows * cols * depth * lanes, bytes_accessed=4 * rows * cols, transcendentals=0),
        name="products",
    )(*slabs)


def total_kernel(slices, ids_ref, *refs):
    parts, outs = refs[:slices], refs[slices:]
    examples = outs[0].shape[0]
    for group, out in enumerate(outs):
        rng = pl.ds(group * examples, examples)
        out[pl.ds(0, examples)] = sum(part[rng].astype(jnp.float32) for part in parts)
        if group:
            out[pl.ds(examples, 2)] = ids_ref[...]


def totals(parts, ids, examples):
    rows, cols = parts[0].shape
    groups = rows // examples
    vmem = pl.BlockSpec(memory_space=pltpu.VMEM)
    return pl.pallas_call(
        functools.partial(total_kernel, len(parts)),
        out_shape=[
            jax.ShapeDtypeStruct((examples + (8 if group else 0), cols), jnp.float32)
            for group in range(groups)
        ],
        in_specs=[vmem] * (1 + len(parts)),
        out_specs=[vmem] * groups,
        compiler_params=pltpu.CompilerParams(vmem_limit_bytes=40 * 2**20),
        cost_estimate=pl.CostEstimate(
            flops=rows * cols * len(parts), bytes_accessed=8 * rows * cols, transcendentals=0),
        name="totals",
    )(ids, *parts)


def finish_kernel(factor, column_groups, own_ids_ref, ids_ref, *refs):
    parts, out_ref = refs[:-1], refs[-1]
    examples, cols = parts[0].shape
    width = cols // column_groups
    grp = lax.axis_index("grp")
    own_ids = own_ids_ref[...]
    own_low = (own_ids & 0xFFFF).astype(jnp.float32)
    own_high = ((own_ids >> 16) & 0xFFFF).astype(jnp.float32)
    for row_step, part in enumerate(parts):
        low, high = (part[pl.ds(examples + row, 1)] if row_step else ids_ref[pl.ds(row, 1)]
                     for row in range(2))
        value = part[pl.ds(0, examples)] * factor
        value = jnp.where((own_low == low) & (own_high == high), 0.0, value)
        for column_step in range(column_groups):
            start = (grp ^ row_step ^ (column_step * len(parts))) * width
            out_ref[:, pl.ds(pl.multiple_of(start, width), width)] = (
                value[:, column_step * width:(column_step + 1) * width])


def finish(own_ids, ids, parts, column_groups, factor):
    examples, cols = parts[0].shape
    vmem = pl.BlockSpec(memory_space=pltpu.VMEM)
    return pl.pallas_call(
        functools.partial(finish_kernel, factor, column_groups),
        out_shape=jax.ShapeDtypeStruct((examples, len(parts) * cols), jnp.float32),
        in_specs=[vmem] * (2 + len(parts)),
        out_specs=vmem,
        compiler_params=pltpu.CompilerParams(vmem_limit_bytes=40 * 2**20),
        cost_estimate=pl.CostEstimate(
            flops=8 * examples * cols, bytes_accessed=16 * examples * cols, transcendentals=0),
        name="finish",
    )(own_ids, ids, *parts)


def swap(value, axis, size, distance):
    if distance == 0:
        return value
    return lax.ppermute(value, axis, [(place, place ^ distance) for place in range(size)])


def on_device(members, groups, activations, out_grads, proj_in, proj_out, basis_in, basis_out, eigen, doc_ids):
    examples, tokens, width = activations.shape
    rank = proj_in.shape[1]
    factor = 1.0 / (tokens * rank)
    slices = members // cores
    runs = 2
    pieces = slices // runs
    row_groups = 1 << ((groups.bit_length() - 1) // 2)
    column_groups = groups // row_groups
    feat = features(slices, activations, out_grads, proj_in, proj_out, basis_in, basis_out, eigen, doc_ids)
    got = [swap(feat[index], "mem", members, cores * index) for index in slice_order(slices)]
    slabs = []
    for run in range(runs):
        slab = jnp.concatenate(got[run * pieces:(run + 1) * pieces], axis=0)
        columns = [swap(slab, "grp", groups, row_groups * step) for step in range(column_groups)]
        rows = [swap(slab, "grp", groups, step) for step in range(1, row_groups)]
        slabs += columns + [swap(column, "mem", members, 1) for column in columns] + rows
    *partial, ids = products(slabs, slices, pieces, examples, row_groups, column_groups)
    parts = [swap(partial[index], "mem", members, cores * index) for index in slice_order(slices)]
    sums = totals(parts, ids, examples)
    sums = [swap(value, "grp", groups, step) for step, value in enumerate(sums)]
    return finish(doc_ids[:, None], ids, sums, column_groups, factor)


def solution(mesh):
    return jax.shard_map(
        functools.partial(on_device, mesh.shape["mem"], mesh.shape["grp"]),
        mesh=mesh,
        in_specs=(
            P(("grp", "mem"), None, None),
            P(("grp", "mem"), None, None),
            P(),
            P(),
            P(),
            P(),
            P(),
            P(("grp", "mem")),
        ),
        out_specs=P(("grp", "mem"), None),
        check_vma=False,
    )
```

```python
import functools
import jax
import jax.numpy as jnp
from jax import lax
from jax.experimental import pallas as pl
from jax.experimental.pallas import tpu as pltpu
from jax.sharding import PartitionSpec as P

damping = 0.1
batch = 8
id_rows = 16
cores = 2


def dot_nn(a, b):
    return lax.dot_general(a, b, (((1,), (0,)), ((), ())), preferred_element_type=jnp.float32)


def dot_nt(a, b):
    return lax.dot_general(a, b, (((1,), (1,)), ((), ())), preferred_element_type=jnp.float32)


def split_two(value):
    high = value.astype(jnp.bfloat16)
    low = (value - high.astype(jnp.float32)).astype(jnp.bfloat16)
    return high, low


def feature_kernel(
    tokens, slices, act_hbm, grad_hbm, pin_hbm, pout_hbm, bin_ref, bout_ref, eigen_ref, ids_ref, *refs
):
    out_refs = refs[:slices]
    act, grad, pin, pout, act_proj, grad_proj, gt_ref, feat, act_sem, grad_sem, w_sem = refs[slices:]
    rows, width = act.shape
    rank = bin_ref.shape[0]
    half = rank // 2
    step_rows = batch * tokens
    steps = rows // step_rows
    examples = feat.shape[1]

    def step_copies(step):
        rng = pl.ds(pl.multiple_of(step * step_rows, step_rows), step_rows)
        return (
            pltpu.make_async_copy(act_hbm.at[rng], act.at[rng], act_sem.at[step]),
            pltpu.make_async_copy(grad_hbm.at[rng], grad.at[rng], grad_sem.at[step]),
        )

    weights = [
        pltpu.make_async_copy(pin_hbm, pin, w_sem.at[0]),
        pltpu.make_async_copy(pout_hbm, pout, w_sem.at[1]),
    ]
    def start_step(step):
        for priority, copy in enumerate(step_copies(step)):
            copy.start(priority=priority)

    for copy in weights:
        copy.start()
    for step in range(steps):
        start_step(step)

    bin_hi, bin_lo = split_two(jnp.concatenate([bin_ref[...], bin_ref[...]], axis=1))
    bout_hi, bout_lo = split_two(bout_ref[...].T)
    inverse = 1.0 / jnp.sqrt(eigen_ref[...] + damping)
    inverse = jnp.concatenate([inverse[:half], inverse[half:]], axis=1)
    own_token = (
        lax.broadcasted_iota(jnp.int32, (batch, step_rows), 1) // tokens
        == lax.broadcasted_iota(jnp.int32, (batch, step_rows), 0)
    )
    first_lanes = lax.broadcasted_iota(jnp.int32, (batch, 2 * rank), 1) < rank
    ids = jnp.concatenate([ids_ref[...]] * (2 * rank // examples), axis=1)
    place = lax.broadcasted_iota(jnp.int32, (id_rows, 2 * rank), 0) % 4
    digits = (jnp.broadcast_to(ids, (id_rows, 2 * rank)) >> (place * 8)) & 255
    digits = digits.astype(jnp.float32).astype(jnp.bfloat16)
    for copy in weights:
        copy.wait()

    def project(step):
        for copy in step_copies(step):
            copy.wait()
        rng = pl.ds(pl.multiple_of(step * step_rows, step_rows), step_rows)
        first, second = pl.ds(0, width // 2), pl.ds(width // 2, width // 2)
        return (
            (dot_nt(act[rng, first], pin[:, first]) + dot_nt(act[rng, second], pin[:, second])
             ).astype(jnp.bfloat16),
            (dot_nt(pout[:, first], grad[rng, first]) + dot_nt(pout[:, second], grad[rng, second])
             ).astype(jnp.bfloat16),
        )

    def rotate(step, act_part, grad_part):
        act_hi, act_lo = split_two(dot_nn(act_part, bin_hi) + dot_nn(act_part, bin_lo))
        grad_hi, grad_lo = split_two(dot_nn(bout_hi, grad_part) + dot_nn(bout_lo, grad_part))
        gt_ref[0] = grad_hi.astype(jnp.float32)
        gt_ref[1] = grad_lo.astype(jnp.float32)
        spread_hi, spread_lo = [
            jnp.concatenate([
                jnp.where(own_token, jnp.broadcast_to(gt_ref[part, pl.ds(u, 1)], (batch, step_rows)), 0.0)
                for u in range(rank)
            ], axis=0).astype(jnp.bfloat16)
            for part in range(2)
        ]
        wide = dot_nn(spread_hi, jnp.concatenate([act_hi, act_lo], axis=1))
        rotated = wide[:, :2 * rank] + wide[:, 2 * rank:] + dot_nn(spread_lo, act_hi)
        start = pl.multiple_of(step * batch, batch)
        for u in range(half):
            value = jnp.where(
                first_lanes,
                rotated[u * batch:(u + 1) * batch],
                rotated[(u + half) * batch:(u + half + 1) * batch],
            ) * inverse[u:u + 1]
            feat[u, pl.ds(start, batch)] = value

    act_proj[...], grad_proj[...] = project(0)

    def body(step, carry):
        act_part, grad_part = act_proj[...], grad_proj[...]
        act_next, grad_next = project(step)
        rotate(step - 1, act_part, grad_part)
        act_proj[...] = act_next
        grad_proj[...] = grad_next
        return carry

    lax.fori_loop(1, steps, body, 0)
    rotate(steps - 1, act_proj[...], grad_proj[...])
    depth = half // slices
    me = lax.axis_index("mem") // cores
    for index in range(slices):
        start = (me ^ index) * depth
        piece = feat[pl.ds(start, depth)].astype(jnp.bfloat16)
        out_refs[index][pl.ds(0, depth * examples)] = piece.reshape(depth * examples, 2 * rank)
        out_refs[index][pl.ds(depth * examples, id_rows)] = digits


def features(slices, activations, out_grads, proj_in, proj_out, basis_in, basis_out, eigen, doc_ids):
    examples, tokens, width = activations.shape
    rank = proj_in.shape[1]
    rows = examples * tokens
    steps = examples // batch
    half = rank // 2
    hbm = pl.BlockSpec(memory_space=pl.ANY)
    vmem = pl.BlockSpec(memory_space=pltpu.VMEM)
    return pl.pallas_call(
        functools.partial(feature_kernel, tokens, slices),
        out_shape=[
            jax.ShapeDtypeStruct((half // slices * examples + id_rows, 2 * rank), jnp.bfloat16)
        ] * slices,
        in_specs=[hbm] * 4 + [vmem] * 4,
        out_specs=[vmem] * slices,
        scratch_shapes=[
            pltpu.VMEM((rows, width), jnp.bfloat16),
            pltpu.VMEM((rows, width), jnp.bfloat16),
            pltpu.VMEM((rank, width), jnp.bfloat16),
            pltpu.VMEM((rank, width), jnp.bfloat16),
            pltpu.VMEM((batch * tokens, rank), jnp.bfloat16),
            pltpu.VMEM((rank, batch * tokens), jnp.bfloat16),
            pltpu.VMEM((2, rank, batch * tokens), jnp.float32),
            pltpu.VMEM((half, examples, 2 * rank), jnp.float32),
            pltpu.SemaphoreType.DMA((steps,)),
            pltpu.SemaphoreType.DMA((steps,)),
            pltpu.SemaphoreType.DMA((2,)),
        ],
        compiler_params=pltpu.CompilerParams(vmem_limit_bytes=60 * 2**20),
        cost_estimate=pl.CostEstimate(
            flops=4 * rows * width * rank, bytes_accessed=4 * rows * width, transcendentals=0),
        name="features",
    )(
        activations.reshape(rows, width), out_grads.reshape(rows, width),
        proj_in.T, proj_out.T, basis_in, basis_out, eigen, doc_ids.reshape(1, examples),
    )


def slice_order(slices):
    return [0] + list(range(slices - 1, 0, -1))


def product_kernel(slices, pieces, examples, row_groups, column_groups, *refs):
    runs = slices // pieces
    slabs = row_groups - 1 + 2 * column_groups
    ins, outs = refs[:runs * slabs], refs[runs * slabs:runs * slabs + slices]
    ids_ref, column_stack, row_stack, result = refs[runs * slabs + slices:]
    piece_rows, lanes = ins[0].shape
    piece_rows = piece_rows // pieces
    depth = (piece_rows - id_rows) // examples
    cols = column_stack.shape[0]
    mem = lax.axis_index("mem")
    pair, core = mem // cores, mem % cores

    def place(stack, row, ref, piece):
        start = pl.multiple_of(row * examples, examples)
        for part in range(depth):
            stack[pl.ds(start, examples), pl.ds(part * lanes, lanes)] = (
                ref[pl.ds(piece * piece_rows + part * examples, examples)])

    block = lax.broadcasted_iota(jnp.int32, (id_rows, cols), 1) // examples
    digits = jnp.zeros((id_rows, cols), jnp.float32)
    for run in range(runs):
        part = ins[run * slabs:(run + 1) * slabs]
        columns, others = part[:column_groups], part[column_groups:2 * column_groups]
        rows = (columns[0],) + tuple(part[2 * column_groups:])
        for piece in range(pieces):
            place_of = pair ^ slice_order(slices)[run * pieces + piece]
            for group in range(column_groups):
                for ref, side in ((columns[group], core), (others[group], core ^ 1)):
                    column = (group * slices + place_of) * cores + side
                    place(column_stack, column, ref, piece)
                    some = ref[pl.ds((piece + 1) * piece_rows - id_rows, id_rows)].astype(jnp.float32)
                    some = jnp.concatenate([some] * (cols // lanes), axis=1)
                    digits = jnp.where(block == column, some, digits)
            for group in range(row_groups):
                place(row_stack, place_of * row_groups + group, rows[group], piece)
    result[...] = dot_nt(row_stack[...], column_stack[...]).astype(jnp.bfloat16)
    count = row_groups * examples
    for index in range(slices):
        start = pl.multiple_of((pair ^ index) * count, count)
        outs[index][...] = result[pl.ds(start, count)]
    ids_ref[...] = digits.astype(jnp.bfloat16)


def products(slabs, slices, pieces, examples, row_groups, column_groups):
    piece_rows, lanes = slabs[0].shape
    depth = (piece_rows // pieces - id_rows) // examples
    vmem = pl.BlockSpec(memory_space=pltpu.VMEM)
    rows, cols = row_groups * slices * examples, column_groups * slices * cores * examples
    return pl.pallas_call(
        functools.partial(product_kernel, slices, pieces, examples, row_groups, column_groups),
        out_shape=[jax.ShapeDtypeStruct((row_groups * examples, cols), jnp.bfloat16)] * slices
        + [jax.ShapeDtypeStruct((id_rows, cols), jnp.bfloat16)],
        in_specs=[vmem] * len(slabs),
        out_specs=[vmem] * (slices + 1),
        scratch_shapes=[
            pltpu.VMEM((cols, depth * lanes), jnp.bfloat16),
            pltpu.VMEM((rows, depth * lanes), jnp.bfloat16),
            pltpu.VMEM((rows, cols), jnp.bfloat16),
        ],
        compiler_params=pltpu.CompilerParams(vmem_limit_bytes=40 * 2**20),
        cost_estimate=pl.CostEstimate(
            flops=2 * rows * cols * depth * lanes, bytes_accessed=4 * rows * cols, transcendentals=0),
        name="products",
    )(*slabs)


def total_kernel(slices, ids_ref, *refs):
    parts, outs = refs[:slices], refs[slices:]
    examples = outs[0].shape[0]
    for group, out in enumerate(outs):
        rng = pl.ds(group * examples, examples)
        total = sum(part[rng].astype(jnp.float32) for part in parts)
        out[pl.ds(0, examples)] = total.astype(out.dtype)
        if group:
            out[pl.ds(examples, id_rows)] = ids_ref[...]


def totals(parts, ids, examples):
    rows, cols = parts[0].shape
    groups = rows // examples
    vmem = pl.BlockSpec(memory_space=pltpu.VMEM)
    return pl.pallas_call(
        functools.partial(total_kernel, len(parts)),
        out_shape=[
            jax.ShapeDtypeStruct((examples + id_rows, cols), jnp.bfloat16) if group
            else jax.ShapeDtypeStruct((examples, cols), jnp.float32)
            for group in range(groups)
        ],
        in_specs=[vmem] * (1 + len(parts)),
        out_specs=[vmem] * groups,
        compiler_params=pltpu.CompilerParams(vmem_limit_bytes=40 * 2**20),
        cost_estimate=pl.CostEstimate(
            flops=rows * cols * len(parts), bytes_accessed=8 * rows * cols, transcendentals=0),
        name="totals",
    )(ids, *parts)


def finish_kernel(factor, column_groups, own_ids_ref, ids_ref, *refs):
    parts, out_ref = refs[:-1], refs[-1]
    examples, cols = parts[0].shape
    width = cols // column_groups
    grp = lax.axis_index("grp")
    own_ids = own_ids_ref[...]
    own_low = (own_ids & 0xFFFF).astype(jnp.float32)
    own_high = ((own_ids >> 16) & 0xFFFF).astype(jnp.float32)
    for row_step, part in enumerate(parts):
        digits = part[pl.ds(examples, id_rows)] if row_step else ids_ref[...]
        digits = digits.astype(jnp.float32)
        low, high = (digits[row:row + 1] + digits[row + 1:row + 2] * 256.0 for row in (0, 2))
        value = part[pl.ds(0, examples)].astype(jnp.float32) * factor
        value = jnp.where((own_low == low) & (own_high == high), 0.0, value)
        for column_step in range(column_groups):
            start = (grp ^ row_step ^ (column_step * len(parts))) * width
            out_ref[:, pl.ds(pl.multiple_of(start, width), width)] = (
                value[:, column_step * width:(column_step + 1) * width])


def finish(own_ids, ids, parts, column_groups, factor):
    examples, cols = parts[0].shape
    vmem = pl.BlockSpec(memory_space=pltpu.VMEM)
    return pl.pallas_call(
        functools.partial(finish_kernel, factor, column_groups),
        out_shape=jax.ShapeDtypeStruct((examples, len(parts) * cols), jnp.float32),
        in_specs=[vmem] * (2 + len(parts)),
        out_specs=vmem,
        compiler_params=pltpu.CompilerParams(vmem_limit_bytes=40 * 2**20),
        cost_estimate=pl.CostEstimate(
            flops=8 * examples * cols, bytes_accessed=16 * examples * cols, transcendentals=0),
        name="finish",
    )(own_ids, ids, *parts)


def swap(value, axis, size, distance):
    if distance == 0:
        return value
    return lax.ppermute(value, axis, [(place, place ^ distance) for place in range(size)])


def on_device(members, groups, activations, out_grads, proj_in, proj_out, basis_in, basis_out, eigen, doc_ids):
    examples, tokens, width = activations.shape
    rank = proj_in.shape[1]
    factor = 1.0 / (tokens * rank)
    slices = members // cores
    runs = 2
    pieces = slices // runs
    row_groups = 1 << ((groups.bit_length() - 1) // 2)
    column_groups = groups // row_groups
    feat = features(slices, activations, out_grads, proj_in, proj_out, basis_in, basis_out, eigen, doc_ids)
    got = [swap(feat[index], "mem", members, cores * index) for index in slice_order(slices)]
    slabs = []
    for run in range(runs):
        slab = jnp.concatenate(got[run * pieces:(run + 1) * pieces], axis=0)
        if run:
            slab, slabs[column_groups] = lax.optimization_barrier((slab, slabs[column_groups]))
        columns = [swap(slab, "grp", groups, row_groups * step) for step in range(column_groups)]
        rows = [swap(slab, "grp", groups, step) for step in range(1, row_groups)]
        slabs += columns + [swap(column, "mem", members, 1) for column in columns] + rows
    *partial, ids = products(slabs, slices, pieces, examples, row_groups, column_groups)
    parts = [swap(partial[index], "mem", members, cores * index) for index in slice_order(slices)]
    sums = totals(parts, ids, examples)
    sums = [swap(value, "grp", groups, step) for step, value in enumerate(sums)]
    return finish(doc_ids[:, None], ids, sums, column_groups, factor)


def solution(mesh):
    return jax.shard_map(
        functools.partial(on_device, mesh.shape["mem"], mesh.shape["grp"]),
        mesh=mesh,
        in_specs=(
            P(("grp", "mem"), None, None),
            P(("grp", "mem"), None, None),
            P(),
            P(),
            P(),
            P(),
            P(),
            P(("grp", "mem")),
        ),
        out_specs=P(("grp", "mem"), None),
        check_vma=False,
    )
```

```python
import functools
import jax
import jax.numpy as jnp
from jax import lax
from jax.experimental import pallas as pl
from jax.experimental.pallas import tpu as pltpu
from jax.sharding import PartitionSpec as P

damping = 0.1
blocks = 8
batch = 8
id_rows = 16
cores = 2


def dot_nn(a, b):
    return lax.dot_general(a, b, (((1,), (0,)), ((), ())), preferred_element_type=jnp.float32)


def dot_nt(a, b):
    return lax.dot_general(a, b, (((1,), (1,)), ((), ())), preferred_element_type=jnp.float32)


def split_two(value):
    high = value.astype(jnp.bfloat16)
    low = (value - high.astype(jnp.float32)).astype(jnp.bfloat16)
    return high, low


def feature_kernel(
    tokens, slices, act_hbm, grad_hbm, pin_hbm, pout_hbm, bin_ref, bout_ref, eigen_ref, ids_ref, *refs
):
    out_refs = refs[:slices]
    act, grad, pin, pout, act_proj, grad_proj, gt_ref, feat, act_sem, grad_sem, w_sem = refs[slices:]
    rows, width = act.shape
    rank = bin_ref.shape[0]
    half = rank // 2
    step_rows = batch * tokens
    steps = rows // step_rows
    examples = feat.shape[1]

    def step_copies(step):
        copies = []
        for block in range(blocks):
            start = step * step_rows + block * (step_rows // blocks)
            rng = pl.ds(pl.multiple_of(start, step_rows // blocks), step_rows // blocks)
            copies.append(pltpu.make_async_copy(act_hbm.at[rng], act.at[rng], act_sem.at[step, block]))
            copies.append(pltpu.make_async_copy(grad_hbm.at[rng], grad.at[rng], grad_sem.at[step, block]))
        return copies

    weights = [
        pltpu.make_async_copy(pin_hbm, pin, w_sem.at[0]),
        pltpu.make_async_copy(pout_hbm, pout, w_sem.at[1]),
    ]
    def start_step(step):
        for index, copy in enumerate(step_copies(step)):
            copy.start(priority=index // 2 % 2)

    for copy in weights:
        copy.start()
    for step in range(steps):
        start_step(step)

    bin_hi, bin_lo = split_two(jnp.concatenate([bin_ref[...], bin_ref[...]], axis=1))
    bout_hi, bout_lo = split_two(bout_ref[...].T)
    inverse = 1.0 / jnp.sqrt(eigen_ref[...] + damping)
    inverse = jnp.concatenate([inverse[:half], inverse[half:]], axis=1)
    own_token = (
        lax.broadcasted_iota(jnp.int32, (batch, step_rows), 1) // tokens
        == lax.broadcasted_iota(jnp.int32, (batch, step_rows), 0)
    )
    first_lanes = lax.broadcasted_iota(jnp.int32, (batch, 2 * rank), 1) < rank
    ids = jnp.concatenate([ids_ref[...]] * (2 * rank // examples), axis=1)
    place = lax.broadcasted_iota(jnp.int32, (id_rows, 2 * rank), 0) % 4
    digits = (jnp.broadcast_to(ids, (id_rows, 2 * rank)) >> (place * 8)) & 255
    digits = digits.astype(jnp.float32).astype(jnp.bfloat16)
    for copy in weights:
        copy.wait()

    def project(step):
        for copy in step_copies(step):
            copy.wait()
        rng = pl.ds(pl.multiple_of(step * step_rows, step_rows), step_rows)
        first, second = pl.ds(0, width // 2), pl.ds(width // 2, width // 2)
        return (
            (dot_nt(act[rng, first], pin[:, first]) + dot_nt(act[rng, second], pin[:, second])
             ).astype(jnp.bfloat16),
            (dot_nt(pout[:, first], grad[rng, first]) + dot_nt(pout[:, second], grad[rng, second])
             ).astype(jnp.bfloat16),
        )

    def rotate(step, act_part, grad_part):
        act_hi, act_lo = split_two(dot_nn(act_part, bin_hi) + dot_nn(act_part, bin_lo))
        grad_hi, grad_lo = split_two(dot_nn(bout_hi, grad_part) + dot_nn(bout_lo, grad_part))
        gt_ref[0] = grad_hi.astype(jnp.float32)
        gt_ref[1] = grad_lo.astype(jnp.float32)
        spread_hi, spread_lo = [
            jnp.concatenate([
                jnp.where(own_token, jnp.broadcast_to(gt_ref[part, pl.ds(u, 1)], (batch, step_rows)), 0.0)
                for u in range(rank)
            ], axis=0).astype(jnp.bfloat16)
            for part in range(2)
        ]
        wide = dot_nn(spread_hi, jnp.concatenate([act_hi, act_lo], axis=1))
        rotated = wide[:, :2 * rank] + wide[:, 2 * rank:] + dot_nn(spread_lo, act_hi)
        start = pl.multiple_of(step * batch, batch)
        for u in range(half):
            value = jnp.where(
                first_lanes,
                rotated[u * batch:(u + 1) * batch],
                rotated[(u + half) * batch:(u + half + 1) * batch],
            ) * inverse[u:u + 1]
            feat[u, pl.ds(start, batch)] = value

    act_proj[...], grad_proj[...] = project(0)

    def body(step, carry):
        act_part, grad_part = act_proj[...], grad_proj[...]
        act_next, grad_next = project(step)
        rotate(step - 1, act_part, grad_part)
        act_proj[...] = act_next
        grad_proj[...] = grad_next
        return carry

    lax.fori_loop(1, steps, body, 0)
    rotate(steps - 1, act_proj[...], grad_proj[...])
    depth = half // slices
    me = lax.axis_index("mem") // cores
    for index in range(slices):
        start = (me ^ index) * depth
        piece = feat[pl.ds(start, depth)].astype(jnp.bfloat16)
        out_refs[index][pl.ds(0, depth * examples)] = piece.reshape(depth * examples, 2 * rank)
        out_refs[index][pl.ds(depth * examples, id_rows)] = digits


def features(slices, activations, out_grads, proj_in, proj_out, basis_in, basis_out, eigen, doc_ids):
    examples, tokens, width = activations.shape
    rank = proj_in.shape[1]
    rows = examples * tokens
    steps = examples // batch
    half = rank // 2
    hbm = pl.BlockSpec(memory_space=pl.ANY)
    vmem = pl.BlockSpec(memory_space=pltpu.VMEM)
    return pl.pallas_call(
        functools.partial(feature_kernel, tokens, slices),
        out_shape=[
            jax.ShapeDtypeStruct((half // slices * examples + id_rows, 2 * rank), jnp.bfloat16)
        ] * slices,
        in_specs=[hbm] * 4 + [vmem] * 4,
        out_specs=[vmem] * slices,
        scratch_shapes=[
            pltpu.VMEM((rows, width), jnp.bfloat16),
            pltpu.VMEM((rows, width), jnp.bfloat16),
            pltpu.VMEM((rank, width), jnp.bfloat16),
            pltpu.VMEM((rank, width), jnp.bfloat16),
            pltpu.VMEM((batch * tokens, rank), jnp.bfloat16),
            pltpu.VMEM((rank, batch * tokens), jnp.bfloat16),
            pltpu.VMEM((2, rank, batch * tokens), jnp.float32),
            pltpu.VMEM((half, examples, 2 * rank), jnp.float32),
            pltpu.SemaphoreType.DMA((steps, blocks)),
            pltpu.SemaphoreType.DMA((steps, blocks)),
            pltpu.SemaphoreType.DMA((2,)),
        ],
        compiler_params=pltpu.CompilerParams(vmem_limit_bytes=60 * 2**20),
        cost_estimate=pl.CostEstimate(
            flops=4 * rows * width * rank, bytes_accessed=4 * rows * width, transcendentals=0),
        name="features",
    )(
        activations.reshape(rows, width), out_grads.reshape(rows, width),
        proj_in.T, proj_out.T, basis_in, basis_out, eigen, doc_ids.reshape(1, examples),
    )


def slice_order(slices):
    return [0] + list(range(slices - 1, 0, -1))


def product_kernel(slices, pieces, examples, row_groups, column_groups, *refs):
    runs = slices // pieces
    slabs = row_groups - 1 + 2 * column_groups
    ins, outs = refs[:runs * slabs], refs[runs * slabs:runs * slabs + slices]
    ids_ref, column_stack, row_stack, result = refs[runs * slabs + slices:]
    piece_rows, lanes = ins[0].shape
    piece_rows = piece_rows // pieces
    depth = (piece_rows - id_rows) // examples
    cols = column_stack.shape[0]
    mem = lax.axis_index("mem")
    pair, core = mem // cores, mem % cores

    def place(stack, row, ref, piece):
        start = pl.multiple_of(row * examples, examples)
        for part in range(depth):
            stack[pl.ds(start, examples), pl.ds(part * lanes, lanes)] = (
                ref[pl.ds(piece * piece_rows + part * examples, examples)])

    block = lax.broadcasted_iota(jnp.int32, (id_rows, cols), 1) // examples
    digits = jnp.zeros((id_rows, cols), jnp.float32)
    for run in range(runs):
        part = ins[run * slabs:(run + 1) * slabs]
        columns, others = part[:column_groups], part[column_groups:2 * column_groups]
        rows = (columns[0],) + tuple(part[2 * column_groups:])
        for piece in range(pieces):
            place_of = pair ^ slice_order(slices)[run * pieces + piece]
            for group in range(column_groups):
                for ref, side in ((columns[group], core), (others[group], core ^ 1)):
                    column = (group * slices + place_of) * cores + side
                    place(column_stack, column, ref, piece)
                    some = ref[pl.ds((piece + 1) * piece_rows - id_rows, id_rows)].astype(jnp.float32)
                    some = jnp.concatenate([some] * (cols // lanes), axis=1)
                    digits = jnp.where(block == column, some, digits)
            for group in range(row_groups):
                place(row_stack, place_of * row_groups + group, rows[group], piece)
    result[...] = dot_nt(row_stack[...], column_stack[...]).astype(jnp.bfloat16)
    count = row_groups * examples
    for index in range(slices):
        start = pl.multiple_of((pair ^ index) * count, count)
        outs[index][...] = result[pl.ds(start, count)]
    ids_ref[...] = digits.astype(jnp.bfloat16)


def products(slabs, slices, pieces, examples, row_groups, column_groups):
    piece_rows, lanes = slabs[0].shape
    depth = (piece_rows // pieces - id_rows) // examples
    vmem = pl.BlockSpec(memory_space=pltpu.VMEM)
    rows, cols = row_groups * slices * examples, column_groups * slices * cores * examples
    return pl.pallas_call(
        functools.partial(product_kernel, slices, pieces, examples, row_groups, column_groups),
        out_shape=[jax.ShapeDtypeStruct((row_groups * examples, cols), jnp.bfloat16)] * slices
        + [jax.ShapeDtypeStruct((id_rows, cols), jnp.bfloat16)],
        in_specs=[vmem] * len(slabs),
        out_specs=[vmem] * (slices + 1),
        scratch_shapes=[
            pltpu.VMEM((cols, depth * lanes), jnp.bfloat16),
            pltpu.VMEM((rows, depth * lanes), jnp.bfloat16),
            pltpu.VMEM((rows, cols), jnp.bfloat16),
        ],
        compiler_params=pltpu.CompilerParams(vmem_limit_bytes=40 * 2**20),
        cost_estimate=pl.CostEstimate(
            flops=2 * rows * cols * depth * lanes, bytes_accessed=4 * rows * cols, transcendentals=0),
        name="products",
    )(*slabs)


def total_kernel(slices, ids_ref, *refs):
    parts, outs = refs[:slices], refs[slices:]
    examples = outs[0].shape[0]
    for group, out in enumerate(outs):
        rng = pl.ds(group * examples, examples)
        total = sum(part[rng].astype(jnp.float32) for part in parts)
        out[pl.ds(0, examples)] = total.astype(out.dtype)
        if group:
            out[pl.ds(examples, id_rows)] = ids_ref[...]


def totals(parts, ids, examples):
    rows, cols = parts[0].shape
    groups = rows // examples
    vmem = pl.BlockSpec(memory_space=pltpu.VMEM)
    return pl.pallas_call(
        functools.partial(total_kernel, len(parts)),
        out_shape=[
            jax.ShapeDtypeStruct((examples + id_rows, cols), jnp.bfloat16) if group
            else jax.ShapeDtypeStruct((examples, cols), jnp.float32)
            for group in range(groups)
        ],
        in_specs=[vmem] * (1 + len(parts)),
        out_specs=[vmem] * groups,
        compiler_params=pltpu.CompilerParams(vmem_limit_bytes=40 * 2**20),
        cost_estimate=pl.CostEstimate(
            flops=rows * cols * len(parts), bytes_accessed=8 * rows * cols, transcendentals=0),
        name="totals",
    )(ids, *parts)


def finish_kernel(factor, column_groups, own_ids_ref, ids_ref, *refs):
    parts, out_ref = refs[:-1], refs[-1]
    examples, cols = parts[0].shape
    width = cols // column_groups
    grp = lax.axis_index("grp")
    own_ids = own_ids_ref[...]
    own_low = (own_ids & 0xFFFF).astype(jnp.float32)
    own_high = ((own_ids >> 16) & 0xFFFF).astype(jnp.float32)
    for row_step, part in enumerate(parts):
        digits = part[pl.ds(examples, id_rows)] if row_step else ids_ref[...]
        digits = digits.astype(jnp.float32)
        low, high = (digits[row:row + 1] + digits[row + 1:row + 2] * 256.0 for row in (0, 2))
        value = part[pl.ds(0, examples)].astype(jnp.float32) * factor
        value = jnp.where((own_low == low) & (own_high == high), 0.0, value)
        for column_step in range(column_groups):
            start = (grp ^ row_step ^ (column_step * len(parts))) * width
            out_ref[:, pl.ds(pl.multiple_of(start, width), width)] = (
                value[:, column_step * width:(column_step + 1) * width])


def finish(own_ids, ids, parts, column_groups, factor):
    examples, cols = parts[0].shape
    vmem = pl.BlockSpec(memory_space=pltpu.VMEM)
    return pl.pallas_call(
        functools.partial(finish_kernel, factor, column_groups),
        out_shape=jax.ShapeDtypeStruct((examples, len(parts) * cols), jnp.float32),
        in_specs=[vmem] * (2 + len(parts)),
        out_specs=vmem,
        compiler_params=pltpu.CompilerParams(vmem_limit_bytes=40 * 2**20),
        cost_estimate=pl.CostEstimate(
            flops=8 * examples * cols, bytes_accessed=16 * examples * cols, transcendentals=0),
        name="finish",
    )(own_ids, ids, *parts)


def swap(value, axis, size, distance):
    if distance == 0:
        return value
    return lax.ppermute(value, axis, [(place, place ^ distance) for place in range(size)])


def on_device(members, groups, activations, out_grads, proj_in, proj_out, basis_in, basis_out, eigen, doc_ids):
    examples, tokens, width = activations.shape
    rank = proj_in.shape[1]
    factor = 1.0 / (tokens * rank)
    slices = members // cores
    runs = 2
    pieces = slices // runs
    row_groups = 1 << ((groups.bit_length() - 1) // 2)
    column_groups = groups // row_groups
    feat = features(slices, activations, out_grads, proj_in, proj_out, basis_in, basis_out, eigen, doc_ids)
    got = [swap(feat[index], "mem", members, cores * index) for index in slice_order(slices)]
    slabs = []
    for run in range(runs):
        slab = jnp.concatenate(got[run * pieces:(run + 1) * pieces], axis=0)
        if run:
            slab, slabs[column_groups] = lax.optimization_barrier((slab, slabs[column_groups]))
        columns = [swap(slab, "grp", groups, row_groups * step) for step in range(column_groups)]
        rows = [swap(slab, "grp", groups, step) for step in range(1, row_groups)]
        slabs += columns + [swap(column, "mem", members, 1) for column in columns] + rows
    *partial, ids = products(slabs, slices, pieces, examples, row_groups, column_groups)
    parts = [swap(partial[index], "mem", members, cores * index) for index in slice_order(slices)]
    sums = totals(parts, ids, examples)
    sums = [swap(value, "grp", groups, step) for step, value in enumerate(sums)]
    return finish(doc_ids[:, None], ids, sums, column_groups, factor)


def solution(mesh):
    return jax.shard_map(
        functools.partial(on_device, mesh.shape["mem"], mesh.shape["grp"]),
        mesh=mesh,
        in_specs=(
            P(("grp", "mem"), None, None),
            P(("grp", "mem"), None, None),
            P(),
            P(),
            P(),
            P(),
            P(),
            P(("grp", "mem")),
        ),
        out_specs=P(("grp", "mem"), None),
        check_vma=False,
    )
```

```python
import functools
import jax
import jax.numpy as jnp
from jax import lax
from jax.experimental import pallas as pl
from jax.experimental.pallas import tpu as pltpu
from jax.sharding import PartitionSpec as P

damping = 0.1
batch = 8
id_rows = 16
cores = 2


def dot_nn(a, b):
    return lax.dot_general(a, b, (((1,), (0,)), ((), ())), preferred_element_type=jnp.float32)


def dot_nt(a, b):
    return lax.dot_general(a, b, (((1,), (1,)), ((), ())), preferred_element_type=jnp.float32)


def split_two(value):
    high = value.astype(jnp.bfloat16)
    low = (value - high.astype(jnp.float32)).astype(jnp.bfloat16)
    return high, low


def feature_kernel(
    tokens, act_hbm, grad_hbm, pin_hbm, pout_hbm, bin_hbm, bout_hbm, eigen_hbm, ids_hbm,
    full_ref, first_ref, second_ref,
    act, grad, pin, pout, bin_ref, bout_ref, eigen_ref, ids_ref, act_proj, grad_proj, gt_ref, feat,
    act_sem, grad_sem, w_sem, s_sem,
):
    rows, width = act.shape
    rank = bin_ref.shape[0]
    half = rank // 2
    step_rows = batch * tokens
    steps = rows // step_rows
    examples = feat.shape[1]

    def step_copies(step):
        rng = pl.ds(pl.multiple_of(step * step_rows, step_rows), step_rows)
        return (
            pltpu.make_async_copy(act_hbm.at[rng], act.at[rng], act_sem.at[step]),
            pltpu.make_async_copy(grad_hbm.at[rng], grad.at[rng], grad_sem.at[step]),
        )

    weights = [
        pltpu.make_async_copy(pin_hbm, pin, w_sem.at[0]),
        pltpu.make_async_copy(pout_hbm, pout, w_sem.at[1]),
    ]
    def start_step(step):
        for priority, copy in enumerate(step_copies(step)):
            copy.start(priority=priority)

    small = [
        pltpu.make_async_copy(source, target, s_sem.at[index])
        for index, (source, target) in enumerate((
            (bin_hbm, bin_ref), (bout_hbm, bout_ref), (eigen_hbm, eigen_ref), (ids_hbm, ids_ref)))
    ]
    for copy in weights:
        copy.start()
    start_step(0)
    for copy in small:
        copy.start()
    for step in range(1, steps):
        start_step(step)
    for copy in small:
        copy.wait()

    bin_hi, bin_lo = split_two(jnp.concatenate([bin_ref[...], bin_ref[...]], axis=1))
    bout_hi, bout_lo = split_two(bout_ref[...].T)
    inverse = 1.0 / jnp.sqrt(eigen_ref[...] + damping)
    inverse = jnp.concatenate([inverse[:half], inverse[half:]], axis=1)
    own_token = (
        lax.broadcasted_iota(jnp.int32, (batch, step_rows), 1) // tokens
        == lax.broadcasted_iota(jnp.int32, (batch, step_rows), 0)
    )
    first_lanes = lax.broadcasted_iota(jnp.int32, (batch, 2 * rank), 1) < rank
    ids = jnp.concatenate([ids_ref[...]] * (2 * rank // examples), axis=1)
    place = lax.broadcasted_iota(jnp.int32, (id_rows, 2 * rank), 0) % 4
    digits = (jnp.broadcast_to(ids, (id_rows, 2 * rank)) >> (place * 8)) & 255
    digits = digits.astype(jnp.float32).astype(jnp.bfloat16)
    for copy in weights:
        copy.wait()

    def project(step):
        for copy in step_copies(step):
            copy.wait()
        rng = pl.ds(pl.multiple_of(step * step_rows, step_rows), step_rows)
        first, second = pl.ds(0, width // 2), pl.ds(width // 2, width // 2)
        return (
            (dot_nt(act[rng, first], pin[:, first]) + dot_nt(act[rng, second], pin[:, second])
             ).astype(jnp.bfloat16),
            (dot_nt(pout[:, first], grad[rng, first]) + dot_nt(pout[:, second], grad[rng, second])
             ).astype(jnp.bfloat16),
        )

    def rotate(step, act_part, grad_part):
        act_hi, act_lo = split_two(dot_nn(act_part, bin_hi) + dot_nn(act_part, bin_lo))
        grad_hi, grad_lo = split_two(dot_nn(bout_hi, grad_part) + dot_nn(bout_lo, grad_part))
        gt_ref[0] = grad_hi.astype(jnp.float32)
        gt_ref[1] = grad_lo.astype(jnp.float32)
        spread_hi, spread_lo = [
            jnp.concatenate([
                jnp.where(own_token, jnp.broadcast_to(gt_ref[part, pl.ds(u, 1)], (batch, step_rows)), 0.0)
                for u in range(rank)
            ], axis=0).astype(jnp.bfloat16)
            for part in range(2)
        ]
        wide = dot_nn(spread_hi, jnp.concatenate([act_hi, act_lo], axis=1))
        rotated = wide[:, :2 * rank] + wide[:, 2 * rank:] + dot_nn(spread_lo, act_hi)
        start = pl.multiple_of(step * batch, batch)
        for u in range(half):
            value = jnp.where(
                first_lanes,
                rotated[u * batch:(u + 1) * batch],
                rotated[(u + half) * batch:(u + half + 1) * batch],
            ) * inverse[u:u + 1]
            feat[u, pl.ds(start, batch)] = value

    act_proj[...], grad_proj[...] = project(0)

    def body(step, carry):
        act_part, grad_part = act_proj[...], grad_proj[...]
        act_next, grad_next = project(step)
        rotate(step - 1, act_part, grad_part)
        act_proj[...] = act_next
        grad_proj[...] = grad_next
        return carry

    lax.fori_loop(1, steps, body, 0)
    rotate(steps - 1, act_proj[...], grad_proj[...])
    slab = feat[...].astype(jnp.bfloat16).reshape(half * examples, 2 * rank)
    full_ref[pl.ds(0, half * examples)] = slab
    full_ref[pl.ds(half * examples, id_rows)] = digits
    cut = first_ref.shape[0]
    first_ref[...] = slab[:cut]
    second_ref[...] = slab[cut:]


def features(activations, out_grads, proj_in, proj_out, basis_in, basis_out, eigen, doc_ids):
    examples, tokens, width = activations.shape
    rank = proj_in.shape[1]
    rows = examples * tokens
    steps = examples // batch
    half = rank // 2
    cut = half * 7 // 16
    hbm = pl.BlockSpec(memory_space=pl.ANY)
    vmem = pl.BlockSpec(memory_space=pltpu.VMEM)
    return pl.pallas_call(
        functools.partial(feature_kernel, tokens),
        out_shape=[
            jax.ShapeDtypeStruct((count, 2 * rank), jnp.bfloat16)
            for count in (half * examples + id_rows, cut * examples, (half - cut) * examples)
        ],
        in_specs=[hbm] * 8,
        out_specs=[vmem] * 3,
        scratch_shapes=[
            pltpu.VMEM((rows, width), jnp.bfloat16),
            pltpu.VMEM((rows, width), jnp.bfloat16),
            pltpu.VMEM((rank, width), jnp.bfloat16),
            pltpu.VMEM((rank, width), jnp.bfloat16),
            pltpu.VMEM((rank, rank), jnp.float32),
            pltpu.VMEM((rank, rank), jnp.float32),
            pltpu.VMEM((rank, rank), jnp.float32),
            pltpu.VMEM((1, examples), jnp.int32),
            pltpu.VMEM((batch * tokens, rank), jnp.bfloat16),
            pltpu.VMEM((rank, batch * tokens), jnp.bfloat16),
            pltpu.VMEM((2, rank, batch * tokens), jnp.float32),
            pltpu.VMEM((half, examples, 2 * rank), jnp.float32),
            pltpu.SemaphoreType.DMA((steps,)),
            pltpu.SemaphoreType.DMA((steps,)),
            pltpu.SemaphoreType.DMA((2,)),
            pltpu.SemaphoreType.DMA((4,)),
        ],
        compiler_params=pltpu.CompilerParams(vmem_limit_bytes=60 * 2**20),
        cost_estimate=pl.CostEstimate(
            flops=4 * rows * width * rank, bytes_accessed=4 * rows * width, transcendentals=0),
        name="features",
    )(
        activations.reshape(rows, width), out_grads.reshape(rows, width),
        proj_in.T, proj_out.T, basis_in, basis_out, eigen, doc_ids.reshape(1, examples),
    )


class Grid:
    def __init__(self, groups, members):
        self.groups, self.members, self.pairs = groups, members, members // cores
        self.row_groups = 1 << ((groups.bit_length() - 1) // 2)
        self.column_groups = groups // self.row_groups
        self.column_pairs = 1 << ((self.pairs.bit_length() - 1) // 2)
        self.row_pairs = self.pairs // self.column_pairs
        self.rows = self.row_groups * self.row_pairs
        self.columns = self.column_groups * self.column_pairs

    def row_step(self, slot):
        return slot % self.row_groups, slot // self.row_groups * self.column_pairs

    def column_step(self, slot):
        return slot % self.column_groups * self.row_groups, slot // self.column_groups

    def swap(self, value, group_step, pair_step):
        if not group_step and not pair_step:
            return value
        return lax.ppermute(value, ("grp", "mem"), [
            (group * self.members + member,
             (group ^ group_step) * self.members + (member ^ (pair_step * cores)))
            for group in range(self.groups) for member in range(self.members)
        ])

    def other_core(self, value):
        return lax.ppermute(value, "mem", [(member, member ^ 1) for member in range(self.members)])


def product_kernel(grid, row_parts, *refs):
    refs = list(refs)
    rows = [[refs.pop(0) for _ in range(count)] for count in row_parts]
    columns = [refs.pop(0) for _ in range(grid.columns)]
    others = [refs.pop(0) for _ in range(grid.columns)]
    stack = refs.pop()
    outs = refs
    total, lanes = columns[0].shape
    examples, width = outs[0].shape[0] - id_rows, outs[0].shape[1]
    depth = (total - id_rows) // examples
    grp = lax.axis_index("grp")
    mem = lax.axis_index("mem")
    pair, core = mem // cores, mem % cores

    block = lax.broadcasted_iota(jnp.int32, (id_rows, width), 1) // examples
    digits = jnp.zeros((id_rows, width), jnp.float32)
    for slot in range(grid.columns):
        group_step, pair_step = grid.column_step(slot)
        where = ((grp ^ group_step) // grid.row_groups * grid.column_pairs
                 + (pair ^ pair_step) % grid.column_pairs)
        for ref, side in ((columns[slot], core), (others[slot], core ^ 1)):
            place = where * cores + side
            start = pl.multiple_of(place * examples, examples)
            for part in range(depth):
                stack[pl.ds(start, examples), pl.ds(part * lanes, lanes)] = (
                    ref[pl.ds(part * examples, examples)])
            some = ref[pl.ds(depth * examples, id_rows)].astype(jnp.float32)
            some = jnp.concatenate([some] * (width // lanes), axis=1)
            digits = jnp.where(block == place, some, digits)

    def row_tile(parts, part):
        for ref in parts:
            count = min(ref.shape[0] // examples, depth)
            if part < count:
                return ref[pl.ds(part * examples, examples)]
            part -= count

    chunk = 2
    result = None
    for start in range(0, depth, chunk):
        tile = jnp.concatenate([
            jnp.concatenate([row_tile(parts, start + part) for part in range(chunk)], axis=1)
            for parts in rows
        ], axis=0)
        value = dot_nt(tile, stack[:, pl.ds(start * lanes, chunk * lanes)])
        result = value if result is None else result + value
    for slot in range(grid.rows):
        outs[slot][pl.ds(0, examples)] = result[slot * examples:(slot + 1) * examples]
        outs[slot][pl.ds(examples, id_rows)] = digits


def products(grid, rows, columns, others, examples):
    total, lanes = columns[0].shape
    depth = (total - id_rows) // examples
    width = grid.columns * cores * examples
    vmem = pl.BlockSpec(memory_space=pltpu.VMEM)
    flat = [part for parts in rows for part in parts]
    return pl.pallas_call(
        functools.partial(product_kernel, grid, [len(parts) for parts in rows]),
        out_shape=[jax.ShapeDtypeStruct((examples + id_rows, width), jnp.float32)] * grid.rows,
        in_specs=[vmem] * (len(flat) + 2 * grid.columns),
        out_specs=[vmem] * grid.rows,
        scratch_shapes=[pltpu.VMEM((width, depth * lanes), jnp.bfloat16)],
        compiler_params=pltpu.CompilerParams(vmem_limit_bytes=40 * 2**20),
        cost_estimate=pl.CostEstimate(
            flops=2 * grid.rows * examples * width * depth * lanes,
            bytes_accessed=4 * width * depth * lanes, transcendentals=0),
        name="products",
    )(*flat, *columns, *others)


def finish_kernel(grid, factor, own_ids_ref, *refs):
    parts, out_ref = refs[:grid.rows], refs[grid.rows]
    examples, width = out_ref.shape[0], parts[0].shape[1]
    span = width // grid.column_groups
    grp = lax.axis_index("grp")
    pair = lax.axis_index("mem") // cores
    own_ids = own_ids_ref[...]
    own_low = (own_ids & 0xFFFF).astype(jnp.float32)
    own_high = ((own_ids >> 16) & 0xFFFF).astype(jnp.float32)
    for slot in range(grid.rows):
        group_step, pair_step = grid.row_step(slot)
        digits = parts[slot][pl.ds(examples, id_rows)]
        low, high = (digits[row:row + 1] + digits[row + 1:row + 2] * 256.0 for row in (0, 2))
        value = parts[slot][pl.ds(0, examples)] * factor
        value = jnp.where((own_low == low) & (own_high == high), 0.0, value)
        group = (grp ^ group_step) % grid.row_groups
        line = (pair ^ pair_step) // grid.column_pairs
        for index in range(grid.column_groups):
            start = ((index * grid.row_groups + group) * grid.row_pairs + line) * span
            out_ref[:, pl.ds(pl.multiple_of(start, span), span)] = (
                value[:, index * span:(index + 1) * span])


def finish(grid, own_ids, parts, factor):
    examples, width = own_ids.shape[0], parts[0].shape[1]
    vmem = pl.BlockSpec(memory_space=pltpu.VMEM)
    return pl.pallas_call(
        functools.partial(finish_kernel, grid, factor),
        out_shape=jax.ShapeDtypeStruct((examples, grid.rows * width), jnp.float32),
        in_specs=[vmem] * (1 + grid.rows),
        out_specs=vmem,
        compiler_params=pltpu.CompilerParams(vmem_limit_bytes=40 * 2**20),
        cost_estimate=pl.CostEstimate(
            flops=8 * grid.rows * examples * width, bytes_accessed=16 * grid.rows * examples * width,
            transcendentals=0),
        name="finish",
    )(own_ids, *parts)


def on_device(members, groups, activations, out_grads, proj_in, proj_out, basis_in, basis_out, eigen, doc_ids):
    examples, tokens, width = activations.shape
    rank = proj_in.shape[1]
    factor = 1.0 / (tokens * rank)
    grid = Grid(groups, members)
    full, first, second = features(
        activations, out_grads, proj_in, proj_out, basis_in, basis_out, eigen, doc_ids)
    def after(value, *earlier):
        return lax.optimization_barrier((value, *earlier))[0]

    rows = [[grid.swap(full, *grid.row_step(group))] for group in range(grid.row_groups)]
    near_rows = [parts[0] for parts in rows[1:]]
    for pair in range(1, grid.row_pairs):
        step = grid.row_step(pair * grid.row_groups)
        line = [grid.swap(part, *step) for part in (first, second)]
        rows.append(line)
        for group in range(1, grid.row_groups):
            head = grid.swap(after(line[0], *near_rows), group, 0)
            rows.append([head, grid.swap(after(line[1], head), group, 0)])
    far_row = rows[grid.row_groups][0]
    columns = []
    for pair in range(grid.column_pairs):
        slab = grid.swap(full, *grid.column_step(pair * grid.column_groups))
        for group in range(grid.column_groups):
            columns.append(grid.swap(
                after(slab, far_row, *near_rows) if pair and group else slab, *grid.column_step(group)))
    tails = [parts[-1] for parts in rows[grid.row_groups + 1:]]
    others = [grid.other_core(column) for column in columns[:-1]]
    others.append(grid.other_core(after(columns[-1], *tails)))
    blocks = products(grid, rows, columns, others, examples)
    parts = [grid.swap(value, *grid.row_step(slot)) for slot, value in enumerate(blocks)]
    return finish(grid, doc_ids[:, None], parts, factor)


def solution(mesh):
    return jax.shard_map(
        functools.partial(on_device, mesh.shape["mem"], mesh.shape["grp"]),
        mesh=mesh,
        in_specs=(
            P(("grp", "mem"), None, None),
            P(("grp", "mem"), None, None),
            P(),
            P(),
            P(),
            P(),
            P(),
            P(("grp", "mem")),
        ),
        out_specs=P(("grp", "mem"), None),
        check_vma=False,
    )
```

```python
import functools
import jax
import jax.numpy as jnp
from jax import lax
from jax.experimental import pallas as pl
from jax.experimental.pallas import tpu as pltpu
from jax.sharding import PartitionSpec as P

damping = 0.1
batch = 8
id_rows = 16
cores = 2


def dot_nn(a, b):
    return lax.dot_general(a, b, (((1,), (0,)), ((), ())), preferred_element_type=jnp.float32)


def dot_nt(a, b):
    return lax.dot_general(a, b, (((1,), (1,)), ((), ())), preferred_element_type=jnp.float32)


def split_two(value):
    high = value.astype(jnp.bfloat16)
    low = (value - high.astype(jnp.float32)).astype(jnp.bfloat16)
    return high, low


def feature_kernel(
    tokens, slices, act_hbm, grad_hbm, pin_hbm, pout_hbm, bin_hbm, bout_hbm, eigen_hbm, ids_hbm, *refs
):
    out_refs = refs[:slices]
    (act, grad, pin, pout, bin_ref, bout_ref, eigen_ref, ids_ref, act_proj, grad_proj, gt_ref, feat,
     act_sem, grad_sem, w_sem, s_sem) = refs[slices:]
    rows, width = act.shape
    rank = bin_ref.shape[0]
    half = rank // 2
    step_rows = batch * tokens
    steps = rows // step_rows
    examples = feat.shape[1]

    def step_copies(step):
        rng = pl.ds(pl.multiple_of(step * step_rows, step_rows), step_rows)
        return (
            pltpu.make_async_copy(act_hbm.at[rng], act.at[rng], act_sem.at[step]),
            pltpu.make_async_copy(grad_hbm.at[rng], grad.at[rng], grad_sem.at[step]),
        )

    weights = [
        pltpu.make_async_copy(pin_hbm, pin, w_sem.at[0]),
        pltpu.make_async_copy(pout_hbm, pout, w_sem.at[1]),
    ]
    def start_step(step):
        for priority, copy in enumerate(step_copies(step)):
            copy.start(priority=priority)

    small = [
        pltpu.make_async_copy(source, target, s_sem.at[index])
        for index, (source, target) in enumerate((
            (bin_hbm, bin_ref), (bout_hbm, bout_ref), (eigen_hbm, eigen_ref), (ids_hbm, ids_ref)))
    ]
    for copy in weights:
        copy.start()
    start_step(0)
    for copy in small:
        copy.start()
    for step in range(1, steps):
        start_step(step)
    for copy in small:
        copy.wait()

    bin_hi, bin_lo = split_two(jnp.concatenate([bin_ref[...], bin_ref[...]], axis=1))
    bout_hi, bout_lo = split_two(bout_ref[...].T)
    inverse = 1.0 / jnp.sqrt(eigen_ref[...] + damping)
    inverse = jnp.concatenate([inverse[:half], inverse[half:]], axis=1)
    own_token = (
        lax.broadcasted_iota(jnp.int32, (batch, step_rows), 1) // tokens
        == lax.broadcasted_iota(jnp.int32, (batch, step_rows), 0)
    )
    first_lanes = lax.broadcasted_iota(jnp.int32, (batch, 2 * rank), 1) < rank
    ids = jnp.concatenate([ids_ref[...]] * (2 * rank // examples), axis=1)
    place = lax.broadcasted_iota(jnp.int32, (id_rows, 2 * rank), 0) % 4
    digits = (jnp.broadcast_to(ids, (id_rows, 2 * rank)) >> (place * 8)) & 255
    digits = digits.astype(jnp.float32).astype(jnp.bfloat16)
    for copy in weights:
        copy.wait()

    def project(step):
        for copy in step_copies(step):
            copy.wait()
        rng = pl.ds(pl.multiple_of(step * step_rows, step_rows), step_rows)
        first, second = pl.ds(0, width // 2), pl.ds(width // 2, width // 2)
        return (
            (dot_nt(act[rng, first], pin[:, first]) + dot_nt(act[rng, second], pin[:, second])
             ).astype(jnp.bfloat16),
            (dot_nt(pout[:, first], grad[rng, first]) + dot_nt(pout[:, second], grad[rng, second])
             ).astype(jnp.bfloat16),
        )

    def rotate(step, act_part, grad_part):
        act_hi, act_lo = split_two(dot_nn(act_part, bin_hi) + dot_nn(act_part, bin_lo))
        grad_hi, grad_lo = split_two(dot_nn(bout_hi, grad_part) + dot_nn(bout_lo, grad_part))
        gt_ref[0] = grad_hi.astype(jnp.float32)
        gt_ref[1] = grad_lo.astype(jnp.float32)
        spread_hi, spread_lo = [
            jnp.concatenate([
                jnp.where(own_token, jnp.broadcast_to(gt_ref[part, pl.ds(u, 1)], (batch, step_rows)), 0.0)
                for u in range(rank)
            ], axis=0).astype(jnp.bfloat16)
            for part in range(2)
        ]
        wide = dot_nn(spread_hi, jnp.concatenate([act_hi, act_lo], axis=1))
        rotated = wide[:, :2 * rank] + wide[:, 2 * rank:] + dot_nn(spread_lo, act_hi)
        start = pl.multiple_of(step * batch, batch)
        for u in range(half):
            value = jnp.where(
                first_lanes,
                rotated[u * batch:(u + 1) * batch],
                rotated[(u + half) * batch:(u + half + 1) * batch],
            ) * inverse[u:u + 1]
            feat[u, pl.ds(start, batch)] = value

    act_proj[...], grad_proj[...] = project(0)

    def body(step, carry):
        act_part, grad_part = act_proj[...], grad_proj[...]
        act_next, grad_next = project(step)
        rotate(step - 1, act_part, grad_part)
        act_proj[...] = act_next
        grad_proj[...] = grad_next
        return carry

    lax.fori_loop(1, steps, body, 0)
    rotate(steps - 1, act_proj[...], grad_proj[...])
    depth = half // slices
    me = lax.axis_index("mem") // cores
    for index in range(slices):
        start = (me ^ index) * depth
        piece = feat[pl.ds(start, depth)].astype(jnp.bfloat16)
        out_refs[index][pl.ds(0, depth * examples)] = piece.reshape(depth * examples, 2 * rank)
        out_refs[index][pl.ds(depth * examples, id_rows)] = digits


def features(slices, activations, out_grads, proj_in, proj_out, basis_in, basis_out, eigen, doc_ids):
    examples, tokens, width = activations.shape
    rank = proj_in.shape[1]
    rows = examples * tokens
    steps = examples // batch
    half = rank // 2
    hbm = pl.BlockSpec(memory_space=pl.ANY)
    vmem = pl.BlockSpec(memory_space=pltpu.VMEM)
    return pl.pallas_call(
        functools.partial(feature_kernel, tokens, slices),
        out_shape=[
            jax.ShapeDtypeStruct((half // slices * examples + id_rows, 2 * rank), jnp.bfloat16)
        ] * slices,
        in_specs=[hbm] * 8,
        out_specs=[vmem] * slices,
        scratch_shapes=[
            pltpu.VMEM((rows, width), jnp.bfloat16),
            pltpu.VMEM((rows, width), jnp.bfloat16),
            pltpu.VMEM((rank, width), jnp.bfloat16),
            pltpu.VMEM((rank, width), jnp.bfloat16),
            pltpu.VMEM((rank, rank), jnp.float32),
            pltpu.VMEM((rank, rank), jnp.float32),
            pltpu.VMEM((rank, rank), jnp.float32),
            pltpu.VMEM((1, examples), jnp.int32),
            pltpu.VMEM((batch * tokens, rank), jnp.bfloat16),
            pltpu.VMEM((rank, batch * tokens), jnp.bfloat16),
            pltpu.VMEM((2, rank, batch * tokens), jnp.float32),
            pltpu.VMEM((half, examples, 2 * rank), jnp.float32),
            pltpu.SemaphoreType.DMA((steps,)),
            pltpu.SemaphoreType.DMA((steps,)),
            pltpu.SemaphoreType.DMA((2,)),
            pltpu.SemaphoreType.DMA((4,)),
        ],
        compiler_params=pltpu.CompilerParams(vmem_limit_bytes=60 * 2**20),
        cost_estimate=pl.CostEstimate(
            flops=4 * rows * width * rank, bytes_accessed=4 * rows * width, transcendentals=0),
        name="features",
    )(
        activations.reshape(rows, width), out_grads.reshape(rows, width),
        proj_in.T, proj_out.T, basis_in, basis_out, eigen, doc_ids.reshape(1, examples),
    )


def slice_order(slices):
    return [0] + list(range(slices - 1, 0, -1))


def product_kernel(slices, pieces, examples, row_groups, column_groups, *refs):
    runs = slices // pieces
    slabs = row_groups - 1 + 2 * column_groups
    ins, outs = refs[:runs * slabs], refs[runs * slabs:runs * slabs + slices]
    ids_ref, column_stack, row_stack, result = refs[runs * slabs + slices:]
    piece_rows, lanes = ins[0].shape
    piece_rows = piece_rows // pieces
    depth = (piece_rows - id_rows) // examples
    cols = column_stack.shape[0]
    mem = lax.axis_index("mem")
    pair, core = mem // cores, mem % cores

    def place(stack, row, ref, piece):
        start = pl.multiple_of(row * examples, examples)
        for part in range(depth):
            stack[pl.ds(start, examples), pl.ds(part * lanes, lanes)] = (
                ref[pl.ds(piece * piece_rows + part * examples, examples)])

    block = lax.broadcasted_iota(jnp.int32, (id_rows, cols), 1) // examples
    digits = jnp.zeros((id_rows, cols), jnp.float32)
    for run in range(runs):
        part = ins[run * slabs:(run + 1) * slabs]
        columns, others = part[:column_groups], part[column_groups:2 * column_groups]
        rows = (columns[0],) + tuple(part[2 * column_groups:])
        for piece in range(pieces):
            place_of = pair ^ slice_order(slices)[run * pieces + piece]
            for group in range(column_groups):
                for ref, side in ((columns[group], core), (others[group], core ^ 1)):
                    column = (group * slices + place_of) * cores + side
                    place(column_stack, column, ref, piece)
                    some = ref[pl.ds((piece + 1) * piece_rows - id_rows, id_rows)].astype(jnp.float32)
                    some = jnp.concatenate([some] * (cols // lanes), axis=1)
                    digits = jnp.where(block == column, some, digits)
            for group in range(row_groups):
                place(row_stack, place_of * row_groups + group, rows[group], piece)
    result[...] = dot_nt(row_stack[...], column_stack[...]).astype(jnp.bfloat16)
    count = row_groups * examples
    for index in range(slices):
        start = pl.multiple_of((pair ^ index) * count, count)
        outs[index][...] = result[pl.ds(start, count)]
    ids_ref[...] = digits.astype(jnp.bfloat16)


def products(slabs, slices, pieces, examples, row_groups, column_groups):
    piece_rows, lanes = slabs[0].shape
    depth = (piece_rows // pieces - id_rows) // examples
    vmem = pl.BlockSpec(memory_space=pltpu.VMEM)
    rows, cols = row_groups * slices * examples, column_groups * slices * cores * examples
    return pl.pallas_call(
        functools.partial(product_kernel, slices, pieces, examples, row_groups, column_groups),
        out_shape=[jax.ShapeDtypeStruct((row_groups * examples, cols), jnp.bfloat16)] * slices
        + [jax.ShapeDtypeStruct((id_rows, cols), jnp.bfloat16)],
        in_specs=[vmem] * len(slabs),
        out_specs=[vmem] * (slices + 1),
        scratch_shapes=[
            pltpu.VMEM((cols, depth * lanes), jnp.bfloat16),
            pltpu.VMEM((rows, depth * lanes), jnp.bfloat16),
            pltpu.VMEM((rows, cols), jnp.bfloat16),
        ],
        compiler_params=pltpu.CompilerParams(vmem_limit_bytes=40 * 2**20),
        cost_estimate=pl.CostEstimate(
            flops=2 * rows * cols * depth * lanes, bytes_accessed=4 * rows * cols, transcendentals=0),
        name="products",
    )(*slabs)


def total_kernel(slices, ids_ref, *refs):
    parts, outs = refs[:slices], refs[slices:]
    examples = outs[0].shape[0]
    for group, out in enumerate(outs):
        rng = pl.ds(group * examples, examples)
        total = sum(part[rng].astype(jnp.float32) for part in parts)
        out[pl.ds(0, examples)] = total.astype(out.dtype)
        if group:
            out[pl.ds(examples, id_rows)] = ids_ref[...]


def totals(parts, ids, examples):
    rows, cols = parts[0].shape
    groups = rows // examples
    vmem = pl.BlockSpec(memory_space=pltpu.VMEM)
    return pl.pallas_call(
        functools.partial(total_kernel, len(parts)),
        out_shape=[
            jax.ShapeDtypeStruct((examples + id_rows, cols), jnp.bfloat16) if group
            else jax.ShapeDtypeStruct((examples, cols), jnp.float32)
            for group in range(groups)
        ],
        in_specs=[vmem] * (1 + len(parts)),
        out_specs=[vmem] * groups,
        compiler_params=pltpu.CompilerParams(vmem_limit_bytes=40 * 2**20),
        cost_estimate=pl.CostEstimate(
            flops=rows * cols * len(parts), bytes_accessed=8 * rows * cols, transcendentals=0),
        name="totals",
    )(ids, *parts)


def finish_kernel(factor, column_groups, own_ids_ref, ids_ref, *refs):
    parts, out_ref = refs[:-1], refs[-1]
    examples, cols = parts[0].shape
    width = cols // column_groups
    grp = lax.axis_index("grp")
    own_ids = own_ids_ref[...]
    own_low = (own_ids & 0xFFFF).astype(jnp.float32)
    own_high = ((own_ids >> 16) & 0xFFFF).astype(jnp.float32)
    for row_step, part in enumerate(parts):
        digits = part[pl.ds(examples, id_rows)] if row_step else ids_ref[...]
        digits = digits.astype(jnp.float32)
        low, high = (digits[row:row + 1] + digits[row + 1:row + 2] * 256.0 for row in (0, 2))
        value = part[pl.ds(0, examples)].astype(jnp.float32) * factor
        value = jnp.where((own_low == low) & (own_high == high), 0.0, value)
        for column_step in range(column_groups):
            start = (grp ^ row_step ^ (column_step * len(parts))) * width
            out_ref[:, pl.ds(pl.multiple_of(start, width), width)] = (
                value[:, column_step * width:(column_step + 1) * width])


def finish(own_ids, ids, parts, column_groups, factor):
    examples, cols = parts[0].shape
    vmem = pl.BlockSpec(memory_space=pltpu.VMEM)
    return pl.pallas_call(
        functools.partial(finish_kernel, factor, column_groups),
        out_shape=jax.ShapeDtypeStruct((examples, len(parts) * cols), jnp.float32),
        in_specs=[vmem] * (2 + len(parts)),
        out_specs=vmem,
        compiler_params=pltpu.CompilerParams(vmem_limit_bytes=40 * 2**20),
        cost_estimate=pl.CostEstimate(
            flops=8 * examples * cols, bytes_accessed=16 * examples * cols, transcendentals=0),
        name="finish",
    )(own_ids, ids, *parts)


def swap(value, axis, size, distance):
    if distance == 0:
        return value
    return lax.ppermute(value, axis, [(place, place ^ distance) for place in range(size)])


def on_device(members, groups, activations, out_grads, proj_in, proj_out, basis_in, basis_out, eigen, doc_ids):
    examples, tokens, width = activations.shape
    rank = proj_in.shape[1]
    factor = 1.0 / (tokens * rank)
    slices = members // cores
    runs = 2
    pieces = slices // runs
    row_groups = 1 << ((groups.bit_length() - 1) // 2)
    column_groups = groups // row_groups
    feat = features(slices, activations, out_grads, proj_in, proj_out, basis_in, basis_out, eigen, doc_ids)
    got = [swap(feat[index], "mem", members, cores * index) for index in slice_order(slices)]
    slabs = []
    for run in range(runs):
        slab = jnp.concatenate(got[run * pieces:(run + 1) * pieces], axis=0)
        if run:
            slab, slabs[column_groups] = lax.optimization_barrier((slab, slabs[column_groups]))
        columns = [swap(slab, "grp", groups, row_groups * step) for step in range(column_groups)]
        rows = [swap(slab, "grp", groups, step) for step in range(1, row_groups)]
        held = lax.optimization_barrier((*columns[1:], *rows))[:column_groups - 1]
        others = [swap(column, "mem", members, 1) for column in (slab, *held)]
        slabs += columns + others + rows
    *partial, ids = products(slabs, slices, pieces, examples, row_groups, column_groups)
    parts = [swap(partial[index], "mem", members, cores * index) for index in slice_order(slices)]
    sums = totals(parts, ids, examples)
    sums = [swap(value, "grp", groups, step) for step, value in enumerate(sums)]
    return finish(doc_ids[:, None], ids, sums, column_groups, factor)


def solution(mesh):
    return jax.shard_map(
        functools.partial(on_device, mesh.shape["mem"], mesh.shape["grp"]),
        mesh=mesh,
        in_specs=(
            P(("grp", "mem"), None, None),
            P(("grp", "mem"), None, None),
            P(),
            P(),
            P(),
            P(),
            P(),
            P(("grp", "mem")),
        ),
        out_specs=P(("grp", "mem"), None),
        check_vma=False,
    )
```

```python
import functools
import jax
import jax.numpy as jnp
from jax import lax
from jax.experimental import pallas as pl
from jax.experimental.pallas import tpu as pltpu
from jax.sharding import PartitionSpec as P

damping = 0.1
batch = 8
id_rows = 16
cores = 2


def dot_nn(a, b):
    return lax.dot_general(a, b, (((1,), (0,)), ((), ())), preferred_element_type=jnp.float32)


def dot_nt(a, b):
    return lax.dot_general(a, b, (((1,), (1,)), ((), ())), preferred_element_type=jnp.float32)


def split_two(value):
    high = value.astype(jnp.bfloat16)
    low = (value - high.astype(jnp.float32)).astype(jnp.bfloat16)
    return high, low


def feature_kernel(
    tokens, slices, act_hbm, grad_hbm, pin_hbm, pout_hbm, bin_hbm, bout_hbm, eigen_hbm, ids_hbm, *refs
):
    out_refs = refs[:slices]
    (act, grad, pin, pout, bin_ref, bout_ref, eigen_ref, ids_ref, act_proj, grad_proj, gt_ref, feat,
     act_sem, grad_sem, w_sem, s_sem) = refs[slices:]
    rows, width = act.shape
    rank = bin_ref.shape[0]
    half = rank // 2
    step_rows = batch * tokens
    steps = rows // step_rows
    examples = feat.shape[1]

    def step_copies(step):
        rng = pl.ds(pl.multiple_of(step * step_rows, step_rows), step_rows)
        return (
            pltpu.make_async_copy(act_hbm.at[rng], act.at[rng], act_sem.at[step]),
            pltpu.make_async_copy(grad_hbm.at[rng], grad.at[rng], grad_sem.at[step]),
        )

    weights = [
        pltpu.make_async_copy(pin_hbm, pin, w_sem.at[0]),
        pltpu.make_async_copy(pout_hbm, pout, w_sem.at[1]),
    ]
    def start_step(step):
        for priority, copy in enumerate(step_copies(step)):
            copy.start(priority=priority)

    small = [
        pltpu.make_async_copy(source, target, s_sem.at[index])
        for index, (source, target) in enumerate((
            (bin_hbm, bin_ref), (bout_hbm, bout_ref), (eigen_hbm, eigen_ref), (ids_hbm, ids_ref)))
    ]
    for copy in weights:
        copy.start()
    start_step(0)
    for copy in small:
        copy.start()
    for step in range(1, steps):
        start_step(step)
    for copy in small:
        copy.wait()

    bin_hi, bin_lo = split_two(jnp.concatenate([bin_ref[...], bin_ref[...]], axis=1))
    bout_hi, bout_lo = split_two(bout_ref[...].T)
    inverse = 1.0 / jnp.sqrt(eigen_ref[...] + damping)
    inverse = jnp.concatenate([inverse[:half], inverse[half:]], axis=1)
    own_token = (
        lax.broadcasted_iota(jnp.int32, (batch, step_rows), 1) // tokens
        == lax.broadcasted_iota(jnp.int32, (batch, step_rows), 0)
    )
    first_lanes = lax.broadcasted_iota(jnp.int32, (batch, 2 * rank), 1) < rank
    ids = jnp.concatenate([ids_ref[...]] * (2 * rank // examples), axis=1)
    place = lax.broadcasted_iota(jnp.int32, (id_rows, 2 * rank), 0) % 4
    digits = (jnp.broadcast_to(ids, (id_rows, 2 * rank)) >> (place * 8)) & 255
    digits = digits.astype(jnp.float32).astype(jnp.bfloat16)
    for copy in weights:
        copy.wait()

    def project(step):
        for copy in step_copies(step):
            copy.wait()
        rng = pl.ds(pl.multiple_of(step * step_rows, step_rows), step_rows)
        first, second = pl.ds(0, width // 2), pl.ds(width // 2, width // 2)
        return (
            (dot_nt(act[rng, first], pin[:, first]) + dot_nt(act[rng, second], pin[:, second])
             ).astype(jnp.bfloat16),
            (dot_nt(pout[:, first], grad[rng, first]) + dot_nt(pout[:, second], grad[rng, second])
             ).astype(jnp.bfloat16),
        )

    def rotate(step, act_part, grad_part):
        act_hi, act_lo = split_two(dot_nn(act_part, bin_hi) + dot_nn(act_part, bin_lo))
        grad_hi, grad_lo = split_two(dot_nn(bout_hi, grad_part) + dot_nn(bout_lo, grad_part))
        gt_ref[0] = grad_hi.astype(jnp.float32)
        gt_ref[1] = grad_lo.astype(jnp.float32)
        spread_hi, spread_lo = [
            jnp.concatenate([
                jnp.where(own_token, jnp.broadcast_to(gt_ref[part, pl.ds(u, 1)], (batch, step_rows)), 0.0)
                for u in range(rank)
            ], axis=0).astype(jnp.bfloat16)
            for part in range(2)
        ]
        wide = dot_nn(spread_hi, jnp.concatenate([act_hi, act_lo], axis=1))
        rotated = wide[:, :2 * rank] + wide[:, 2 * rank:] + dot_nn(spread_lo, act_hi)
        start = pl.multiple_of(step * batch, batch)
        for u in range(half):
            value = jnp.where(
                first_lanes,
                rotated[u * batch:(u + 1) * batch],
                rotated[(u + half) * batch:(u + half + 1) * batch],
            ) * inverse[u:u + 1]
            feat[u, pl.ds(start, batch)] = value

    act_proj[...], grad_proj[...] = project(0)

    def body(step, carry):
        act_part, grad_part = act_proj[...], grad_proj[...]
        act_next, grad_next = project(step)
        rotate(step - 1, act_part, grad_part)
        act_proj[...] = act_next
        grad_proj[...] = grad_next
        return carry

    lax.fori_loop(1, steps, body, 0)
    rotate(steps - 1, act_proj[...], grad_proj[...])
    depth = half // slices
    me = lax.axis_index("mem") // cores
    for index in range(slices):
        start = (me ^ index) * depth
        piece = feat[pl.ds(start, depth)].astype(jnp.bfloat16)
        out_refs[index][pl.ds(0, depth * examples)] = piece.reshape(depth * examples, 2 * rank)
        out_refs[index][pl.ds(depth * examples, id_rows)] = digits


def features(slices, activations, out_grads, proj_in, proj_out, basis_in, basis_out, eigen, doc_ids):
    examples, tokens, width = activations.shape
    rank = proj_in.shape[1]
    rows = examples * tokens
    steps = examples // batch
    half = rank // 2
    hbm = pl.BlockSpec(memory_space=pl.ANY)
    vmem = pl.BlockSpec(memory_space=pltpu.VMEM)
    return pl.pallas_call(
        functools.partial(feature_kernel, tokens, slices),
        out_shape=[
            jax.ShapeDtypeStruct((half // slices * examples + id_rows, 2 * rank), jnp.bfloat16)
        ] * slices,
        in_specs=[hbm] * 8,
        out_specs=[vmem] * slices,
        scratch_shapes=[
            pltpu.VMEM((rows, width), jnp.bfloat16),
            pltpu.VMEM((rows, width), jnp.bfloat16),
            pltpu.VMEM((rank, width), jnp.bfloat16),
            pltpu.VMEM((rank, width), jnp.bfloat16),
            pltpu.VMEM((rank, rank), jnp.float32),
            pltpu.VMEM((rank, rank), jnp.float32),
            pltpu.VMEM((rank, rank), jnp.float32),
            pltpu.VMEM((1, examples), jnp.int32),
            pltpu.VMEM((batch * tokens, rank), jnp.bfloat16),
            pltpu.VMEM((rank, batch * tokens), jnp.bfloat16),
            pltpu.VMEM((2, rank, batch * tokens), jnp.float32),
            pltpu.VMEM((half, examples, 2 * rank), jnp.float32),
            pltpu.SemaphoreType.DMA((steps,)),
            pltpu.SemaphoreType.DMA((steps,)),
            pltpu.SemaphoreType.DMA((2,)),
            pltpu.SemaphoreType.DMA((4,)),
        ],
        compiler_params=pltpu.CompilerParams(vmem_limit_bytes=60 * 2**20),
        cost_estimate=pl.CostEstimate(
            flops=4 * rows * width * rank, bytes_accessed=4 * rows * width, transcendentals=0),
        name="features",
    )(
        activations.reshape(rows, width), out_grads.reshape(rows, width),
        proj_in.T, proj_out.T, basis_in, basis_out, eigen, doc_ids.reshape(1, examples),
    )


def slice_order(slices):
    return [0] + list(range(slices - 1, 0, -1))


def product_kernel(slices, pieces, examples, row_groups, column_groups, *refs):
    runs = slices // pieces
    slabs = row_groups - 1 + 2 * column_groups
    ins, (out_ref, column_stack, row_stack) = refs[:runs * slabs], refs[runs * slabs:]
    piece_rows, lanes = ins[0].shape
    piece_rows = piece_rows // pieces
    depth = (piece_rows - id_rows) // examples
    grp = lax.axis_index("grp")
    mem = lax.axis_index("mem")
    pair, core = mem // cores, mem % cores

    def place(stack, digits, row, ref, piece):
        start = pl.multiple_of(row * examples, examples)
        for part in range(depth):
            stack[pl.ds(start, examples), pl.ds(part * lanes, lanes)] = (
                ref[pl.ds(piece * piece_rows + part * examples, examples)])
        some = ref[pl.ds((piece + 1) * piece_rows - id_rows, id_rows)].astype(jnp.float32)
        some = jnp.concatenate([some] * (digits.shape[1] // lanes), axis=1)
        block = lax.broadcasted_iota(jnp.int32, digits.shape, 1) // examples
        return jnp.where(block == row, some, digits)

    column_digits = jnp.zeros((id_rows, column_stack.shape[0]), jnp.float32)
    row_digits = jnp.zeros((id_rows, row_stack.shape[0]), jnp.float32)
    for run in range(runs):
        part = ins[run * slabs:(run + 1) * slabs]
        columns, others = part[:column_groups], part[column_groups:2 * column_groups]
        rows = (columns[0],) + tuple(part[2 * column_groups:])
        for piece in range(pieces):
            place_of = pair ^ slice_order(slices)[run * pieces + piece]
            for group in range(column_groups):
                for ref, side in ((columns[group], core), (others[group], core ^ 1)):
                    column = (group * slices + place_of) * cores + side
                    column_digits = place(column_stack, column_digits, column, ref, piece)
            for group in range(row_groups):
                row = (grp % row_groups ^ group) * slices + place_of
                row_digits = place(row_stack, row_digits, row, rows[group], piece)

    def halves(digits):
        return (digits[0:1] + digits[1:2] * 256.0, digits[2:3] + digits[3:4] * 256.0)

    column_low, column_high = halves(column_digits)
    row_low, row_high = halves(row_digits)
    result = dot_nt(row_stack[...], column_stack[...])
    count = 128 // examples
    for start in range(0, row_stack.shape[0], 128):
        low, high = (
            jnp.broadcast_to(row[:, start:start + 128], (128, 128)).T[:, 0:1] for row in (row_low, row_high))
        value = result[start:start + 128]
        value = jnp.where((low == column_low) & (high == column_high), 0.0, value)
        out_ref[pl.ds(start // examples, count)] = (
            value.astype(jnp.bfloat16).reshape(count, examples, value.shape[1]))


def products(slabs, slices, pieces, examples, row_groups, column_groups):
    piece_rows, lanes = slabs[0].shape
    depth = (piece_rows // pieces - id_rows) // examples
    vmem = pl.BlockSpec(memory_space=pltpu.VMEM)
    rows, cols = row_groups * slices * examples, column_groups * slices * cores * examples
    return pl.pallas_call(
        functools.partial(product_kernel, slices, pieces, examples, row_groups, column_groups),
        out_shape=jax.ShapeDtypeStruct((row_groups * slices, examples, cols), jnp.bfloat16),
        in_specs=[vmem] * len(slabs),
        out_specs=vmem,
        scratch_shapes=[
            pltpu.VMEM((cols, depth * lanes), jnp.bfloat16),
            pltpu.VMEM((rows, depth * lanes), jnp.bfloat16),
        ],
        compiler_params=pltpu.CompilerParams(vmem_limit_bytes=40 * 2**20),
        cost_estimate=pl.CostEstimate(
            flops=2 * rows * cols * depth * lanes, bytes_accessed=4 * rows * cols, transcendentals=0),
        name="products",
    )(*slabs)


def finish_kernel(factor, row_groups, column_groups, parts_ref, out_ref):
    count, examples, cols = parts_ref.shape
    slices = count // row_groups
    width = cols // column_groups
    grp = lax.axis_index("grp")
    for side in range(row_groups):
        value = sum(
            parts_ref[side * slices + index].astype(jnp.float32) for index in range(slices)) * factor
        for step in range(column_groups):
            start = ((grp // row_groups ^ step) * row_groups + side) * width
            out_ref[:, pl.ds(pl.multiple_of(start, width), width)] = (
                value[:, step * width:(step + 1) * width])


def finish(parts, row_groups, column_groups, factor):
    count, examples, cols = parts.shape
    vmem = pl.BlockSpec(memory_space=pltpu.VMEM)
    return pl.pallas_call(
        functools.partial(finish_kernel, factor, row_groups, column_groups),
        out_shape=jax.ShapeDtypeStruct((examples, row_groups * cols), jnp.float32),
        in_specs=[vmem],
        out_specs=vmem,
        compiler_params=pltpu.CompilerParams(vmem_limit_bytes=40 * 2**20),
        cost_estimate=pl.CostEstimate(
            flops=count * examples * cols, bytes_accessed=2 * count * examples * cols, transcendentals=0),
        name="finish",
    )(parts)


def swap(value, axis, size, distance):
    if distance == 0:
        return value
    return lax.ppermute(value, axis, [(place, place ^ distance) for place in range(size)])


def on_device(members, groups, activations, out_grads, proj_in, proj_out, basis_in, basis_out, eigen, doc_ids):
    examples, tokens, width = activations.shape
    rank = proj_in.shape[1]
    factor = 1.0 / (tokens * rank)
    slices = members // cores
    runs = 2
    pieces = slices // runs
    row_groups = 1 << ((groups.bit_length() - 1) // 2)
    column_groups = groups // row_groups
    feat = features(slices, activations, out_grads, proj_in, proj_out, basis_in, basis_out, eigen, doc_ids)
    got = [swap(feat[index], "mem", members, cores * index) for index in slice_order(slices)]
    slabs = []
    for run in range(runs):
        slab = jnp.concatenate(got[run * pieces:(run + 1) * pieces], axis=0)
        if run:
            slab, slabs[column_groups] = lax.optimization_barrier((slab, slabs[column_groups]))
        columns = [swap(slab, "grp", groups, row_groups * step) for step in range(column_groups)]
        rows = [swap(slab, "grp", groups, step) for step in range(1, row_groups)]
        held = lax.optimization_barrier((*columns[1:], *rows))[:column_groups - 1]
        others = [swap(column, "mem", members, 1) for column in (slab, *held)]
        slabs += columns + others + rows
    partial = products(slabs, slices, pieces, examples, row_groups, column_groups)
    lines = [
        [(line * row_groups + side) * members + pair * cores + core
         for side in range(row_groups) for pair in range(slices)]
        for line in range(column_groups) for core in range(cores)
    ]
    parts = lax.all_to_all(partial, ("grp", "mem"), 0, 0, axis_index_groups=lines, tiled=True)
    return finish(parts, row_groups, column_groups, factor)


def solution(mesh):
    return jax.shard_map(
        functools.partial(on_device, mesh.shape["mem"], mesh.shape["grp"]),
        mesh=mesh,
        in_specs=(
            P(("grp", "mem"), None, None),
            P(("grp", "mem"), None, None),
            P(),
            P(),
            P(),
            P(),
            P(),
            P(("grp", "mem")),
        ),
        out_specs=P(("grp", "mem"), None),
        check_vma=False,
    )
```

```python
import functools
import jax
import jax.numpy as jnp
from jax import lax
from jax.experimental import pallas as pl
from jax.experimental.pallas import tpu as pltpu
from jax.sharding import PartitionSpec as P

damping = 0.1
parts = 2
batch = 8
id_rows = 16
cores = 2


def dot_nn(a, b):
    return lax.dot_general(a, b, (((1,), (0,)), ((), ())), preferred_element_type=jnp.float32)


def dot_nt(a, b):
    return lax.dot_general(a, b, (((1,), (1,)), ((), ())), preferred_element_type=jnp.float32)


def split_two(value):
    high = value.astype(jnp.bfloat16)
    low = (value - high.astype(jnp.float32)).astype(jnp.bfloat16)
    return high, low


def feature_kernel(
    tokens, slices, act_hbm, grad_hbm, pin_hbm, pout_hbm, bin_hbm, bout_hbm, eigen_hbm, ids_hbm, *refs
):
    out_refs = refs[:slices]
    (act, grad, pin, pout, bin_ref, bout_ref, eigen_ref, ids_ref, act_proj, grad_proj, gt_ref, feat,
     act_sem, grad_sem, w_sem, s_sem) = refs[slices:]
    rows = act.shape[0]
    rank = bin_ref.shape[0]
    half = rank // 2
    step_rows = batch * tokens
    steps = rows // step_rows
    examples = feat.shape[1]

    part_rows = step_rows // parts

    def part_copies(step, part):
        rng = pl.ds(pl.multiple_of(step * step_rows + part * part_rows, part_rows), part_rows)
        return (
            pltpu.make_async_copy(act_hbm.at[rng], act.at[rng], act_sem.at[step, part]),
            pltpu.make_async_copy(grad_hbm.at[rng], grad.at[rng], grad_sem.at[step, part]),
        )

    weights = [
        pltpu.make_async_copy(pin_hbm, pin, w_sem.at[0]),
        pltpu.make_async_copy(pout_hbm, pout, w_sem.at[1]),
    ]
    def start_step(step):
        for part in range(parts):
            for priority, copy in enumerate(part_copies(step, part)):
                copy.start(priority=priority)

    small = [
        pltpu.make_async_copy(source, target, s_sem.at[index])
        for index, (source, target) in enumerate((
            (bin_hbm, bin_ref), (bout_hbm, bout_ref), (eigen_hbm, eigen_ref), (ids_hbm, ids_ref)))
    ]
    for copy in weights:
        copy.start()
    start_step(0)
    for copy in small:
        copy.start()
    for step in range(1, steps):
        start_step(step)
    for copy in small:
        copy.wait()

    bin_hi, bin_lo = split_two(jnp.concatenate([bin_ref[...], bin_ref[...]], axis=1))
    bout_hi, bout_lo = split_two(bout_ref[...].T)
    inverse = 1.0 / jnp.sqrt(eigen_ref[...] + damping)
    inverse = jnp.concatenate([inverse[:half], inverse[half:]], axis=1)
    own_token = (
        lax.broadcasted_iota(jnp.int32, (batch, step_rows), 1) // tokens
        == lax.broadcasted_iota(jnp.int32, (batch, step_rows), 0)
    )
    first_lanes = lax.broadcasted_iota(jnp.int32, (batch, 2 * rank), 1) < rank
    ids = jnp.concatenate([ids_ref[...]] * (2 * rank // examples), axis=1)
    place = lax.broadcasted_iota(jnp.int32, (id_rows, 2 * rank), 0) % 4
    digits = (jnp.broadcast_to(ids, (id_rows, 2 * rank)) >> (place * 8)) & 255
    digits = digits.astype(jnp.float32).astype(jnp.bfloat16)
    for copy in weights:
        copy.wait()

    def project(step):
        acts, grads = [], []
        for part in range(parts):
            for copy in part_copies(step, part):
                copy.wait()
            rng = pl.ds(pl.multiple_of(step * step_rows + part * part_rows, part_rows), part_rows)
            acts.append(dot_nt(act[rng], pin[...]).astype(jnp.bfloat16))
            grads.append(dot_nt(pout[...], grad[rng]).astype(jnp.bfloat16))
        return jnp.concatenate(acts, axis=0), jnp.concatenate(grads, axis=1)

    def rotate(step, act_part, grad_part):
        act_hi, act_lo = split_two(dot_nn(act_part, bin_hi) + dot_nn(act_part, bin_lo))
        grad_hi, grad_lo = split_two(dot_nn(bout_hi, grad_part) + dot_nn(bout_lo, grad_part))
        gt_ref[0] = grad_hi.astype(jnp.float32)
        gt_ref[1] = grad_lo.astype(jnp.float32)
        spread_hi, spread_lo = [
            jnp.concatenate([
                jnp.where(own_token, jnp.broadcast_to(gt_ref[part, pl.ds(u, 1)], (batch, step_rows)), 0.0)
                for u in range(rank)
            ], axis=0).astype(jnp.bfloat16)
            for part in range(2)
        ]
        wide = dot_nn(spread_hi, jnp.concatenate([act_hi, act_lo], axis=1))
        rotated = wide[:, :2 * rank] + wide[:, 2 * rank:] + dot_nn(spread_lo, act_hi)
        start = pl.multiple_of(step * batch, batch)
        for u in range(half):
            value = jnp.where(
                first_lanes,
                rotated[u * batch:(u + 1) * batch],
                rotated[(u + half) * batch:(u + half + 1) * batch],
            ) * inverse[u:u + 1]
            feat[u, pl.ds(start, batch)] = value

    act_proj[...], grad_proj[...] = project(0)

    def body(step, carry):
        act_part, grad_part = act_proj[...], grad_proj[...]
        act_next, grad_next = project(step)
        rotate(step - 1, act_part, grad_part)
        act_proj[...] = act_next
        grad_proj[...] = grad_next
        return carry

    lax.fori_loop(1, steps, body, 0)
    rotate(steps - 1, act_proj[...], grad_proj[...])
    depth = half // slices
    me = lax.axis_index("mem") // cores
    for index in range(slices):
        start = (me ^ index) * depth
        piece = feat[pl.ds(start, depth)].astype(jnp.bfloat16)
        out_refs[index][pl.ds(0, depth * examples)] = piece.reshape(depth * examples, 2 * rank)
        out_refs[index][pl.ds(depth * examples, id_rows)] = digits


def features(slices, activations, out_grads, proj_in, proj_out, basis_in, basis_out, eigen, doc_ids):
    examples, tokens, width = activations.shape
    rank = proj_in.shape[1]
    rows = examples * tokens
    steps = examples // batch
    half = rank // 2
    hbm = pl.BlockSpec(memory_space=pl.ANY)
    vmem = pl.BlockSpec(memory_space=pltpu.VMEM)
    return pl.pallas_call(
        functools.partial(feature_kernel, tokens, slices),
        out_shape=[
            jax.ShapeDtypeStruct((half // slices * examples + id_rows, 2 * rank), jnp.bfloat16)
        ] * slices,
        in_specs=[hbm] * 8,
        out_specs=[vmem] * slices,
        scratch_shapes=[
            pltpu.VMEM((rows, width), jnp.bfloat16),
            pltpu.VMEM((rows, width), jnp.bfloat16),
            pltpu.VMEM((rank, width), jnp.bfloat16),
            pltpu.VMEM((rank, width), jnp.bfloat16),
            pltpu.VMEM((rank, rank), jnp.float32),
            pltpu.VMEM((rank, rank), jnp.float32),
            pltpu.VMEM((rank, rank), jnp.float32),
            pltpu.VMEM((1, examples), jnp.int32),
            pltpu.VMEM((batch * tokens, rank), jnp.bfloat16),
            pltpu.VMEM((rank, batch * tokens), jnp.bfloat16),
            pltpu.VMEM((2, rank, batch * tokens), jnp.float32),
            pltpu.VMEM((half, examples, 2 * rank), jnp.float32),
            pltpu.SemaphoreType.DMA((steps, parts)),
            pltpu.SemaphoreType.DMA((steps, parts)),
            pltpu.SemaphoreType.DMA((2,)),
            pltpu.SemaphoreType.DMA((4,)),
        ],
        compiler_params=pltpu.CompilerParams(vmem_limit_bytes=60 * 2**20),
        cost_estimate=pl.CostEstimate(
            flops=4 * rows * width * rank, bytes_accessed=4 * rows * width, transcendentals=0),
        name="features",
    )(
        activations.reshape(rows, width), out_grads.reshape(rows, width),
        proj_in.T, proj_out.T, basis_in, basis_out, eigen, doc_ids.reshape(1, examples),
    )


def slice_order(slices):
    return list(range(slices))


def product_kernel(slices, pieces, examples, row_groups, column_groups, *refs):
    runs = slices // pieces
    slabs = row_groups - 1 + 2 * column_groups
    ins, outs = refs[:runs * slabs], refs[runs * slabs:runs * slabs + slices]
    column_stack, row_stack, masked = refs[runs * slabs + slices:]
    piece_rows, lanes = ins[0].shape
    piece_rows = piece_rows // pieces
    depth = (piece_rows - id_rows) // examples
    mem = lax.axis_index("mem")
    pair, core = mem // cores, mem % cores

    def place(stack, digits, row, ref, piece):
        start = pl.multiple_of(row * examples, examples)
        for part in range(depth):
            stack[pl.ds(start, examples), pl.ds(part * lanes, lanes)] = (
                ref[pl.ds(piece * piece_rows + part * examples, examples)])
        some = ref[pl.ds((piece + 1) * piece_rows - id_rows, id_rows)].astype(jnp.float32)
        some = jnp.concatenate([some] * (digits.shape[1] // lanes), axis=1)
        block = lax.broadcasted_iota(jnp.int32, digits.shape, 1) // examples
        return jnp.where(block == row, some, digits)

    column_digits = jnp.zeros((id_rows, column_stack.shape[0]), jnp.float32)
    row_digits = jnp.zeros((id_rows, row_stack.shape[0]), jnp.float32)
    for run in range(runs):
        part = ins[run * slabs:(run + 1) * slabs]
        columns, others = part[:column_groups], part[column_groups:2 * column_groups]
        rows = (columns[0],) + tuple(part[2 * column_groups:])
        for piece in range(pieces):
            place_of = pair ^ slice_order(slices)[run * pieces + piece]
            for group in range(column_groups):
                for ref, side in ((columns[group], core), (others[group], core ^ 1)):
                    column = (group * slices + place_of) * cores + side
                    column_digits = place(column_stack, column_digits, column, ref, piece)
            for group in range(row_groups):
                row = place_of * row_groups + group
                row_digits = place(row_stack, row_digits, row, rows[group], piece)

    def halves(digits):
        return (digits[0:1] + digits[1:2] * 256.0, digits[2:3] + digits[3:4] * 256.0)

    column_low, column_high = halves(column_digits)
    row_low, row_high = halves(row_digits)
    result = dot_nt(row_stack[...], column_stack[...])
    for start in range(0, row_stack.shape[0], 128):
        low, high = (
            jnp.broadcast_to(row[:, start:start + 128], (128, 128)).T[:, 0:1] for row in (row_low, row_high))
        value = result[start:start + 128]
        value = jnp.where((low == column_low) & (high == column_high), 0.0, value)
        masked[pl.ds(start, 128)] = value.astype(jnp.bfloat16)
    count = row_groups * examples
    for index in range(slices):
        start = pl.multiple_of((pair ^ index) * count, count)
        outs[index][...] = masked[pl.ds(start, count)]


def products(slabs, slices, pieces, examples, row_groups, column_groups):
    piece_rows, lanes = slabs[0].shape
    depth = (piece_rows // pieces - id_rows) // examples
    vmem = pl.BlockSpec(memory_space=pltpu.VMEM)
    rows, cols = row_groups * slices * examples, column_groups * slices * cores * examples
    return pl.pallas_call(
        functools.partial(product_kernel, slices, pieces, examples, row_groups, column_groups),
        out_shape=[jax.ShapeDtypeStruct((row_groups * examples, cols), jnp.bfloat16)] * slices,
        in_specs=[vmem] * len(slabs),
        out_specs=[vmem] * slices,
        scratch_shapes=[
            pltpu.VMEM((cols, depth * lanes), jnp.bfloat16),
            pltpu.VMEM((rows, depth * lanes), jnp.bfloat16),
            pltpu.VMEM((rows, cols), jnp.bfloat16),
        ],
        compiler_params=pltpu.CompilerParams(vmem_limit_bytes=40 * 2**20),
        cost_estimate=pl.CostEstimate(
            flops=2 * rows * cols * depth * lanes, bytes_accessed=4 * rows * cols, transcendentals=0),
        name="products",
    )(*slabs)


def total_kernel(slices, *refs):
    parts, outs = refs[:slices], refs[slices:]
    examples = outs[0].shape[0]
    for group, out in enumerate(outs):
        rng = pl.ds(group * examples, examples)
        out[...] = sum(part[rng].astype(jnp.float32) for part in parts).astype(out.dtype)


def totals(parts, examples):
    rows, cols = parts[0].shape
    groups = rows // examples
    vmem = pl.BlockSpec(memory_space=pltpu.VMEM)
    return pl.pallas_call(
        functools.partial(total_kernel, len(parts)),
        out_shape=[
            jax.ShapeDtypeStruct((examples, cols), jnp.bfloat16 if group else jnp.float32)
            for group in range(groups)
        ],
        in_specs=[vmem] * len(parts),
        out_specs=[vmem] * groups,
        compiler_params=pltpu.CompilerParams(vmem_limit_bytes=40 * 2**20),
        cost_estimate=pl.CostEstimate(
            flops=rows * cols * len(parts), bytes_accessed=8 * rows * cols, transcendentals=0),
        name="totals",
    )(*parts)


def finish_kernel(factor, column_groups, *refs):
    parts, out_ref = refs[:-1], refs[-1]
    cols = parts[0].shape[1]
    width = cols // column_groups
    grp = lax.axis_index("grp")
    for row_step, part in enumerate(parts):
        value = part[...].astype(jnp.float32) * factor
        for column_step in range(column_groups):
            start = (grp ^ row_step ^ (column_step * len(parts))) * width
            out_ref[:, pl.ds(pl.multiple_of(start, width), width)] = (
                value[:, column_step * width:(column_step + 1) * width])


def finish(parts, column_groups, factor):
    examples, cols = parts[0].shape
    vmem = pl.BlockSpec(memory_space=pltpu.VMEM)
    return pl.pallas_call(
        functools.partial(finish_kernel, factor, column_groups),
        out_shape=jax.ShapeDtypeStruct((examples, len(parts) * cols), jnp.float32),
        in_specs=[vmem] * len(parts),
        out_specs=vmem,
        compiler_params=pltpu.CompilerParams(vmem_limit_bytes=40 * 2**20),
        cost_estimate=pl.CostEstimate(
            flops=8 * examples * cols, bytes_accessed=16 * examples * cols, transcendentals=0),
        name="finish",
    )(*parts)


def swap(value, axis, size, distance):
    if distance == 0:
        return value
    return lax.ppermute(value, axis, [(place, place ^ distance) for place in range(size)])


def on_device(members, groups, activations, out_grads, proj_in, proj_out, basis_in, basis_out, eigen, doc_ids):
    examples, tokens, width = activations.shape
    rank = proj_in.shape[1]
    factor = 1.0 / (tokens * rank)
    slices = members // cores
    runs = 2
    pieces = slices // runs
    row_groups = 1 << ((groups.bit_length() - 1) // 2)
    column_groups = groups // row_groups
    feat = features(slices, activations, out_grads, proj_in, proj_out, basis_in, basis_out, eigen, doc_ids)
    got = [swap(feat[index], "mem", members, cores * index) for index in slice_order(slices)]
    slabs = []
    for run in range(runs):
        slab = jnp.concatenate(got[run * pieces:(run + 1) * pieces], axis=0)
        if run:
            slab, slabs[column_groups] = lax.optimization_barrier((slab, slabs[column_groups]))
        columns = [swap(slab, "grp", groups, row_groups * step) for step in range(column_groups)]
        rows = [swap(slab, "grp", groups, step) for step in range(1, row_groups)]
        held = lax.optimization_barrier((*columns[1:], *rows))[:column_groups - 1]
        others = [swap(column, "mem", members, 1) for column in (slab, *held)]
        slabs += columns + others + rows
    partial = products(slabs, slices, pieces, examples, row_groups, column_groups)
    parts = [swap(partial[index], "mem", members, cores * index) for index in slice_order(slices)]
    sums = totals(parts, examples)
    sums = [swap(value, "grp", groups, step) for step, value in enumerate(sums)]
    return finish(sums, column_groups, factor)


def solution(mesh):
    return jax.shard_map(
        functools.partial(on_device, mesh.shape["mem"], mesh.shape["grp"]),
        mesh=mesh,
        in_specs=(
            P(("grp", "mem"), None, None),
            P(("grp", "mem"), None, None),
            P(),
            P(),
            P(),
            P(),
            P(),
            P(("grp", "mem")),
        ),
        out_specs=P(("grp", "mem"), None),
        check_vma=False,
    )
```

```python
import functools
import jax
import jax.numpy as jnp
from jax import lax
from jax.experimental import pallas as pl
from jax.experimental.pallas import tpu as pltpu
from jax.sharding import PartitionSpec as P

damping = 0.1
batch = 8
id_rows = 16
cores = 2


def dot_nn(a, b):
    return lax.dot_general(a, b, (((1,), (0,)), ((), ())), preferred_element_type=jnp.float32)


def dot_nt(a, b):
    return lax.dot_general(a, b, (((1,), (1,)), ((), ())), preferred_element_type=jnp.float32)


def split_two(value):
    high = value.astype(jnp.bfloat16)
    low = (value - high.astype(jnp.float32)).astype(jnp.bfloat16)
    return high, low


def feature_kernel(
    tokens, slices, act_hbm, grad_hbm, pin_hbm, pout_hbm, bin_hbm, bout_hbm, eigen_hbm, ids_hbm, *refs
):
    out_refs = refs[:slices]
    (act, grad, pin, pout, bin_ref, bout_ref, eigen_ref, ids_ref, act_proj, grad_proj, gt_ref, feat,
     act_sem, grad_sem, w_sem, s_sem) = refs[slices:]
    rows, width = act.shape
    rank = bin_ref.shape[0]
    half = rank // 2
    step_rows = batch * tokens
    steps = rows // step_rows
    examples = feat.shape[1]

    def step_copies(step):
        rng = pl.ds(pl.multiple_of(step * step_rows, step_rows), step_rows)
        return (
            pltpu.make_async_copy(act_hbm.at[rng], act.at[rng], act_sem.at[step]),
            pltpu.make_async_copy(grad_hbm.at[rng], grad.at[rng], grad_sem.at[step]),
        )

    weights = [
        pltpu.make_async_copy(pin_hbm, pin, w_sem.at[0]),
        pltpu.make_async_copy(pout_hbm, pout, w_sem.at[1]),
    ]
    def start_step(step):
        for priority, copy in enumerate(step_copies(step)):
            copy.start(priority=priority)

    small = [
        pltpu.make_async_copy(source, target, s_sem.at[index])
        for index, (source, target) in enumerate((
            (bin_hbm, bin_ref), (bout_hbm, bout_ref), (eigen_hbm, eigen_ref), (ids_hbm, ids_ref)))
    ]
    for copy in weights:
        copy.start()
    start_step(0)
    for copy in small:
        copy.start()
    for step in range(1, steps):
        start_step(step)
    for copy in small:
        copy.wait()

    bin_hi, bin_lo = split_two(jnp.concatenate([bin_ref[...], bin_ref[...]], axis=1))
    bout_hi, bout_lo = split_two(bout_ref[...].T)
    inverse = 1.0 / jnp.sqrt(eigen_ref[...] + damping)
    inverse = jnp.concatenate([inverse[:half], inverse[half:]], axis=1)
    own_token = (
        lax.broadcasted_iota(jnp.int32, (batch, step_rows), 1) // tokens
        == lax.broadcasted_iota(jnp.int32, (batch, step_rows), 0)
    )
    first_lanes = lax.broadcasted_iota(jnp.int32, (batch, 2 * rank), 1) < rank
    ids = jnp.concatenate([ids_ref[...]] * (2 * rank // examples), axis=1)
    place = lax.broadcasted_iota(jnp.int32, (id_rows, 2 * rank), 0) % 4
    digits = (jnp.broadcast_to(ids, (id_rows, 2 * rank)) >> (place * 8)) & 255
    digits = digits.astype(jnp.float32).astype(jnp.bfloat16)
    for copy in weights:
        copy.wait()

    def project(step):
        for copy in step_copies(step):
            copy.wait()
        rng = pl.ds(pl.multiple_of(step * step_rows, step_rows), step_rows)
        first, second = pl.ds(0, width // 2), pl.ds(width // 2, width // 2)
        return (
            (dot_nt(act[rng, first], pin[:, first]) + dot_nt(act[rng, second], pin[:, second])
             ).astype(jnp.bfloat16),
            (dot_nt(pout[:, first], grad[rng, first]) + dot_nt(pout[:, second], grad[rng, second])
             ).astype(jnp.bfloat16),
        )

    def rotate(step, act_part, grad_part):
        act_hi, act_lo = split_two(dot_nn(act_part, bin_hi) + dot_nn(act_part, bin_lo))
        gt_ref[...] = dot_nn(bout_hi, grad_part) + dot_nn(bout_lo, grad_part)
        spread = jnp.concatenate([
            jnp.where(own_token, jnp.broadcast_to(gt_ref[pl.ds(u, 1)], (batch, step_rows)), 0.0)
            for u in range(rank)
        ], axis=0).astype(jnp.bfloat16)
        wide = dot_nn(spread, jnp.concatenate([act_hi, act_lo], axis=1))
        rotated = wide[:, :2 * rank] + wide[:, 2 * rank:]
        start = pl.multiple_of(step * batch, batch)
        for u in range(half):
            value = jnp.where(
                first_lanes,
                rotated[u * batch:(u + 1) * batch],
                rotated[(u + half) * batch:(u + half + 1) * batch],
            ) * inverse[u:u + 1]
            feat[u, pl.ds(start, batch)] = value

    act_proj[...], grad_proj[...] = project(0)

    def body(step, carry):
        act_part, grad_part = act_proj[...], grad_proj[...]
        act_next, grad_next = project(step)
        rotate(step - 1, act_part, grad_part)
        act_proj[...] = act_next
        grad_proj[...] = grad_next
        return carry

    lax.fori_loop(1, steps, body, 0)
    rotate(steps - 1, act_proj[...], grad_proj[...])
    depth = half // slices
    me = lax.axis_index("mem") // cores
    for index in range(slices):
        start = (me ^ index) * depth
        piece = feat[pl.ds(start, depth)].astype(jnp.bfloat16)
        out_refs[index][pl.ds(0, depth * examples)] = piece.reshape(depth * examples, 2 * rank)
        out_refs[index][pl.ds(depth * examples, id_rows)] = digits


def features(slices, activations, out_grads, proj_in, proj_out, basis_in, basis_out, eigen, doc_ids):
    examples, tokens, width = activations.shape
    rank = proj_in.shape[1]
    rows = examples * tokens
    steps = examples // batch
    half = rank // 2
    hbm = pl.BlockSpec(memory_space=pl.ANY)
    vmem = pl.BlockSpec(memory_space=pltpu.VMEM)
    return pl.pallas_call(
        functools.partial(feature_kernel, tokens, slices),
        out_shape=[
            jax.ShapeDtypeStruct((half // slices * examples + id_rows, 2 * rank), jnp.bfloat16)
        ] * slices,
        in_specs=[hbm] * 8,
        out_specs=[vmem] * slices,
        scratch_shapes=[
            pltpu.VMEM((rows, width), jnp.bfloat16),
            pltpu.VMEM((rows, width), jnp.bfloat16),
            pltpu.VMEM((rank, width), jnp.bfloat16),
            pltpu.VMEM((rank, width), jnp.bfloat16),
            pltpu.VMEM((rank, rank), jnp.float32),
            pltpu.VMEM((rank, rank), jnp.float32),
            pltpu.VMEM((rank, rank), jnp.float32),
            pltpu.VMEM((1, examples), jnp.int32),
            pltpu.VMEM((batch * tokens, rank), jnp.bfloat16),
            pltpu.VMEM((rank, batch * tokens), jnp.bfloat16),
            pltpu.VMEM((rank, batch * tokens), jnp.float32),
            pltpu.VMEM((half, examples, 2 * rank), jnp.float32),
            pltpu.SemaphoreType.DMA((steps,)),
            pltpu.SemaphoreType.DMA((steps,)),
            pltpu.SemaphoreType.DMA((2,)),
            pltpu.SemaphoreType.DMA((4,)),
        ],
        compiler_params=pltpu.CompilerParams(vmem_limit_bytes=60 * 2**20),
        cost_estimate=pl.CostEstimate(
            flops=4 * rows * width * rank, bytes_accessed=4 * rows * width, transcendentals=0),
        name="features",
    )(
        activations.reshape(rows, width), out_grads.reshape(rows, width),
        proj_in.T, proj_out.T, basis_in, basis_out, eigen, doc_ids.reshape(1, examples),
    )


def slice_order(slices):
    return list(range(slices))


def product_kernel(slices, pieces, examples, row_groups, column_groups, *refs):
    runs = slices // pieces
    slabs = row_groups - 1 + 2 * column_groups
    count = row_groups * slices
    ins, outs = refs[:runs * slabs], refs[runs * slabs:runs * slabs + count]
    column_stack, row_stack, masked = refs[runs * slabs + count:]
    piece_rows, lanes = ins[0].shape
    piece_rows = piece_rows // pieces
    depth = (piece_rows - id_rows) // examples
    mem = lax.axis_index("mem")
    pair, core = mem // cores, mem % cores

    def place(stack, digits, row, ref, piece):
        start = pl.multiple_of(row * examples, examples)
        for part in range(depth):
            stack[pl.ds(start, examples), pl.ds(part * lanes, lanes)] = (
                ref[pl.ds(piece * piece_rows + part * examples, examples)])
        some = ref[pl.ds((piece + 1) * piece_rows - id_rows, id_rows)].astype(jnp.float32)
        some = jnp.concatenate([some] * (digits.shape[1] // lanes), axis=1)
        block = lax.broadcasted_iota(jnp.int32, digits.shape, 1) // examples
        return jnp.where(block == row, some, digits)

    column_digits = jnp.zeros((id_rows, column_stack.shape[0]), jnp.float32)
    row_digits = jnp.zeros((id_rows, row_stack.shape[0]), jnp.float32)
    for run in range(runs):
        part = ins[run * slabs:(run + 1) * slabs]
        columns, others = part[:column_groups], part[column_groups:2 * column_groups]
        rows = (columns[0],) + tuple(part[2 * column_groups:])
        for piece in range(pieces):
            place_of = pair ^ slice_order(slices)[run * pieces + piece]
            for group in range(column_groups):
                for ref, side in ((columns[group], core), (others[group], core ^ 1)):
                    column = (group * slices + place_of) * cores + side
                    column_digits = place(column_stack, column_digits, column, ref, piece)
            for group in range(row_groups):
                row = place_of * row_groups + group
                row_digits = place(row_stack, row_digits, row, rows[group], piece)

    def halves(digits):
        return (digits[0:1] + digits[1:2] * 256.0, digits[2:3] + digits[3:4] * 256.0)

    column_low, column_high = halves(column_digits)
    row_low, row_high = halves(row_digits)
    result = dot_nt(row_stack[...], column_stack[...])
    for start in range(0, row_stack.shape[0], 128):
        low, high = (
            jnp.broadcast_to(row[:, start:start + 128], (128, 128)).T[:, 0:1] for row in (row_low, row_high))
        value = result[start:start + 128]
        value = jnp.where((low == column_low) & (high == column_high), 0.0, value)
        masked[pl.ds(start, 128)] = value.astype(jnp.bfloat16)
    for index in range(count):
        group, step = index % row_groups, index // row_groups
        start = pl.multiple_of(((pair ^ step) * row_groups + group) * examples, examples)
        outs[index][...] = masked[pl.ds(start, examples)]


def products(slabs, slices, pieces, examples, row_groups, column_groups):
    piece_rows, lanes = slabs[0].shape
    depth = (piece_rows // pieces - id_rows) // examples
    vmem = pl.BlockSpec(memory_space=pltpu.VMEM)
    rows, cols = row_groups * slices * examples, column_groups * slices * cores * examples
    return pl.pallas_call(
        functools.partial(product_kernel, slices, pieces, examples, row_groups, column_groups),
        out_shape=[jax.ShapeDtypeStruct((examples, cols), jnp.bfloat16)] * (row_groups * slices),
        in_specs=[vmem] * len(slabs),
        out_specs=[vmem] * (row_groups * slices),
        scratch_shapes=[
            pltpu.VMEM((cols, depth * lanes), jnp.bfloat16),
            pltpu.VMEM((rows, depth * lanes), jnp.bfloat16),
            pltpu.VMEM((rows, cols), jnp.bfloat16),
        ],
        compiler_params=pltpu.CompilerParams(vmem_limit_bytes=40 * 2**20),
        cost_estimate=pl.CostEstimate(
            flops=2 * rows * cols * depth * lanes, bytes_accessed=4 * rows * cols, transcendentals=0),
        name="products",
    )(*slabs)


def finish_kernel(factor, row_groups, column_groups, *refs):
    parts, out_ref = refs[:-1], refs[-1]
    cols = parts[0].shape[1]
    width = cols // column_groups
    grp = lax.axis_index("grp")
    for row_step in range(row_groups):
        value = sum(part[...].astype(jnp.float32) for part in parts[row_step::row_groups]) * factor
        for column_step in range(column_groups):
            start = (grp ^ row_step ^ (column_step * row_groups)) * width
            out_ref[:, pl.ds(pl.multiple_of(start, width), width)] = (
                value[:, column_step * width:(column_step + 1) * width])


def finish(parts, row_groups, column_groups, factor):
    examples, cols = parts[0].shape
    vmem = pl.BlockSpec(memory_space=pltpu.VMEM)
    return pl.pallas_call(
        functools.partial(finish_kernel, factor, row_groups, column_groups),
        out_shape=jax.ShapeDtypeStruct((examples, row_groups * cols), jnp.float32),
        in_specs=[vmem] * len(parts),
        out_specs=vmem,
        compiler_params=pltpu.CompilerParams(vmem_limit_bytes=40 * 2**20),
        cost_estimate=pl.CostEstimate(
            flops=len(parts) * examples * cols, bytes_accessed=2 * len(parts) * examples * cols,
            transcendentals=0),
        name="finish",
    )(*parts)


def swap(value, axis, size, distance):
    if distance == 0:
        return value
    return lax.ppermute(value, axis, [(place, place ^ distance) for place in range(size)])


def on_device(members, groups, activations, out_grads, proj_in, proj_out, basis_in, basis_out, eigen, doc_ids):
    examples, tokens, width = activations.shape
    rank = proj_in.shape[1]
    factor = 1.0 / (tokens * rank)
    slices = members // cores
    runs = 2
    pieces = slices // runs
    row_groups = 1 << ((groups.bit_length() - 1) // 2)
    column_groups = groups // row_groups
    feat = features(slices, activations, out_grads, proj_in, proj_out, basis_in, basis_out, eigen, doc_ids)
    got = [swap(feat[index], "mem", members, cores * index) for index in slice_order(slices)]
    slabs = []
    for run in range(runs):
        slab = jnp.concatenate(got[run * pieces:(run + 1) * pieces], axis=0)
        if run:
            slab, slabs[column_groups] = lax.optimization_barrier((slab, slabs[column_groups]))
        columns = [swap(slab, "grp", groups, row_groups * step) for step in range(column_groups)]
        rows = [swap(slab, "grp", groups, step) for step in range(1, row_groups)]
        held = columns[1:]
        if run + 1 < runs:
            held = lax.optimization_barrier((*held, *rows))[:column_groups - 1]
        others = [swap(column, "mem", members, 1) for column in (slab, *held)]
        slabs += columns + others + rows
    partial = products(slabs, slices, pieces, examples, row_groups, column_groups)
    parts = [None] * len(partial)
    for index in reversed(range(len(partial))):
        group, step = index % row_groups, index // row_groups
        parts[index] = partial[index] if index == 0 else lax.ppermute(
            partial[index], ("grp", "mem"), [
                (place * members + member, (place ^ group) * members + (member ^ (step * cores)))
                for place in range(groups) for member in range(members)
            ])
    return finish(parts, row_groups, column_groups, factor)


def solution(mesh):
    return jax.shard_map(
        functools.partial(on_device, mesh.shape["mem"], mesh.shape["grp"]),
        mesh=mesh,
        in_specs=(
            P(("grp", "mem"), None, None),
            P(("grp", "mem"), None, None),
            P(),
            P(),
            P(),
            P(),
            P(),
            P(("grp", "mem")),
        ),
        out_specs=P(("grp", "mem"), None),
        check_vma=False,
    )
```

```python
import functools
import jax
import jax.numpy as jnp
from jax import lax
from jax.experimental import pallas as pl
from jax.experimental.pallas import tpu as pltpu
from jax.sharding import PartitionSpec as P

damping = 0.1
batch = 8
id_rows = 16
cores = 2


def dot_nn(a, b):
    return lax.dot_general(a, b, (((1,), (0,)), ((), ())), preferred_element_type=jnp.float32)


def dot_nt(a, b):
    return lax.dot_general(a, b, (((1,), (1,)), ((), ())), preferred_element_type=jnp.float32)


def split_two(value):
    high = value.astype(jnp.bfloat16)
    low = (value - high.astype(jnp.float32)).astype(jnp.bfloat16)
    return high, low


def feature_kernel(
    tokens, slices, act_hbm, grad_hbm, pin_hbm, pout_hbm, bin_hbm, bout_hbm, eigen_hbm, ids_hbm, *refs
):
    out_refs = refs[:slices]
    (act, grad, pin, pout, bin_ref, bout_ref, eigen_ref, ids_ref, act_proj, grad_proj, gt_ref, feat,
     act_sem, grad_sem, w_sem, s_sem) = refs[slices:]
    rows, width = act.shape
    rank = bin_ref.shape[0]
    half = rank // 2
    step_rows = batch * tokens
    steps = rows // step_rows
    examples = feat.shape[1]

    def step_copies(step):
        rng = pl.ds(pl.multiple_of(step * step_rows, step_rows), step_rows)
        return (
            pltpu.make_async_copy(act_hbm.at[rng], act.at[rng], act_sem.at[step]),
            pltpu.make_async_copy(grad_hbm.at[rng], grad.at[rng], grad_sem.at[step]),
        )

    weights = [
        pltpu.make_async_copy(pin_hbm, pin, w_sem.at[0]),
        pltpu.make_async_copy(pout_hbm, pout, w_sem.at[1]),
    ]
    def start_step(step):
        for priority, copy in enumerate(step_copies(step)):
            copy.start(priority=priority)

    small = [
        pltpu.make_async_copy(source, target, s_sem.at[index])
        for index, (source, target) in enumerate((
            (bin_hbm, bin_ref), (bout_hbm, bout_ref), (eigen_hbm, eigen_ref), (ids_hbm, ids_ref)))
    ]
    for copy in weights:
        copy.start()
    start_step(0)
    for copy in small:
        copy.start()
    for step in range(1, steps):
        start_step(step)
    for copy in small:
        copy.wait()

    bin_hi, bin_lo = split_two(jnp.concatenate([bin_ref[...], bin_ref[...]], axis=1))
    bout_hi, bout_lo = split_two(bout_ref[...].T)
    inverse = 1.0 / jnp.sqrt(eigen_ref[...] + damping)
    inverse = jnp.concatenate([inverse[:half], inverse[half:]], axis=1)
    own_token = (
        lax.broadcasted_iota(jnp.int32, (batch, step_rows), 1) // tokens
        == lax.broadcasted_iota(jnp.int32, (batch, step_rows), 0)
    )
    first_lanes = lax.broadcasted_iota(jnp.int32, (batch, 2 * rank), 1) < rank
    ids = jnp.concatenate([ids_ref[...]] * (2 * rank // examples), axis=1)
    place = lax.broadcasted_iota(jnp.int32, (id_rows, 2 * rank), 0) % 4
    digits = (jnp.broadcast_to(ids, (id_rows, 2 * rank)) >> (place * 8)) & 255
    digits = digits.astype(jnp.float32).astype(jnp.bfloat16)
    for copy in weights:
        copy.wait()

    def project(step):
        for copy in step_copies(step):
            copy.wait()
        rng = pl.ds(pl.multiple_of(step * step_rows, step_rows), step_rows)
        first, second = pl.ds(0, width // 2), pl.ds(width // 2, width // 2)
        return (
            (dot_nt(act[rng, first], pin[:, first]) + dot_nt(act[rng, second], pin[:, second])
             ).astype(jnp.bfloat16),
            (dot_nt(pout[:, first], grad[rng, first]) + dot_nt(pout[:, second], grad[rng, second])
             ).astype(jnp.bfloat16),
        )

    def rotate(step, act_part, grad_part):
        act_hi, act_lo = split_two(dot_nn(act_part, bin_hi) + dot_nn(act_part, bin_lo))
        grad_hi, grad_lo = split_two(dot_nn(bout_hi, grad_part) + dot_nn(bout_lo, grad_part))
        gt_ref[0] = grad_hi.astype(jnp.float32)
        gt_ref[1] = grad_lo.astype(jnp.float32)
        spread_hi, spread_lo = [
            jnp.concatenate([
                jnp.where(own_token, jnp.broadcast_to(gt_ref[part, pl.ds(u, 1)], (batch, step_rows)), 0.0)
                for u in range(rank)
            ], axis=0).astype(jnp.bfloat16)
            for part in range(2)
        ]
        wide = dot_nn(spread_hi, jnp.concatenate([act_hi, act_lo], axis=1))
        rotated = wide[:, :2 * rank] + wide[:, 2 * rank:] + dot_nn(spread_lo, act_hi)
        start = pl.multiple_of(step * batch, batch)
        for u in range(half):
            value = jnp.where(
                first_lanes,
                rotated[u * batch:(u + 1) * batch],
                rotated[(u + half) * batch:(u + half + 1) * batch],
            ) * inverse[u:u + 1]
            feat[u, pl.ds(start, batch)] = value

    act_proj[...], grad_proj[...] = project(0)

    def body(step, carry):
        act_part, grad_part = act_proj[...], grad_proj[...]
        act_next, grad_next = project(step)
        rotate(step - 1, act_part, grad_part)
        act_proj[...] = act_next
        grad_proj[...] = grad_next
        return carry

    lax.fori_loop(1, steps, body, 0)
    rotate(steps - 1, act_proj[...], grad_proj[...])
    depth = half // slices
    me = lax.axis_index("mem") // cores
    for index in range(slices):
        start = (me ^ index) * depth
        piece = feat[pl.ds(start, depth)].astype(jnp.bfloat16)
        out_refs[index][pl.ds(0, depth * examples)] = piece.reshape(depth * examples, 2 * rank)
        out_refs[index][pl.ds(depth * examples, id_rows)] = digits


def features(slices, activations, out_grads, proj_in, proj_out, basis_in, basis_out, eigen, doc_ids):
    examples, tokens, width = activations.shape
    rank = proj_in.shape[1]
    rows = examples * tokens
    steps = examples // batch
    half = rank // 2
    hbm = pl.BlockSpec(memory_space=pl.ANY)
    vmem = pl.BlockSpec(memory_space=pltpu.VMEM)
    return pl.pallas_call(
        functools.partial(feature_kernel, tokens, slices),
        out_shape=[
            jax.ShapeDtypeStruct((half // slices * examples + id_rows, 2 * rank), jnp.bfloat16)
        ] * slices,
        in_specs=[hbm] * 8,
        out_specs=[vmem] * slices,
        scratch_shapes=[
            pltpu.VMEM((rows, width), jnp.bfloat16),
            pltpu.VMEM((rows, width), jnp.bfloat16),
            pltpu.VMEM((rank, width), jnp.bfloat16),
            pltpu.VMEM((rank, width), jnp.bfloat16),
            pltpu.VMEM((rank, rank), jnp.float32),
            pltpu.VMEM((rank, rank), jnp.float32),
            pltpu.VMEM((rank, rank), jnp.float32),
            pltpu.VMEM((1, examples), jnp.int32),
            pltpu.VMEM((batch * tokens, rank), jnp.bfloat16),
            pltpu.VMEM((rank, batch * tokens), jnp.bfloat16),
            pltpu.VMEM((2, rank, batch * tokens), jnp.float32),
            pltpu.VMEM((half, examples, 2 * rank), jnp.float32),
            pltpu.SemaphoreType.DMA((steps,)),
            pltpu.SemaphoreType.DMA((steps,)),
            pltpu.SemaphoreType.DMA((2,)),
            pltpu.SemaphoreType.DMA((4,)),
        ],
        compiler_params=pltpu.CompilerParams(vmem_limit_bytes=60 * 2**20),
        cost_estimate=pl.CostEstimate(
            flops=4 * rows * width * rank, bytes_accessed=4 * rows * width, transcendentals=0),
        name="features",
    )(
        activations.reshape(rows, width), out_grads.reshape(rows, width),
        proj_in.T, proj_out.T, basis_in, basis_out, eigen, doc_ids.reshape(1, examples),
    )


def slice_order(slices):
    return list(range(slices))


def product_kernel(slices, pieces, examples, row_groups, column_groups, *refs):
    runs = slices // pieces
    slabs = row_groups - 1 + 2 * column_groups
    ins, outs = refs[:runs * slabs], refs[runs * slabs:runs * slabs + slices]
    column_stack, row_stack, masked = refs[runs * slabs + slices:]
    piece_rows, lanes = ins[0].shape
    piece_rows = piece_rows // pieces
    depth = (piece_rows - id_rows) // examples
    mem = lax.axis_index("mem")
    pair, core = mem // cores, mem % cores

    def place(stack, digits, row, ref, piece):
        start = pl.multiple_of(row * examples, examples)
        for part in range(depth):
            stack[pl.ds(start, examples), pl.ds(part * lanes, lanes)] = (
                ref[pl.ds(piece * piece_rows + part * examples, examples)])
        some = ref[pl.ds((piece + 1) * piece_rows - id_rows, id_rows)].astype(jnp.float32)
        some = jnp.concatenate([some] * (digits.shape[1] // lanes), axis=1)
        block = lax.broadcasted_iota(jnp.int32, digits.shape, 1) // examples
        return jnp.where(block == row, some, digits)

    column_digits = jnp.zeros((id_rows, column_stack.shape[0]), jnp.float32)
    row_digits = jnp.zeros((id_rows, row_stack.shape[0]), jnp.float32)
    for run in range(runs):
        part = ins[run * slabs:(run + 1) * slabs]
        columns, others = part[:column_groups], part[column_groups:2 * column_groups]
        rows = (columns[0],) + tuple(part[2 * column_groups:])
        for piece in range(pieces):
            place_of = pair ^ slice_order(slices)[run * pieces + piece]
            for group in range(column_groups):
                for ref, side in ((columns[group], core), (others[group], core ^ 1)):
                    column = (group * slices + place_of) * cores + side
                    column_digits = place(column_stack, column_digits, column, ref, piece)
            for group in range(row_groups):
                row = place_of * row_groups + group
                row_digits = place(row_stack, row_digits, row, rows[group], piece)

    def halves(digits):
        return (digits[0:1] + digits[1:2] * 256.0, digits[2:3] + digits[3:4] * 256.0)

    column_low, column_high = halves(column_digits)
    row_low, row_high = halves(row_digits)
    result = dot_nt(row_stack[...], column_stack[...])
    for start in range(0, row_stack.shape[0], 128):
        low, high = (
            jnp.broadcast_to(row[:, start:start + 128], (128, 128)).T[:, 0:1] for row in (row_low, row_high))
        value = result[start:start + 128]
        value = jnp.where((low == column_low) & (high == column_high), 0.0, value)
        masked[pl.ds(start, 128)] = value.astype(jnp.bfloat16)
    count = row_groups * examples
    for index in range(slices):
        start = pl.multiple_of((pair ^ index) * count, count)
        outs[index][...] = masked[pl.ds(start, count)]


def products(slabs, slices, pieces, examples, row_groups, column_groups):
    piece_rows, lanes = slabs[0].shape
    depth = (piece_rows // pieces - id_rows) // examples
    vmem = pl.BlockSpec(memory_space=pltpu.VMEM)
    rows, cols = row_groups * slices * examples, column_groups * slices * cores * examples
    return pl.pallas_call(
        functools.partial(product_kernel, slices, pieces, examples, row_groups, column_groups),
        out_shape=[jax.ShapeDtypeStruct((row_groups * examples, cols), jnp.bfloat16)] * slices,
        in_specs=[vmem] * len(slabs),
        out_specs=[vmem] * slices,
        scratch_shapes=[
            pltpu.VMEM((cols, depth * lanes), jnp.bfloat16),
            pltpu.VMEM((rows, depth * lanes), jnp.bfloat16),
            pltpu.VMEM((rows, cols), jnp.bfloat16),
        ],
        compiler_params=pltpu.CompilerParams(vmem_limit_bytes=40 * 2**20),
        cost_estimate=pl.CostEstimate(
            flops=2 * rows * cols * depth * lanes, bytes_accessed=4 * rows * cols, transcendentals=0),
        name="products",
    )(*slabs)


def total_kernel(slices, *refs):
    parts, outs = refs[:slices], refs[slices:]
    examples = outs[0].shape[0]
    for group, out in enumerate(outs):
        rng = pl.ds(group * examples, examples)
        out[...] = sum(part[rng].astype(jnp.float32) for part in parts).astype(out.dtype)


def totals(parts, examples):
    rows, cols = parts[0].shape
    groups = rows // examples
    vmem = pl.BlockSpec(memory_space=pltpu.VMEM)
    return pl.pallas_call(
        functools.partial(total_kernel, len(parts)),
        out_shape=[
            jax.ShapeDtypeStruct((examples, cols), jnp.bfloat16 if group else jnp.float32)
            for group in range(groups)
        ],
        in_specs=[vmem] * len(parts),
        out_specs=[vmem] * groups,
        compiler_params=pltpu.CompilerParams(vmem_limit_bytes=40 * 2**20),
        cost_estimate=pl.CostEstimate(
            flops=rows * cols * len(parts), bytes_accessed=8 * rows * cols, transcendentals=0),
        name="totals",
    )(*parts)


def finish_kernel(factor, column_groups, *refs):
    parts, out_ref = refs[:-1], refs[-1]
    cols = parts[0].shape[1]
    width = cols // column_groups
    grp = lax.axis_index("grp")
    for row_step, part in enumerate(parts):
        value = part[...].astype(jnp.float32) * factor
        for column_step in range(column_groups):
            start = (grp ^ row_step ^ (column_step * len(parts))) * width
            out_ref[:, pl.ds(pl.multiple_of(start, width), width)] = (
                value[:, column_step * width:(column_step + 1) * width])


def finish(parts, column_groups, factor):
    examples, cols = parts[0].shape
    vmem = pl.BlockSpec(memory_space=pltpu.VMEM)
    return pl.pallas_call(
        functools.partial(finish_kernel, factor, column_groups),
        out_shape=jax.ShapeDtypeStruct((examples, len(parts) * cols), jnp.float32),
        in_specs=[vmem] * len(parts),
        out_specs=vmem,
        compiler_params=pltpu.CompilerParams(vmem_limit_bytes=40 * 2**20),
        cost_estimate=pl.CostEstimate(
            flops=8 * examples * cols, bytes_accessed=16 * examples * cols, transcendentals=0),
        name="finish",
    )(*parts)


def swap(value, axis, size, distance):
    if distance == 0:
        return value
    return lax.ppermute(value, axis, [(place, place ^ distance) for place in range(size)])


def on_device(members, groups, activations, out_grads, proj_in, proj_out, basis_in, basis_out, eigen, doc_ids):
    examples, tokens, width = activations.shape
    rank = proj_in.shape[1]
    factor = 1.0 / (tokens * rank)
    slices = members // cores
    runs = 2
    pieces = slices // runs
    row_groups = 1 << ((groups.bit_length() - 1) // 2)
    column_groups = groups // row_groups
    feat = features(slices, activations, out_grads, proj_in, proj_out, basis_in, basis_out, eigen, doc_ids)
    got = [swap(feat[index], "mem", members, cores * index) for index in slice_order(slices)]
    slabs = []
    for run in range(runs):
        slab = jnp.concatenate(got[run * pieces:(run + 1) * pieces], axis=0)
        if run:
            slab, slabs[column_groups] = lax.optimization_barrier((slab, slabs[column_groups]))
        columns = [swap(slab, "grp", groups, row_groups * step) for step in range(column_groups)]
        rows = [swap(slab, "grp", groups, step) for step in range(1, row_groups)]
        held = columns[1:]
        if run + 1 < runs:
            held = lax.optimization_barrier((*held, *rows))[:column_groups - 1]
        others = [swap(column, "mem", members, 1) for column in (slab, *held)]
        slabs += columns + others + rows
    partial = products(slabs, slices, pieces, examples, row_groups, column_groups)
    parts = [partial[0]] + [
        swap(partial[index], "mem", members, cores * index) for index in reversed(range(1, slices))]
    sums = totals(parts, examples)
    sums = [swap(value, "grp", groups, step) for step, value in enumerate(sums)]
    return finish(sums, column_groups, factor)


def solution(mesh):
    return jax.shard_map(
        functools.partial(on_device, mesh.shape["mem"], mesh.shape["grp"]),
        mesh=mesh,
        in_specs=(
            P(("grp", "mem"), None, None),
            P(("grp", "mem"), None, None),
            P(),
            P(),
            P(),
            P(),
            P(),
            P(("grp", "mem")),
        ),
        out_specs=P(("grp", "mem"), None),
        check_vma=False,
    )
```

```python
import functools
import jax
import jax.numpy as jnp
from jax import lax
from jax.experimental import pallas as pl
from jax.experimental.pallas import tpu as pltpu
from jax.sharding import PartitionSpec as P

damping = 0.1
batch = 8
id_rows = 16
cores = 2


def dot_nn(a, b):
    return lax.dot_general(a, b, (((1,), (0,)), ((), ())), preferred_element_type=jnp.float32)


def dot_nt(a, b):
    return lax.dot_general(a, b, (((1,), (1,)), ((), ())), preferred_element_type=jnp.float32)


def split_two(value):
    high = value.astype(jnp.bfloat16)
    low = (value - high.astype(jnp.float32)).astype(jnp.bfloat16)
    return high, low


def feature_kernel(
    tokens, slices, act_hbm, grad_hbm, pin_hbm, pout_hbm, bin_hbm, bout_hbm, eigen_hbm, ids_hbm, *refs
):
    out_refs = refs[:slices]
    (act, grad, pin, pout, bin_ref, bout_ref, eigen_ref, ids_ref, act_proj, grad_proj, gt_ref, feat,
     act_sem, grad_sem, w_sem, s_sem) = refs[slices:]
    rows, width = act.shape
    rank = bin_ref.shape[0]
    half = rank // 2
    step_rows = batch * tokens
    steps = rows // step_rows
    examples = feat.shape[1]

    def step_copies(step):
        rng = pl.ds(pl.multiple_of(step * step_rows, step_rows), step_rows)
        return (
            pltpu.make_async_copy(act_hbm.at[rng], act.at[rng], act_sem.at[step]),
            pltpu.make_async_copy(grad_hbm.at[rng], grad.at[rng], grad_sem.at[step]),
        )

    weights = [
        pltpu.make_async_copy(pin_hbm, pin, w_sem.at[0]),
        pltpu.make_async_copy(pout_hbm, pout, w_sem.at[1]),
    ]
    def start_step(step):
        for priority, copy in enumerate(step_copies(step)):
            copy.start(priority=priority)

    small = [
        pltpu.make_async_copy(source, target, s_sem.at[index])
        for index, (source, target) in enumerate((
            (bin_hbm, bin_ref), (bout_hbm, bout_ref), (eigen_hbm, eigen_ref), (ids_hbm, ids_ref)))
    ]
    for copy in weights:
        copy.start()
    start_step(0)
    for copy in small:
        copy.start()
    for step in range(1, steps):
        start_step(step)
    for copy in small:
        copy.wait()

    bin_hi, bin_lo = split_two(jnp.concatenate([bin_ref[...], bin_ref[...]], axis=1))
    bout_hi, bout_lo = split_two(bout_ref[...].T)
    inverse = 1.0 / jnp.sqrt(eigen_ref[...] + damping)
    inverse = jnp.concatenate([inverse[:half], inverse[half:]], axis=1)
    own_token = (
        lax.broadcasted_iota(jnp.int32, (batch, step_rows), 1) // tokens
        == lax.broadcasted_iota(jnp.int32, (batch, step_rows), 0)
    )
    first_lanes = lax.broadcasted_iota(jnp.int32, (batch, 2 * rank), 1) < rank
    ids = jnp.concatenate([ids_ref[...]] * (2 * rank // examples), axis=1)
    place = lax.broadcasted_iota(jnp.int32, (id_rows, 2 * rank), 0) % 4
    digits = (jnp.broadcast_to(ids, (id_rows, 2 * rank)) >> (place * 8)) & 255
    digits = digits.astype(jnp.float32).astype(jnp.bfloat16)
    for copy in weights:
        copy.wait()

    def project(step):
        for copy in step_copies(step):
            copy.wait()
        rng = pl.ds(pl.multiple_of(step * step_rows, step_rows), step_rows)
        first, second = pl.ds(0, width // 2), pl.ds(width // 2, width // 2)
        return (
            (dot_nt(act[rng, first], pin[:, first]) + dot_nt(act[rng, second], pin[:, second])
             ).astype(jnp.bfloat16),
            (dot_nt(pout[:, first], grad[rng, first]) + dot_nt(pout[:, second], grad[rng, second])
             ).astype(jnp.bfloat16),
        )

    def rotate(step, act_part, grad_part):
        act_hi, act_lo = split_two(dot_nn(act_part, bin_hi) + dot_nn(act_part, bin_lo))
        grad_hi, grad_lo = split_two(dot_nn(bout_hi, grad_part) + dot_nn(bout_lo, grad_part))
        gt_ref[0] = grad_hi.astype(jnp.float32)
        gt_ref[1] = grad_lo.astype(jnp.float32)
        spread_hi, spread_lo = [
            jnp.concatenate([
                jnp.where(own_token, jnp.broadcast_to(gt_ref[part, pl.ds(u, 1)], (batch, step_rows)), 0.0)
                for u in range(rank)
            ], axis=0).astype(jnp.bfloat16)
            for part in range(2)
        ]
        wide = dot_nn(spread_hi, jnp.concatenate([act_hi, act_lo], axis=1))
        rotated = wide[:, :2 * rank] + wide[:, 2 * rank:] + dot_nn(spread_lo, act_hi)
        start = pl.multiple_of(step * batch, batch)
        for u in range(half):
            value = jnp.where(
                first_lanes,
                rotated[u * batch:(u + 1) * batch],
                rotated[(u + half) * batch:(u + half + 1) * batch],
            ) * inverse[u:u + 1]
            feat[u, pl.ds(start, batch)] = value

    act_proj[...], grad_proj[...] = project(0)

    def body(step, carry):
        act_part, grad_part = act_proj[...], grad_proj[...]
        act_next, grad_next = project(step)
        rotate(step - 1, act_part, grad_part)
        act_proj[...] = act_next
        grad_proj[...] = grad_next
        return carry

    lax.fori_loop(1, steps, body, 0)
    rotate(steps - 1, act_proj[...], grad_proj[...])
    depth = half // slices
    me = lax.axis_index("mem") // cores
    for index in range(slices):
        start = (me ^ index) * depth
        piece = feat[pl.ds(start, depth)].astype(jnp.bfloat16)
        out_refs[index][pl.ds(0, depth * examples)] = piece.reshape(depth * examples, 2 * rank)
        out_refs[index][pl.ds(depth * examples, id_rows)] = digits


def features(slices, activations, out_grads, proj_in, proj_out, basis_in, basis_out, eigen, doc_ids):
    examples, tokens, width = activations.shape
    rank = proj_in.shape[1]
    rows = examples * tokens
    steps = examples // batch
    half = rank // 2
    hbm = pl.BlockSpec(memory_space=pl.ANY)
    vmem = pl.BlockSpec(memory_space=pltpu.VMEM)
    return pl.pallas_call(
        functools.partial(feature_kernel, tokens, slices),
        out_shape=[
            jax.ShapeDtypeStruct((half // slices * examples + id_rows, 2 * rank), jnp.bfloat16)
        ] * slices,
        in_specs=[hbm] * 8,
        out_specs=[vmem] * slices,
        scratch_shapes=[
            pltpu.VMEM((rows, width), jnp.bfloat16),
            pltpu.VMEM((rows, width), jnp.bfloat16),
            pltpu.VMEM((rank, width), jnp.bfloat16),
            pltpu.VMEM((rank, width), jnp.bfloat16),
            pltpu.VMEM((rank, rank), jnp.float32),
            pltpu.VMEM((rank, rank), jnp.float32),
            pltpu.VMEM((rank, rank), jnp.float32),
            pltpu.VMEM((1, examples), jnp.int32),
            pltpu.VMEM((batch * tokens, rank), jnp.bfloat16),
            pltpu.VMEM((rank, batch * tokens), jnp.bfloat16),
            pltpu.VMEM((2, rank, batch * tokens), jnp.float32),
            pltpu.VMEM((half, examples, 2 * rank), jnp.float32),
            pltpu.SemaphoreType.DMA((steps,)),
            pltpu.SemaphoreType.DMA((steps,)),
            pltpu.SemaphoreType.DMA((2,)),
            pltpu.SemaphoreType.DMA((4,)),
        ],
        compiler_params=pltpu.CompilerParams(vmem_limit_bytes=60 * 2**20),
        cost_estimate=pl.CostEstimate(
            flops=4 * rows * width * rank, bytes_accessed=4 * rows * width, transcendentals=0),
        name="features",
    )(
        activations.reshape(rows, width), out_grads.reshape(rows, width),
        proj_in.T, proj_out.T, basis_in, basis_out, eigen, doc_ids.reshape(1, examples),
    )


def slice_order(slices):
    return [0, 1] + list(range(slices - 1, 1, -1))


def product_kernel(slices, pieces, examples, row_groups, column_groups, *refs):
    runs = slices // pieces
    slabs = row_groups - 1 + 2 * column_groups
    ins, outs = refs[:runs * slabs], refs[runs * slabs:runs * slabs + slices]
    column_stack, row_stack, masked = refs[runs * slabs + slices:]
    piece_rows, lanes = ins[0].shape
    piece_rows = piece_rows // pieces
    depth = (piece_rows - id_rows) // examples
    mem = lax.axis_index("mem")
    pair, core = mem // cores, mem % cores

    def place(stack, digits, row, ref, piece):
        start = pl.multiple_of(row * examples, examples)
        for part in range(depth):
            stack[pl.ds(start, examples), pl.ds(part * lanes, lanes)] = (
                ref[pl.ds(piece * piece_rows + part * examples, examples)])
        some = ref[pl.ds((piece + 1) * piece_rows - id_rows, id_rows)].astype(jnp.float32)
        some = jnp.concatenate([some] * (digits.shape[1] // lanes), axis=1)
        block = lax.broadcasted_iota(jnp.int32, digits.shape, 1) // examples
        return jnp.where(block == row, some, digits)

    column_digits = jnp.zeros((id_rows, column_stack.shape[0]), jnp.float32)
    row_digits = jnp.zeros((id_rows, row_stack.shape[0]), jnp.float32)
    for run in range(runs):
        part = ins[run * slabs:(run + 1) * slabs]
        columns, others = part[:column_groups], part[column_groups:2 * column_groups]
        rows = (columns[0],) + tuple(part[2 * column_groups:])
        for piece in range(pieces):
            place_of = pair ^ slice_order(slices)[run * pieces + piece]
            for group in range(column_groups):
                for ref, side in ((columns[group], core), (others[group], core ^ 1)):
                    column = (group * slices + place_of) * cores + side
                    column_digits = place(column_stack, column_digits, column, ref, piece)
            for group in range(row_groups):
                row = place_of * row_groups + group
                row_digits = place(row_stack, row_digits, row, rows[group], piece)

    def halves(digits):
        return (digits[0:1] + digits[1:2] * 256.0, digits[2:3] + digits[3:4] * 256.0)

    column_low, column_high = halves(column_digits)
    row_low, row_high = halves(row_digits)
    result = dot_nt(row_stack[...], column_stack[...])
    for start in range(0, row_stack.shape[0], 128):
        low, high = (
            jnp.broadcast_to(row[:, start:start + 128], (128, 128)).T[:, 0:1] for row in (row_low, row_high))
        value = result[start:start + 128]
        value = jnp.where((low == column_low) & (high == column_high), 0.0, value)
        masked[pl.ds(start, 128)] = value.astype(jnp.bfloat16)
    count = row_groups * examples
    for index in range(slices):
        start = pl.multiple_of((pair ^ index) * count, count)
        outs[index][...] = masked[pl.ds(start, count)]


def products(slabs, slices, pieces, examples, row_groups, column_groups):
    piece_rows, lanes = slabs[0].shape
    depth = (piece_rows // pieces - id_rows) // examples
    vmem = pl.BlockSpec(memory_space=pltpu.VMEM)
    rows, cols = row_groups * slices * examples, column_groups * slices * cores * examples
    return pl.pallas_call(
        functools.partial(product_kernel, slices, pieces, examples, row_groups, column_groups),
        out_shape=[jax.ShapeDtypeStruct((row_groups * examples, cols), jnp.bfloat16)] * slices,
        in_specs=[vmem] * len(slabs),
        out_specs=[vmem] * slices,
        scratch_shapes=[
            pltpu.VMEM((cols, depth * lanes), jnp.bfloat16),
            pltpu.VMEM((rows, depth * lanes), jnp.bfloat16),
            pltpu.VMEM((rows, cols), jnp.bfloat16),
        ],
        compiler_params=pltpu.CompilerParams(vmem_limit_bytes=40 * 2**20),
        cost_estimate=pl.CostEstimate(
            flops=2 * rows * cols * depth * lanes, bytes_accessed=4 * rows * cols, transcendentals=0),
        name="products",
    )(*slabs)


def total_kernel(slices, *refs):
    parts, outs = refs[:slices], refs[slices:]
    examples = outs[0].shape[0]
    for group, out in enumerate(outs):
        rng = pl.ds(group * examples, examples)
        out[...] = sum(part[rng].astype(jnp.float32) for part in parts).astype(out.dtype)


def totals(parts, examples):
    rows, cols = parts[0].shape
    groups = rows // examples
    vmem = pl.BlockSpec(memory_space=pltpu.VMEM)
    return pl.pallas_call(
        functools.partial(total_kernel, len(parts)),
        out_shape=[
            jax.ShapeDtypeStruct((examples, cols), jnp.bfloat16 if group else jnp.float32)
            for group in range(groups)
        ],
        in_specs=[vmem] * len(parts),
        out_specs=[vmem] * groups,
        compiler_params=pltpu.CompilerParams(vmem_limit_bytes=40 * 2**20),
        cost_estimate=pl.CostEstimate(
            flops=rows * cols * len(parts), bytes_accessed=8 * rows * cols, transcendentals=0),
        name="totals",
    )(*parts)


def finish_kernel(factor, column_groups, *refs):
    parts, out_ref = refs[:-1], refs[-1]
    cols = parts[0].shape[1]
    width = cols // column_groups
    grp = lax.axis_index("grp")
    for row_step, part in enumerate(parts):
        value = part[...].astype(jnp.float32) * factor
        for column_step in range(column_groups):
            start = (grp ^ row_step ^ (column_step * len(parts))) * width
            out_ref[:, pl.ds(pl.multiple_of(start, width), width)] = (
                value[:, column_step * width:(column_step + 1) * width])


def finish(parts, column_groups, factor):
    examples, cols = parts[0].shape
    vmem = pl.BlockSpec(memory_space=pltpu.VMEM)
    return pl.pallas_call(
        functools.partial(finish_kernel, factor, column_groups),
        out_shape=jax.ShapeDtypeStruct((examples, len(parts) * cols), jnp.float32),
        in_specs=[vmem] * len(parts),
        out_specs=vmem,
        compiler_params=pltpu.CompilerParams(vmem_limit_bytes=40 * 2**20),
        cost_estimate=pl.CostEstimate(
            flops=8 * examples * cols, bytes_accessed=16 * examples * cols, transcendentals=0),
        name="finish",
    )(*parts)


def swap(value, axis, size, distance):
    if distance == 0:
        return value
    return lax.ppermute(value, axis, [(place, place ^ distance) for place in range(size)])


def on_device(members, groups, activations, out_grads, proj_in, proj_out, basis_in, basis_out, eigen, doc_ids):
    examples, tokens, width = activations.shape
    rank = proj_in.shape[1]
    factor = 1.0 / (tokens * rank)
    slices = members // cores
    runs = 2
    pieces = slices // runs
    row_groups = 1 << ((groups.bit_length() - 1) // 2)
    column_groups = groups // row_groups
    feat = features(slices, activations, out_grads, proj_in, proj_out, basis_in, basis_out, eigen, doc_ids)
    got = [swap(feat[index], "mem", members, cores * index) for index in slice_order(slices)]
    slabs = []
    for run in range(runs):
        slab = jnp.concatenate(got[run * pieces:(run + 1) * pieces], axis=0)
        if run:
            slab, slabs[column_groups] = lax.optimization_barrier((slab, slabs[column_groups]))
        columns = [swap(slab, "grp", groups, row_groups * step) for step in range(column_groups)]
        rows = [swap(slab, "grp", groups, step) for step in range(1, row_groups)]
        held = columns[1:]
        if run + 1 < runs:
            held = lax.optimization_barrier((*held, *rows))[:column_groups - 1]
        others = [swap(column, "mem", members, 1) for column in (slab, *held)]
        slabs += columns + others + rows
    partial = products(slabs, slices, pieces, examples, row_groups, column_groups)
    parts = [partial[0]] + [
        swap(partial[index], "mem", members, cores * index) for index in reversed(range(1, slices))]
    sums = totals(parts, examples)
    sums = [swap(value, "grp", groups, step) for step, value in enumerate(sums)]
    return finish(sums, column_groups, factor)


def solution(mesh):
    return jax.shard_map(
        functools.partial(on_device, mesh.shape["mem"], mesh.shape["grp"]),
        mesh=mesh,
        in_specs=(
            P(("grp", "mem"), None, None),
            P(("grp", "mem"), None, None),
            P(),
            P(),
            P(),
            P(),
            P(),
            P(("grp", "mem")),
        ),
        out_specs=P(("grp", "mem"), None),
        check_vma=False,
    )
```

```python
import functools
import jax
import jax.numpy as jnp
from jax import lax
from jax.experimental import pallas as pl
from jax.experimental.pallas import tpu as pltpu
from jax.sharding import PartitionSpec as P

damping = 0.1
halves = 2
batch = 8
id_rows = 16
cores = 2


def dot_nn(a, b):
    return lax.dot_general(a, b, (((1,), (0,)), ((), ())), preferred_element_type=jnp.float32)


def dot_nt(a, b):
    return lax.dot_general(a, b, (((1,), (1,)), ((), ())), preferred_element_type=jnp.float32)


def split_two(value):
    high = value.astype(jnp.bfloat16)
    low = (value - high.astype(jnp.float32)).astype(jnp.bfloat16)
    return high, low


def feature_kernel(
    tokens, slices, act_hbm, grad_hbm, pin_hbm, pout_hbm, bin_hbm, bout_hbm, eigen_hbm, ids_hbm, *refs
):
    out_refs = refs[:slices]
    (act, grad, pin, pout, bin_ref, bout_ref, eigen_ref, ids_ref, act_proj, grad_proj, gt_ref, feat,
     act_sem, grad_sem, w_sem, s_sem) = refs[slices:]
    rows, width = act.shape
    rank = bin_ref.shape[0]
    half = rank // 2
    step_rows = batch * tokens
    steps = rows // step_rows
    examples = feat.shape[1]

    half_rows = rows // halves

    def half_copies(index):
        rng = pl.ds(index * half_rows, half_rows)
        return (
            pltpu.make_async_copy(act_hbm.at[rng], act.at[rng], act_sem.at[index]),
            pltpu.make_async_copy(grad_hbm.at[rng], grad.at[rng], grad_sem.at[index]),
        )

    weights = [
        pltpu.make_async_copy(pin_hbm, pin, w_sem.at[0]),
        pltpu.make_async_copy(pout_hbm, pout, w_sem.at[1]),
    ]
    def start_half(index):
        for priority, copy in enumerate(half_copies(index)):
            copy.start(priority=priority)

    small = [
        pltpu.make_async_copy(source, target, s_sem.at[index])
        for index, (source, target) in enumerate((
            (bin_hbm, bin_ref), (bout_hbm, bout_ref), (eigen_hbm, eigen_ref), (ids_hbm, ids_ref)))
    ]
    for copy in weights:
        copy.start()
    start_half(0)
    for copy in small:
        copy.start()
    for index in range(1, halves):
        start_half(index)
    for copy in small:
        copy.wait()

    bin_hi, bin_lo = split_two(jnp.concatenate([bin_ref[...], bin_ref[...]], axis=1))
    bout_hi, bout_lo = split_two(bout_ref[...].T)
    inverse = 1.0 / jnp.sqrt(eigen_ref[...] + damping)
    inverse = jnp.concatenate([inverse[:half], inverse[half:]], axis=1)
    own_token = (
        lax.broadcasted_iota(jnp.int32, (batch, step_rows), 1) // tokens
        == lax.broadcasted_iota(jnp.int32, (batch, step_rows), 0)
    )
    first_lanes = lax.broadcasted_iota(jnp.int32, (batch, 2 * rank), 1) < rank
    ids = jnp.concatenate([ids_ref[...]] * (2 * rank // examples), axis=1)
    place = lax.broadcasted_iota(jnp.int32, (id_rows, 2 * rank), 0) % 4
    digits = (jnp.broadcast_to(ids, (id_rows, 2 * rank)) >> (place * 8)) & 255
    digits = digits.astype(jnp.float32).astype(jnp.bfloat16)
    for copy in weights:
        copy.wait()

    def project(index):
        rng = pl.ds(index * half_rows, half_rows)
        act_copy, grad_copy = half_copies(index)
        act_copy.wait()
        act_proj[rng] = dot_nt(pin[...], act[rng]).T.astype(jnp.bfloat16)
        grad_copy.wait()
        grad_proj[:, rng] = dot_nt(pout[...], grad[rng]).astype(jnp.bfloat16)

    def rotate(step):
        rng = pl.ds(pl.multiple_of(step * step_rows, step_rows), step_rows)
        act_part, grad_part = act_proj[rng], grad_proj[:, rng]
        act_hi, act_lo = split_two(dot_nn(act_part, bin_hi) + dot_nn(act_part, bin_lo))
        grad_hi, grad_lo = split_two(dot_nn(bout_hi, grad_part) + dot_nn(bout_lo, grad_part))
        gt_ref[0] = grad_hi.astype(jnp.float32)
        gt_ref[1] = grad_lo.astype(jnp.float32)
        spread_hi, spread_lo = [
            jnp.concatenate([
                jnp.where(own_token, jnp.broadcast_to(gt_ref[part, pl.ds(u, 1)], (batch, step_rows)), 0.0)
                for u in range(rank)
            ], axis=0).astype(jnp.bfloat16)
            for part in range(2)
        ]
        wide = dot_nn(spread_hi, jnp.concatenate([act_hi, act_lo], axis=1))
        rotated = wide[:, :2 * rank] + wide[:, 2 * rank:] + dot_nn(spread_lo, act_hi)
        start = pl.multiple_of(step * batch, batch)
        for u in range(half):
            value = jnp.where(
                first_lanes,
                rotated[u * batch:(u + 1) * batch],
                rotated[(u + half) * batch:(u + half + 1) * batch],
            ) * inverse[u:u + 1]
            feat[u, pl.ds(start, batch)] = value

    each = steps // halves
    project(0)
    for index in range(1, halves):
        project(index)
        for step in range((index - 1) * each, index * each):
            rotate(step)
    lax.fori_loop(steps - each, steps, lambda step, carry: (rotate(step), carry)[1], 0)
    depth = half // slices
    me = lax.axis_index("mem") // cores
    for index in range(slices):
        start = (me ^ index) * depth
        piece = feat[pl.ds(start, depth)].astype(jnp.bfloat16)
        out_refs[index][pl.ds(0, depth * examples)] = piece.reshape(depth * examples, 2 * rank)
        out_refs[index][pl.ds(depth * examples, id_rows)] = digits


def features(slices, activations, out_grads, proj_in, proj_out, basis_in, basis_out, eigen, doc_ids):
    examples, tokens, width = activations.shape
    rank = proj_in.shape[1]
    rows = examples * tokens
    half = rank // 2
    hbm = pl.BlockSpec(memory_space=pl.ANY)
    vmem = pl.BlockSpec(memory_space=pltpu.VMEM)
    return pl.pallas_call(
        functools.partial(feature_kernel, tokens, slices),
        out_shape=[
            jax.ShapeDtypeStruct((half // slices * examples + id_rows, 2 * rank), jnp.bfloat16)
        ] * slices,
        in_specs=[hbm] * 8,
        out_specs=[vmem] * slices,
        scratch_shapes=[
            pltpu.VMEM((rows, width), jnp.bfloat16),
            pltpu.VMEM((rows, width), jnp.bfloat16),
            pltpu.VMEM((rank, width), jnp.bfloat16),
            pltpu.VMEM((rank, width), jnp.bfloat16),
            pltpu.VMEM((rank, rank), jnp.float32),
            pltpu.VMEM((rank, rank), jnp.float32),
            pltpu.VMEM((rank, rank), jnp.float32),
            pltpu.VMEM((1, examples), jnp.int32),
            pltpu.VMEM((rows, rank), jnp.bfloat16),
            pltpu.VMEM((rank, rows), jnp.bfloat16),
            pltpu.VMEM((2, rank, batch * tokens), jnp.float32),
            pltpu.VMEM((half, examples, 2 * rank), jnp.float32),
            pltpu.SemaphoreType.DMA((halves,)),
            pltpu.SemaphoreType.DMA((halves,)),
            pltpu.SemaphoreType.DMA((2,)),
            pltpu.SemaphoreType.DMA((4,)),
        ],
        compiler_params=pltpu.CompilerParams(vmem_limit_bytes=60 * 2**20),
        cost_estimate=pl.CostEstimate(
            flops=4 * rows * width * rank, bytes_accessed=4 * rows * width, transcendentals=0),
        name="features",
    )(
        activations.reshape(rows, width), out_grads.reshape(rows, width),
        proj_in.T, proj_out.T, basis_in, basis_out, eigen, doc_ids.reshape(1, examples),
    )


def slice_order(slices):
    return list(range(slices))


def product_kernel(slices, pieces, examples, row_groups, column_groups, *refs):
    runs = slices // pieces
    slabs = row_groups - 1 + 2 * column_groups
    ins, outs = refs[:runs * slabs], refs[runs * slabs:runs * slabs + slices]
    column_stack, row_stack, masked = refs[runs * slabs + slices:]
    piece_rows, lanes = ins[0].shape
    piece_rows = piece_rows // pieces
    depth = (piece_rows - id_rows) // examples
    mem = lax.axis_index("mem")
    pair, core = mem // cores, mem % cores

    def place(stack, digits, row, ref, piece):
        start = pl.multiple_of(row * examples, examples)
        for part in range(depth):
            stack[pl.ds(start, examples), pl.ds(part * lanes, lanes)] = (
                ref[pl.ds(piece * piece_rows + part * examples, examples)])
        some = ref[pl.ds((piece + 1) * piece_rows - id_rows, id_rows)].astype(jnp.float32)
        some = jnp.concatenate([some] * (digits.shape[1] // lanes), axis=1)
        block = lax.broadcasted_iota(jnp.int32, digits.shape, 1) // examples
        return jnp.where(block == row, some, digits)

    column_digits = jnp.zeros((id_rows, column_stack.shape[0]), jnp.float32)
    row_digits = jnp.zeros((id_rows, row_stack.shape[0]), jnp.float32)
    for run in range(runs):
        part = ins[run * slabs:(run + 1) * slabs]
        columns, others = part[:column_groups], part[column_groups:2 * column_groups]
        rows = (columns[0],) + tuple(part[2 * column_groups:])
        for piece in range(pieces):
            place_of = pair ^ slice_order(slices)[run * pieces + piece]
            for group in range(column_groups):
                for ref, side in ((columns[group], core), (others[group], core ^ 1)):
                    column = (group * slices + place_of) * cores + side
                    column_digits = place(column_stack, column_digits, column, ref, piece)
            for group in range(row_groups):
                row = place_of * row_groups + group
                row_digits = place(row_stack, row_digits, row, rows[group], piece)

    def halves(digits):
        return (digits[0:1] + digits[1:2] * 256.0, digits[2:3] + digits[3:4] * 256.0)

    column_low, column_high = halves(column_digits)
    row_low, row_high = halves(row_digits)
    result = dot_nt(row_stack[...], column_stack[...])
    for start in range(0, row_stack.shape[0], 128):
        low, high = (
            jnp.broadcast_to(row[:, start:start + 128], (128, 128)).T[:, 0:1] for row in (row_low, row_high))
        value = result[start:start + 128]
        value = jnp.where((low == column_low) & (high == column_high), 0.0, value)
        masked[pl.ds(start, 128)] = value.astype(jnp.bfloat16)
    count = row_groups * examples
    for index in range(slices):
        start = pl.multiple_of((pair ^ index) * count, count)
        outs[index][...] = masked[pl.ds(start, count)]


def products(slabs, slices, pieces, examples, row_groups, column_groups):
    piece_rows, lanes = slabs[0].shape
    depth = (piece_rows // pieces - id_rows) // examples
    vmem = pl.BlockSpec(memory_space=pltpu.VMEM)
    rows, cols = row_groups * slices * examples, column_groups * slices * cores * examples
    return pl.pallas_call(
        functools.partial(product_kernel, slices, pieces, examples, row_groups, column_groups),
        out_shape=[jax.ShapeDtypeStruct((row_groups * examples, cols), jnp.bfloat16)] * slices,
        in_specs=[vmem] * len(slabs),
        out_specs=[vmem] * slices,
        scratch_shapes=[
            pltpu.VMEM((cols, depth * lanes), jnp.bfloat16),
            pltpu.VMEM((rows, depth * lanes), jnp.bfloat16),
            pltpu.VMEM((rows, cols), jnp.bfloat16),
        ],
        compiler_params=pltpu.CompilerParams(vmem_limit_bytes=40 * 2**20),
        cost_estimate=pl.CostEstimate(
            flops=2 * rows * cols * depth * lanes, bytes_accessed=4 * rows * cols, transcendentals=0),
        name="products",
    )(*slabs)


def total_kernel(slices, *refs):
    parts, outs = refs[:slices], refs[slices:]
    examples = outs[0].shape[0]
    for group, out in enumerate(outs):
        rng = pl.ds(group * examples, examples)
        out[...] = sum(part[rng].astype(jnp.float32) for part in parts).astype(out.dtype)


def totals(parts, examples):
    rows, cols = parts[0].shape
    groups = rows // examples
    vmem = pl.BlockSpec(memory_space=pltpu.VMEM)
    return pl.pallas_call(
        functools.partial(total_kernel, len(parts)),
        out_shape=[
            jax.ShapeDtypeStruct((examples, cols), jnp.bfloat16 if group else jnp.float32)
            for group in range(groups)
        ],
        in_specs=[vmem] * len(parts),
        out_specs=[vmem] * groups,
        compiler_params=pltpu.CompilerParams(vmem_limit_bytes=40 * 2**20),
        cost_estimate=pl.CostEstimate(
            flops=rows * cols * len(parts), bytes_accessed=8 * rows * cols, transcendentals=0),
        name="totals",
    )(*parts)


def finish_kernel(factor, column_groups, *refs):
    parts, out_ref = refs[:-1], refs[-1]
    cols = parts[0].shape[1]
    width = cols // column_groups
    grp = lax.axis_index("grp")
    for row_step, part in enumerate(parts):
        value = part[...].astype(jnp.float32) * factor
        for column_step in range(column_groups):
            start = (grp ^ row_step ^ (column_step * len(parts))) * width
            out_ref[:, pl.ds(pl.multiple_of(start, width), width)] = (
                value[:, column_step * width:(column_step + 1) * width])


def finish(parts, column_groups, factor):
    examples, cols = parts[0].shape
    vmem = pl.BlockSpec(memory_space=pltpu.VMEM)
    return pl.pallas_call(
        functools.partial(finish_kernel, factor, column_groups),
        out_shape=jax.ShapeDtypeStruct((examples, len(parts) * cols), jnp.float32),
        in_specs=[vmem] * len(parts),
        out_specs=vmem,
        compiler_params=pltpu.CompilerParams(vmem_limit_bytes=40 * 2**20),
        cost_estimate=pl.CostEstimate(
            flops=8 * examples * cols, bytes_accessed=16 * examples * cols, transcendentals=0),
        name="finish",
    )(*parts)


def swap(value, axis, size, distance):
    if distance == 0:
        return value
    return lax.ppermute(value, axis, [(place, place ^ distance) for place in range(size)])


def on_device(members, groups, activations, out_grads, proj_in, proj_out, basis_in, basis_out, eigen, doc_ids):
    examples, tokens, width = activations.shape
    rank = proj_in.shape[1]
    factor = 1.0 / (tokens * rank)
    slices = members // cores
    runs = 2
    pieces = slices // runs
    row_groups = 1 << ((groups.bit_length() - 1) // 2)
    column_groups = groups // row_groups
    feat = features(slices, activations, out_grads, proj_in, proj_out, basis_in, basis_out, eigen, doc_ids)
    got = [swap(feat[index], "mem", members, cores * index) for index in slice_order(slices)]
    slabs = []
    for run in range(runs):
        slab = jnp.concatenate(got[run * pieces:(run + 1) * pieces], axis=0)
        if run:
            slab, slabs[column_groups] = lax.optimization_barrier((slab, slabs[column_groups]))
        columns = [swap(slab, "grp", groups, row_groups * step) for step in range(column_groups)]
        rows = [swap(slab, "grp", groups, step) for step in range(1, row_groups)]
        held = columns[1:]
        if run + 1 < runs:
            held = lax.optimization_barrier((*held, *rows))[:column_groups - 1]
        others = [swap(column, "mem", members, 1) for column in (slab, *held)]
        slabs += columns + others + rows
    partial = products(slabs, slices, pieces, examples, row_groups, column_groups)
    parts = [partial[0]] + [
        swap(partial[index], "mem", members, cores * index) for index in reversed(range(1, slices))]
    sums = totals(parts, examples)
    sums = [swap(value, "grp", groups, step) for step, value in enumerate(sums)]
    return finish(sums, column_groups, factor)


def solution(mesh):
    return jax.shard_map(
        functools.partial(on_device, mesh.shape["mem"], mesh.shape["grp"]),
        mesh=mesh,
        in_specs=(
            P(("grp", "mem"), None, None),
            P(("grp", "mem"), None, None),
            P(),
            P(),
            P(),
            P(),
            P(),
            P(("grp", "mem")),
        ),
        out_specs=P(("grp", "mem"), None),
        check_vma=False,
    )
```

```python
import functools
import jax
import jax.numpy as jnp
from jax import lax
from jax.experimental import pallas as pl
from jax.experimental.pallas import tpu as pltpu
from jax.sharding import PartitionSpec as P

damping = 0.1
halves = 2
batch = 8
id_rows = 16
cores = 2


def dot_nn(a, b):
    return lax.dot_general(a, b, (((1,), (0,)), ((), ())), preferred_element_type=jnp.float32)


def dot_nt(a, b):
    return lax.dot_general(a, b, (((1,), (1,)), ((), ())), preferred_element_type=jnp.float32)


def split_two(value):
    high = value.astype(jnp.bfloat16)
    low = (value - high.astype(jnp.float32)).astype(jnp.bfloat16)
    return high, low


def feature_kernel(
    tokens, slices, act_hbm, grad_hbm, pin_hbm, pout_hbm, bin_hbm, bout_hbm, eigen_hbm, ids_hbm, *refs
):
    out_refs = refs[:slices]
    (act, grad, pin, pout, bin_ref, bout_ref, eigen_ref, ids_ref, act_proj, grad_proj, gt_ref, feat,
     act_sem, grad_sem, w_sem, s_sem) = refs[slices:]
    rows, width = act.shape
    rank = bin_ref.shape[0]
    half = rank // 2
    step_rows = batch * tokens
    steps = rows // step_rows
    examples = feat.shape[1]

    half_rows = rows // halves

    def half_copies(index):
        piece_rows = half_rows // 2
        sets = []
        for source, target, sem in ((act_hbm, act, act_sem), (grad_hbm, grad, grad_sem)):
            pieces = []
            for piece in range(2):
                rng = pl.ds(index * half_rows + piece * piece_rows, piece_rows)
                pieces.append(pltpu.make_async_copy(source.at[rng], target.at[rng], sem.at[index, piece]))
            sets.append(pieces)
        return sets

    weights = [
        pltpu.make_async_copy(pin_hbm, pin, w_sem.at[0]),
        pltpu.make_async_copy(pout_hbm, pout, w_sem.at[1]),
    ]
    def start_half(index):
        for pieces in half_copies(index):
            for priority, copy in enumerate(pieces):
                copy.start(priority=priority)

    small = [
        pltpu.make_async_copy(source, target, s_sem.at[index])
        for index, (source, target) in enumerate((
            (bin_hbm, bin_ref), (bout_hbm, bout_ref), (eigen_hbm, eigen_ref), (ids_hbm, ids_ref)))
    ]
    for copy in weights:
        copy.start()
    start_half(0)
    for copy in small:
        copy.start()
    for index in range(1, halves):
        start_half(index)
    for copy in small:
        copy.wait()

    bin_hi, bin_lo = split_two(jnp.concatenate([bin_ref[...], bin_ref[...]], axis=1))
    bout_hi, bout_lo = split_two(bout_ref[...].T)
    inverse = 1.0 / jnp.sqrt(eigen_ref[...] + damping)
    inverse = jnp.concatenate([inverse[:half], inverse[half:]], axis=1)
    own_token = (
        lax.broadcasted_iota(jnp.int32, (batch, step_rows), 1) // tokens
        == lax.broadcasted_iota(jnp.int32, (batch, step_rows), 0)
    )
    first_lanes = lax.broadcasted_iota(jnp.int32, (batch, 2 * rank), 1) < rank
    ids = jnp.concatenate([ids_ref[...]] * (2 * rank // examples), axis=1)
    place = lax.broadcasted_iota(jnp.int32, (id_rows, 2 * rank), 0) % 4
    digits = (jnp.broadcast_to(ids, (id_rows, 2 * rank)) >> (place * 8)) & 255
    digits = digits.astype(jnp.float32).astype(jnp.bfloat16)
    for copy in weights:
        copy.wait()

    def project(index, between):
        rng = pl.ds(index * half_rows, half_rows)
        act_copies, grad_copies = half_copies(index)
        for copy in act_copies:
            copy.wait()
        act_proj[rng] = dot_nt(pin[...], act[rng]).T.astype(jnp.bfloat16)
        between()
        for copy in grad_copies:
            copy.wait()
        grad_proj[:, rng] = dot_nt(pout[...], grad[rng]).astype(jnp.bfloat16)

    def rotate(step):
        rng = pl.ds(pl.multiple_of(step * step_rows, step_rows), step_rows)
        act_part, grad_part = act_proj[rng], grad_proj[:, rng]
        act_hi, act_lo = split_two(dot_nn(act_part, bin_hi) + dot_nn(act_part, bin_lo))
        grad_hi, grad_lo = split_two(dot_nn(bout_hi, grad_part) + dot_nn(bout_lo, grad_part))
        gt_ref[0] = grad_hi.astype(jnp.float32)
        gt_ref[1] = grad_lo.astype(jnp.float32)
        spread_hi, spread_lo = [
            jnp.concatenate([
                jnp.where(own_token, jnp.broadcast_to(gt_ref[part, pl.ds(u, 1)], (batch, step_rows)), 0.0)
                for u in range(rank)
            ], axis=0).astype(jnp.bfloat16)
            for part in range(2)
        ]
        wide = dot_nn(spread_hi, jnp.concatenate([act_hi, act_lo], axis=1))
        rotated = wide[:, :2 * rank] + wide[:, 2 * rank:] + dot_nn(spread_lo, act_hi)
        start = pl.multiple_of(step * batch, batch)
        for u in range(half):
            value = jnp.where(
                first_lanes,
                rotated[u * batch:(u + 1) * batch],
                rotated[(u + half) * batch:(u + half + 1) * batch],
            ) * inverse[u:u + 1]
            feat[u, pl.ds(start, batch)] = value

    each = steps // halves
    project(0, lambda: None)
    for index in range(1, halves):
        project(index, lambda: [rotate(step) for step in range((index - 1) * each, index * each)])
    lax.fori_loop(steps - each, steps, lambda step, carry: (rotate(step), carry)[1], 0)
    depth = half // slices
    me = lax.axis_index("mem") // cores
    for index in range(slices):
        start = (me ^ index) * depth
        piece = feat[pl.ds(start, depth)].astype(jnp.bfloat16)
        out_refs[index][pl.ds(0, depth * examples)] = piece.reshape(depth * examples, 2 * rank)
        out_refs[index][pl.ds(depth * examples, id_rows)] = digits


def features(slices, activations, out_grads, proj_in, proj_out, basis_in, basis_out, eigen, doc_ids):
    examples, tokens, width = activations.shape
    rank = proj_in.shape[1]
    rows = examples * tokens
    half = rank // 2
    hbm = pl.BlockSpec(memory_space=pl.ANY)
    vmem = pl.BlockSpec(memory_space=pltpu.VMEM)
    return pl.pallas_call(
        functools.partial(feature_kernel, tokens, slices),
        out_shape=[
            jax.ShapeDtypeStruct((half // slices * examples + id_rows, 2 * rank), jnp.bfloat16)
        ] * slices,
        in_specs=[hbm] * 8,
        out_specs=[vmem] * slices,
        scratch_shapes=[
            pltpu.VMEM((rows, width), jnp.bfloat16),
            pltpu.VMEM((rows, width), jnp.bfloat16),
            pltpu.VMEM((rank, width), jnp.bfloat16),
            pltpu.VMEM((rank, width), jnp.bfloat16),
            pltpu.VMEM((rank, rank), jnp.float32),
            pltpu.VMEM((rank, rank), jnp.float32),
            pltpu.VMEM((rank, rank), jnp.float32),
            pltpu.VMEM((1, examples), jnp.int32),
            pltpu.VMEM((rows, rank), jnp.bfloat16),
            pltpu.VMEM((rank, rows), jnp.bfloat16),
            pltpu.VMEM((2, rank, batch * tokens), jnp.float32),
            pltpu.VMEM((half, examples, 2 * rank), jnp.float32),
            pltpu.SemaphoreType.DMA((halves, 2)),
            pltpu.SemaphoreType.DMA((halves, 2)),
            pltpu.SemaphoreType.DMA((2,)),
            pltpu.SemaphoreType.DMA((4,)),
        ],
        compiler_params=pltpu.CompilerParams(vmem_limit_bytes=60 * 2**20),
        cost_estimate=pl.CostEstimate(
            flops=4 * rows * width * rank, bytes_accessed=4 * rows * width, transcendentals=0),
        name="features",
    )(
        activations.reshape(rows, width), out_grads.reshape(rows, width),
        proj_in.T, proj_out.T, basis_in, basis_out, eigen, doc_ids.reshape(1, examples),
    )


def slice_order(slices):
    return list(range(slices))


def product_kernel(slices, pieces, examples, row_groups, column_groups, *refs):
    runs = slices // pieces
    slabs = row_groups - 1 + 2 * column_groups
    ins, outs = refs[:runs * slabs], refs[runs * slabs:runs * slabs + slices]
    column_stack, row_stack, masked = refs[runs * slabs + slices:]
    piece_rows, lanes = ins[0].shape
    piece_rows = piece_rows // pieces
    depth = (piece_rows - id_rows) // examples
    mem = lax.axis_index("mem")
    pair, core = mem // cores, mem % cores

    def place(stack, digits, row, ref, piece):
        start = pl.multiple_of(row * examples, examples)
        for part in range(depth):
            stack[pl.ds(start, examples), pl.ds(part * lanes, lanes)] = (
                ref[pl.ds(piece * piece_rows + part * examples, examples)])
        some = ref[pl.ds((piece + 1) * piece_rows - id_rows, id_rows)].astype(jnp.float32)
        some = jnp.concatenate([some] * (digits.shape[1] // lanes), axis=1)
        block = lax.broadcasted_iota(jnp.int32, digits.shape, 1) // examples
        return jnp.where(block == row, some, digits)

    column_digits = jnp.zeros((id_rows, column_stack.shape[0]), jnp.float32)
    row_digits = jnp.zeros((id_rows, row_stack.shape[0]), jnp.float32)
    for run in range(runs):
        part = ins[run * slabs:(run + 1) * slabs]
        columns, others = part[:column_groups], part[column_groups:2 * column_groups]
        rows = (columns[0],) + tuple(part[2 * column_groups:])
        for piece in range(pieces):
            place_of = pair ^ slice_order(slices)[run * pieces + piece]
            for group in range(column_groups):
                for ref, side in ((columns[group], core), (others[group], core ^ 1)):
                    column = (group * slices + place_of) * cores + side
                    column_digits = place(column_stack, column_digits, column, ref, piece)
            for group in range(row_groups):
                row = place_of * row_groups + group
                row_digits = place(row_stack, row_digits, row, rows[group], piece)

    def halves(digits):
        return (digits[0:1] + digits[1:2] * 256.0, digits[2:3] + digits[3:4] * 256.0)

    column_low, column_high = halves(column_digits)
    row_low, row_high = halves(row_digits)
    result = dot_nt(row_stack[...], column_stack[...])
    for start in range(0, row_stack.shape[0], 128):
        low, high = (
            jnp.broadcast_to(row[:, start:start + 128], (128, 128)).T[:, 0:1] for row in (row_low, row_high))
        value = result[start:start + 128]
        value = jnp.where((low == column_low) & (high == column_high), 0.0, value)
        masked[pl.ds(start, 128)] = value.astype(jnp.bfloat16)
    count = row_groups * examples
    for index in range(slices):
        start = pl.multiple_of((pair ^ index) * count, count)
        outs[index][...] = masked[pl.ds(start, count)]


def products(slabs, slices, pieces, examples, row_groups, column_groups):
    piece_rows, lanes = slabs[0].shape
    depth = (piece_rows // pieces - id_rows) // examples
    vmem = pl.BlockSpec(memory_space=pltpu.VMEM)
    rows, cols = row_groups * slices * examples, column_groups * slices * cores * examples
    return pl.pallas_call(
        functools.partial(product_kernel, slices, pieces, examples, row_groups, column_groups),
        out_shape=[jax.ShapeDtypeStruct((row_groups * examples, cols), jnp.bfloat16)] * slices,
        in_specs=[vmem] * len(slabs),
        out_specs=[vmem] * slices,
        scratch_shapes=[
            pltpu.VMEM((cols, depth * lanes), jnp.bfloat16),
            pltpu.VMEM((rows, depth * lanes), jnp.bfloat16),
            pltpu.VMEM((rows, cols), jnp.bfloat16),
        ],
        compiler_params=pltpu.CompilerParams(vmem_limit_bytes=40 * 2**20),
        cost_estimate=pl.CostEstimate(
            flops=2 * rows * cols * depth * lanes, bytes_accessed=4 * rows * cols, transcendentals=0),
        name="products",
    )(*slabs)


def total_kernel(slices, *refs):
    parts, outs = refs[:slices], refs[slices:]
    examples = outs[0].shape[0]
    for group, out in enumerate(outs):
        rng = pl.ds(group * examples, examples)
        out[...] = sum(part[rng].astype(jnp.float32) for part in parts).astype(out.dtype)


def totals(parts, examples):
    rows, cols = parts[0].shape
    groups = rows // examples
    vmem = pl.BlockSpec(memory_space=pltpu.VMEM)
    return pl.pallas_call(
        functools.partial(total_kernel, len(parts)),
        out_shape=[
            jax.ShapeDtypeStruct((examples, cols), jnp.bfloat16 if group else jnp.float32)
            for group in range(groups)
        ],
        in_specs=[vmem] * len(parts),
        out_specs=[vmem] * groups,
        compiler_params=pltpu.CompilerParams(vmem_limit_bytes=40 * 2**20),
        cost_estimate=pl.CostEstimate(
            flops=rows * cols * len(parts), bytes_accessed=8 * rows * cols, transcendentals=0),
        name="totals",
    )(*parts)


def finish_kernel(factor, column_groups, *refs):
    parts, out_ref = refs[:-1], refs[-1]
    cols = parts[0].shape[1]
    width = cols // column_groups
    grp = lax.axis_index("grp")
    for row_step, part in enumerate(parts):
        value = part[...].astype(jnp.float32) * factor
        for column_step in range(column_groups):
            start = (grp ^ row_step ^ (column_step * len(parts))) * width
            out_ref[:, pl.ds(pl.multiple_of(start, width), width)] = (
                value[:, column_step * width:(column_step + 1) * width])


def finish(parts, column_groups, factor):
    examples, cols = parts[0].shape
    vmem = pl.BlockSpec(memory_space=pltpu.VMEM)
    return pl.pallas_call(
        functools.partial(finish_kernel, factor, column_groups),
        out_shape=jax.ShapeDtypeStruct((examples, len(parts) * cols), jnp.float32),
        in_specs=[vmem] * len(parts),
        out_specs=vmem,
        compiler_params=pltpu.CompilerParams(vmem_limit_bytes=40 * 2**20),
        cost_estimate=pl.CostEstimate(
            flops=8 * examples * cols, bytes_accessed=16 * examples * cols, transcendentals=0),
        name="finish",
    )(*parts)


def swap(value, axis, size, distance):
    if distance == 0:
        return value
    return lax.ppermute(value, axis, [(place, place ^ distance) for place in range(size)])


def on_device(members, groups, activations, out_grads, proj_in, proj_out, basis_in, basis_out, eigen, doc_ids):
    examples, tokens, width = activations.shape
    rank = proj_in.shape[1]
    factor = 1.0 / (tokens * rank)
    slices = members // cores
    runs = 2
    pieces = slices // runs
    row_groups = 1 << ((groups.bit_length() - 1) // 2)
    column_groups = groups // row_groups
    feat = features(slices, activations, out_grads, proj_in, proj_out, basis_in, basis_out, eigen, doc_ids)
    got = [swap(feat[index], "mem", members, cores * index) for index in slice_order(slices)]
    slabs = []
    for run in range(runs):
        slab = jnp.concatenate(got[run * pieces:(run + 1) * pieces], axis=0)
        if run:
            slab, slabs[column_groups] = lax.optimization_barrier((slab, slabs[column_groups]))
        columns = [swap(slab, "grp", groups, row_groups * step) for step in range(column_groups)]
        rows = [swap(slab, "grp", groups, step) for step in range(1, row_groups)]
        held = columns[1:]
        if run + 1 < runs:
            held = lax.optimization_barrier((*held, *rows))[:column_groups - 1]
        others = [swap(column, "mem", members, 1) for column in (slab, *held)]
        slabs += columns + others + rows
    partial = products(slabs, slices, pieces, examples, row_groups, column_groups)
    parts = [partial[0]] + [
        swap(partial[index], "mem", members, cores * index) for index in reversed(range(1, slices))]
    sums = totals(parts, examples)
    sums = [swap(value, "grp", groups, step) for step, value in enumerate(sums)]
    return finish(sums, column_groups, factor)


def solution(mesh):
    return jax.shard_map(
        functools.partial(on_device, mesh.shape["mem"], mesh.shape["grp"]),
        mesh=mesh,
        in_specs=(
            P(("grp", "mem"), None, None),
            P(("grp", "mem"), None, None),
            P(),
            P(),
            P(),
            P(),
            P(),
            P(("grp", "mem")),
        ),
        out_specs=P(("grp", "mem"), None),
        check_vma=False,
    )
```

```python
import functools
import jax
import jax.numpy as jnp
from jax import lax
from jax.experimental import pallas as pl
from jax.experimental.pallas import tpu as pltpu
from jax.sharding import PartitionSpec as P

damping = 0.1
halves = 2
batch = 8
id_rows = 16
cores = 2


def dot_nn(a, b):
    return lax.dot_general(a, b, (((1,), (0,)), ((), ())), preferred_element_type=jnp.float32)


def dot_nt(a, b):
    return lax.dot_general(a, b, (((1,), (1,)), ((), ())), preferred_element_type=jnp.float32)


def split_two(value):
    high = value.astype(jnp.bfloat16)
    low = (value - high.astype(jnp.float32)).astype(jnp.bfloat16)
    return high, low


def feature_kernel(
    tokens, slices, act_hbm, grad_hbm, pin_hbm, pout_hbm, bin_hbm, bout_hbm, eigen_hbm, ids_hbm, *refs
):
    out_refs = refs[:slices]
    (act, grad, pin, pout, bin_ref, bout_ref, eigen_ref, ids_ref, act_proj, grad_proj, gt_ref, feat,
     act_sem, grad_sem, w_sem, s_sem) = refs[slices:]
    rows, width = act.shape
    rank = bin_ref.shape[0]
    half = rank // 2
    step_rows = batch * tokens
    steps = rows // step_rows
    examples = feat.shape[1]

    half_rows = rows // halves

    def half_copies(index):
        rng = pl.ds(index * half_rows, half_rows)
        return (
            pltpu.make_async_copy(act_hbm.at[rng], act.at[rng], act_sem.at[index]),
            pltpu.make_async_copy(grad_hbm.at[rng], grad.at[rng], grad_sem.at[index]),
        )

    weights = [
        pltpu.make_async_copy(pin_hbm, pin, w_sem.at[0]),
        pltpu.make_async_copy(pout_hbm, pout, w_sem.at[1]),
    ]
    def start_half(index):
        for priority, copy in enumerate(half_copies(index)):
            copy.start(priority=priority)

    small = [
        pltpu.make_async_copy(source, target, s_sem.at[index])
        for index, (source, target) in enumerate((
            (bin_hbm, bin_ref), (bout_hbm, bout_ref), (eigen_hbm, eigen_ref), (ids_hbm, ids_ref)))
    ]
    for copy in weights:
        copy.start()
    start_half(0)
    for copy in small:
        copy.start()
    for index in range(1, halves):
        start_half(index)
    for copy in small:
        copy.wait()

    bin_hi, bin_lo = split_two(jnp.concatenate([bin_ref[...], bin_ref[...]], axis=1))
    bout_hi, bout_lo = split_two(bout_ref[...].T)
    inverse = 1.0 / jnp.sqrt(eigen_ref[...] + damping)
    inverse = jnp.concatenate([inverse[:half], inverse[half:]], axis=1)
    own_token = (
        lax.broadcasted_iota(jnp.int32, (batch, step_rows), 1) // tokens
        == lax.broadcasted_iota(jnp.int32, (batch, step_rows), 0)
    )
    first_lanes = lax.broadcasted_iota(jnp.int32, (batch, 2 * rank), 1) < rank
    ids = jnp.concatenate([ids_ref[...]] * (2 * rank // examples), axis=1)
    place = lax.broadcasted_iota(jnp.int32, (id_rows, 2 * rank), 0) % 4
    digits = (jnp.broadcast_to(ids, (id_rows, 2 * rank)) >> (place * 8)) & 255
    digits = digits.astype(jnp.float32).astype(jnp.bfloat16)
    for copy in weights:
        copy.wait()

    def project(index, beside):
        rng = pl.ds(index * half_rows, half_rows)
        act_copy, grad_copy = half_copies(index)
        act_copy.wait()
        act_proj[rng] = dot_nt(pin[...], act[rng]).T.astype(jnp.bfloat16)
        for step in beside[0::2]:
            rotate(step)
        grad_copy.wait()
        grad_proj[:, rng] = dot_nt(pout[...], grad[rng]).astype(jnp.bfloat16)
        for step in beside[1::2]:
            rotate(step)

    def rotate(step):
        rng = pl.ds(step * step_rows, step_rows)
        act_part, grad_part = act_proj[rng], grad_proj[:, rng]
        act_hi, act_lo = split_two(dot_nn(act_part, bin_hi) + dot_nn(act_part, bin_lo))
        grad_hi, grad_lo = split_two(dot_nn(bout_hi, grad_part) + dot_nn(bout_lo, grad_part))
        gt_ref[step, 0] = grad_hi.astype(jnp.float32)
        gt_ref[step, 1] = grad_lo.astype(jnp.float32)
        spread_hi, spread_lo = [
            jnp.concatenate([
                jnp.where(own_token, jnp.broadcast_to(gt_ref[step, part, pl.ds(u, 1)], (batch, step_rows)), 0.0)
                for u in range(rank)
            ], axis=0).astype(jnp.bfloat16)
            for part in range(2)
        ]
        wide = dot_nn(spread_hi, jnp.concatenate([act_hi, act_lo], axis=1))
        rotated = wide[:, :2 * rank] + wide[:, 2 * rank:] + dot_nn(spread_lo, act_hi)
        start = step * batch
        for u in range(half):
            value = jnp.where(
                first_lanes,
                rotated[u * batch:(u + 1) * batch],
                rotated[(u + half) * batch:(u + half + 1) * batch],
            ) * inverse[u:u + 1]
            feat[u, pl.ds(start, batch)] = value

    each = steps // halves
    for index in range(halves + 1):
        beside = list(range(max(index - 1, 0) * each, index * each))
        if index < halves:
            project(index, beside)
        else:
            for step in beside:
                rotate(step)
    depth = half // slices
    me = lax.axis_index("mem") // cores
    for index in range(slices):
        start = (me ^ index) * depth
        piece = feat[pl.ds(start, depth)].astype(jnp.bfloat16)
        out_refs[index][pl.ds(0, depth * examples)] = piece.reshape(depth * examples, 2 * rank)
        out_refs[index][pl.ds(depth * examples, id_rows)] = digits


def features(slices, activations, out_grads, proj_in, proj_out, basis_in, basis_out, eigen, doc_ids):
    examples, tokens, width = activations.shape
    rank = proj_in.shape[1]
    rows = examples * tokens
    half = rank // 2
    hbm = pl.BlockSpec(memory_space=pl.ANY)
    vmem = pl.BlockSpec(memory_space=pltpu.VMEM)
    return pl.pallas_call(
        functools.partial(feature_kernel, tokens, slices),
        out_shape=[
            jax.ShapeDtypeStruct((half // slices * examples + id_rows, 2 * rank), jnp.bfloat16)
        ] * slices,
        in_specs=[hbm] * 8,
        out_specs=[vmem] * slices,
        scratch_shapes=[
            pltpu.VMEM((rows, width), jnp.bfloat16),
            pltpu.VMEM((rows, width), jnp.bfloat16),
            pltpu.VMEM((rank, width), jnp.bfloat16),
            pltpu.VMEM((rank, width), jnp.bfloat16),
            pltpu.VMEM((rank, rank), jnp.float32),
            pltpu.VMEM((rank, rank), jnp.float32),
            pltpu.VMEM((rank, rank), jnp.float32),
            pltpu.VMEM((1, examples), jnp.int32),
            pltpu.VMEM((rows, rank), jnp.bfloat16),
            pltpu.VMEM((rank, rows), jnp.bfloat16),
            pltpu.VMEM((examples // batch, 2, rank, batch * tokens), jnp.float32),
            pltpu.VMEM((half, examples, 2 * rank), jnp.float32),
            pltpu.SemaphoreType.DMA((halves,)),
            pltpu.SemaphoreType.DMA((halves,)),
            pltpu.SemaphoreType.DMA((2,)),
            pltpu.SemaphoreType.DMA((4,)),
        ],
        compiler_params=pltpu.CompilerParams(vmem_limit_bytes=60 * 2**20),
        cost_estimate=pl.CostEstimate(
            flops=4 * rows * width * rank, bytes_accessed=4 * rows * width, transcendentals=0),
        name="features",
    )(
        activations.reshape(rows, width), out_grads.reshape(rows, width),
        proj_in.T, proj_out.T, basis_in, basis_out, eigen, doc_ids.reshape(1, examples),
    )


def slice_order(slices):
    return list(range(slices))


def product_kernel(slices, pieces, examples, row_groups, column_groups, *refs):
    runs = slices // pieces
    slabs = row_groups - 1 + 2 * column_groups
    ins, outs = refs[:runs * slabs], refs[runs * slabs:runs * slabs + slices]
    column_stack, row_stack, masked = refs[runs * slabs + slices:]
    piece_rows, lanes = ins[0].shape
    piece_rows = piece_rows // pieces
    depth = (piece_rows - id_rows) // examples
    mem = lax.axis_index("mem")
    pair, core = mem // cores, mem % cores

    def place(stack, digits, row, ref, piece):
        start = pl.multiple_of(row * examples, examples)
        for part in range(depth):
            stack[pl.ds(start, examples), pl.ds(part * lanes, lanes)] = (
                ref[pl.ds(piece * piece_rows + part * examples, examples)])
        some = ref[pl.ds((piece + 1) * piece_rows - id_rows, id_rows)].astype(jnp.float32)
        some = jnp.concatenate([some] * (digits.shape[1] // lanes), axis=1)
        block = lax.broadcasted_iota(jnp.int32, digits.shape, 1) // examples
        return jnp.where(block == row, some, digits)

    column_digits = jnp.zeros((id_rows, column_stack.shape[0]), jnp.float32)
    row_digits = jnp.zeros((id_rows, row_stack.shape[0]), jnp.float32)
    for run in range(runs):
        part = ins[run * slabs:(run + 1) * slabs]
        columns, others = part[:column_groups], part[column_groups:2 * column_groups]
        rows = (columns[0],) + tuple(part[2 * column_groups:])
        for piece in range(pieces):
            place_of = pair ^ slice_order(slices)[run * pieces + piece]
            for group in range(column_groups):
                for ref, side in ((columns[group], core), (others[group], core ^ 1)):
                    column = (group * slices + place_of) * cores + side
                    column_digits = place(column_stack, column_digits, column, ref, piece)
            for group in range(row_groups):
                row = place_of * row_groups + group
                row_digits = place(row_stack, row_digits, row, rows[group], piece)

    def halves(digits):
        return (digits[0:1] + digits[1:2] * 256.0, digits[2:3] + digits[3:4] * 256.0)

    column_low, column_high = halves(column_digits)
    row_low, row_high = halves(row_digits)
    result = dot_nt(row_stack[...], column_stack[...])
    for start in range(0, row_stack.shape[0], 128):
        low, high = (
            jnp.broadcast_to(row[:, start:start + 128], (128, 128)).T[:, 0:1] for row in (row_low, row_high))
        value = result[start:start + 128]
        value = jnp.where((low == column_low) & (high == column_high), 0.0, value)
        masked[pl.ds(start, 128)] = value.astype(jnp.bfloat16)
    count = row_groups * examples
    for index in range(slices):
        start = pl.multiple_of((pair ^ index) * count, count)
        outs[index][...] = masked[pl.ds(start, count)]


def products(slabs, slices, pieces, examples, row_groups, column_groups):
    piece_rows, lanes = slabs[0].shape
    depth = (piece_rows // pieces - id_rows) // examples
    vmem = pl.BlockSpec(memory_space=pltpu.VMEM)
    rows, cols = row_groups * slices * examples, column_groups * slices * cores * examples
    return pl.pallas_call(
        functools.partial(product_kernel, slices, pieces, examples, row_groups, column_groups),
        out_shape=[jax.ShapeDtypeStruct((row_groups * examples, cols), jnp.bfloat16)] * slices,
        in_specs=[vmem] * len(slabs),
        out_specs=[vmem] * slices,
        scratch_shapes=[
            pltpu.VMEM((cols, depth * lanes), jnp.bfloat16),
            pltpu.VMEM((rows, depth * lanes), jnp.bfloat16),
            pltpu.VMEM((rows, cols), jnp.bfloat16),
        ],
        compiler_params=pltpu.CompilerParams(vmem_limit_bytes=40 * 2**20),
        cost_estimate=pl.CostEstimate(
            flops=2 * rows * cols * depth * lanes, bytes_accessed=4 * rows * cols, transcendentals=0),
        name="products",
    )(*slabs)


def total_kernel(slices, *refs):
    parts, outs = refs[:slices], refs[slices:]
    examples = outs[0].shape[0]
    for group, out in enumerate(outs):
        rng = pl.ds(group * examples, examples)
        out[...] = sum(part[rng].astype(jnp.float32) for part in parts).astype(out.dtype)


def totals(parts, examples):
    rows, cols = parts[0].shape
    groups = rows // examples
    vmem = pl.BlockSpec(memory_space=pltpu.VMEM)
    return pl.pallas_call(
        functools.partial(total_kernel, len(parts)),
        out_shape=[
            jax.ShapeDtypeStruct((examples, cols), jnp.bfloat16 if group else jnp.float32)
            for group in range(groups)
        ],
        in_specs=[vmem] * len(parts),
        out_specs=[vmem] * groups,
        compiler_params=pltpu.CompilerParams(vmem_limit_bytes=40 * 2**20),
        cost_estimate=pl.CostEstimate(
            flops=rows * cols * len(parts), bytes_accessed=8 * rows * cols, transcendentals=0),
        name="totals",
    )(*parts)


def finish_kernel(factor, column_groups, *refs):
    parts, out_ref = refs[:-1], refs[-1]
    cols = parts[0].shape[1]
    width = cols // column_groups
    grp = lax.axis_index("grp")
    for row_step, part in enumerate(parts):
        value = part[...].astype(jnp.float32) * factor
        for column_step in range(column_groups):
            start = (grp ^ row_step ^ (column_step * len(parts))) * width
            out_ref[:, pl.ds(pl.multiple_of(start, width), width)] = (
                value[:, column_step * width:(column_step + 1) * width])


def finish(parts, column_groups, factor):
    examples, cols = parts[0].shape
    vmem = pl.BlockSpec(memory_space=pltpu.VMEM)
    return pl.pallas_call(
        functools.partial(finish_kernel, factor, column_groups),
        out_shape=jax.ShapeDtypeStruct((examples, len(parts) * cols), jnp.float32),
        in_specs=[vmem] * len(parts),
        out_specs=vmem,
        compiler_params=pltpu.CompilerParams(vmem_limit_bytes=40 * 2**20),
        cost_estimate=pl.CostEstimate(
            flops=8 * examples * cols, bytes_accessed=16 * examples * cols, transcendentals=0),
        name="finish",
    )(*parts)


def swap(value, axis, size, distance):
    if distance == 0:
        return value
    return lax.ppermute(value, axis, [(place, place ^ distance) for place in range(size)])


def on_device(members, groups, activations, out_grads, proj_in, proj_out, basis_in, basis_out, eigen, doc_ids):
    examples, tokens, width = activations.shape
    rank = proj_in.shape[1]
    factor = 1.0 / (tokens * rank)
    slices = members // cores
    runs = 2
    pieces = slices // runs
    row_groups = 1 << ((groups.bit_length() - 1) // 2)
    column_groups = groups // row_groups
    feat = features(slices, activations, out_grads, proj_in, proj_out, basis_in, basis_out, eigen, doc_ids)
    got = [swap(feat[index], "mem", members, cores * index) for index in slice_order(slices)]
    slabs = []
    for run in range(runs):
        slab = jnp.concatenate(got[run * pieces:(run + 1) * pieces], axis=0)
        if run:
            slab, slabs[column_groups] = lax.optimization_barrier((slab, slabs[column_groups]))
        columns = [swap(slab, "grp", groups, row_groups * step) for step in range(column_groups)]
        rows = [swap(slab, "grp", groups, step) for step in range(1, row_groups)]
        held = columns[1:]
        if run + 1 < runs:
            held = lax.optimization_barrier((*held, *rows))[:column_groups - 1]
        others = [swap(column, "mem", members, 1) for column in (slab, *held)]
        slabs += columns + others + rows
    partial = products(slabs, slices, pieces, examples, row_groups, column_groups)
    parts = [partial[0]] + [
        swap(partial[index], "mem", members, cores * index) for index in reversed(range(1, slices))]
    sums = totals(parts, examples)
    sums = [swap(value, "grp", groups, step) for step, value in enumerate(sums)]
    return finish(sums, column_groups, factor)


def solution(mesh):
    return jax.shard_map(
        functools.partial(on_device, mesh.shape["mem"], mesh.shape["grp"]),
        mesh=mesh,
        in_specs=(
            P(("grp", "mem"), None, None),
            P(("grp", "mem"), None, None),
            P(),
            P(),
            P(),
            P(),
            P(),
            P(("grp", "mem")),
        ),
        out_specs=P(("grp", "mem"), None),
        check_vma=False,
    )
```

```python
import functools
import jax
import jax.numpy as jnp
from jax import lax
from jax.experimental import pallas as pl
from jax.experimental.pallas import tpu as pltpu
from jax.sharding import PartitionSpec as P

damping = 0.1
halves = 2
batch = 8
id_rows = 16
cores = 2


def dot_nn(a, b):
    return lax.dot_general(a, b, (((1,), (0,)), ((), ())), preferred_element_type=jnp.float32)


def dot_nt(a, b):
    return lax.dot_general(a, b, (((1,), (1,)), ((), ())), preferred_element_type=jnp.float32)


def split_two(value):
    high = value.astype(jnp.bfloat16)
    low = (value - high.astype(jnp.float32)).astype(jnp.bfloat16)
    return high, low


def feature_kernel(
    tokens, slices, act_hbm, grad_hbm, pin_hbm, pout_hbm, bin_hbm, bout_hbm, eigen_hbm, ids_hbm, *refs
):
    out_refs = refs[:slices]
    (act, grad, pin, pout, bin_ref, bout_ref, eigen_ref, ids_ref, act_proj, grad_proj, gt_ref, feat,
     act_sem, grad_sem, w_sem, s_sem) = refs[slices:]
    rows, width = act.shape
    rank = bin_ref.shape[0]
    half = rank // 2
    step_rows = batch * tokens
    steps = rows // step_rows
    examples = feat.shape[1]

    half_rows = rows // halves

    def half_copies(index):
        rng = pl.ds(index * half_rows, half_rows)
        return (
            pltpu.make_async_copy(act_hbm.at[rng], act.at[rng], act_sem.at[index]),
            pltpu.make_async_copy(grad_hbm.at[rng], grad.at[rng], grad_sem.at[index]),
        )

    weights = [
        pltpu.make_async_copy(pin_hbm, pin, w_sem.at[0]),
        pltpu.make_async_copy(pout_hbm, pout, w_sem.at[1]),
    ]
    def start_half(index):
        for priority, copy in enumerate(half_copies(index)):
            copy.start(priority=priority)

    small = [
        pltpu.make_async_copy(source, target, s_sem.at[index])
        for index, (source, target) in enumerate((
            (bin_hbm, bin_ref), (bout_hbm, bout_ref), (eigen_hbm, eigen_ref), (ids_hbm, ids_ref)))
    ]
    for copy in weights:
        copy.start()
    start_half(0)
    for copy in small:
        copy.start()
    for index in range(1, halves):
        start_half(index)
    for copy in small:
        copy.wait()

    bin_hi, bin_lo = split_two(jnp.concatenate([bin_ref[...], bin_ref[...]], axis=1))
    bout_hi, bout_lo = split_two(bout_ref[...].T)
    inverse = 1.0 / jnp.sqrt(eigen_ref[...] + damping)
    inverse = jnp.concatenate([inverse[:half], inverse[half:]], axis=1)
    own_token = (
        lax.broadcasted_iota(jnp.int32, (batch, step_rows), 1) // tokens
        == lax.broadcasted_iota(jnp.int32, (batch, step_rows), 0)
    )
    first_lanes = lax.broadcasted_iota(jnp.int32, (batch, 2 * rank), 1) < rank
    ids = jnp.concatenate([ids_ref[...]] * (2 * rank // examples), axis=1)
    place = lax.broadcasted_iota(jnp.int32, (id_rows, 2 * rank), 0) % 4
    digits = (jnp.broadcast_to(ids, (id_rows, 2 * rank)) >> (place * 8)) & 255
    digits = digits.astype(jnp.float32).astype(jnp.bfloat16)
    for copy in weights:
        copy.wait()

    def project(index, beside):
        rng = pl.ds(index * half_rows, half_rows)
        act_copy, grad_copy = half_copies(index)
        act_copy.wait()
        act_proj[rng] = dot_nt(pin[...], act[rng]).T.astype(jnp.bfloat16)
        for step in beside[0::2]:
            rotate(step)
        grad_copy.wait()
        grad_proj[:, rng] = dot_nt(pout[...], grad[rng]).astype(jnp.bfloat16)
        for step in beside[1::2]:
            rotate(step)

    def rotate(step):
        rng = pl.ds(step * step_rows, step_rows)
        act_part, grad_part = act_proj[rng], grad_proj[:, rng]
        act_hi, act_lo = split_two(dot_nn(act_part, bin_hi) + dot_nn(act_part, bin_lo))
        grad_hi, grad_lo = split_two(dot_nn(bout_hi, grad_part) + dot_nn(bout_lo, grad_part))
        gt_ref[step, 0] = grad_hi.astype(jnp.float32)
        gt_ref[step, 1] = grad_lo.astype(jnp.float32)
        spread_hi, spread_lo = [
            jnp.concatenate([
                jnp.where(own_token, jnp.broadcast_to(gt_ref[step, part, pl.ds(u, 1)], (batch, step_rows)), 0.0)
                for u in range(rank)
            ], axis=0).astype(jnp.bfloat16)
            for part in range(2)
        ]
        wide = dot_nn(spread_hi, jnp.concatenate([act_hi, act_lo], axis=1))
        rotated = wide[:, :2 * rank] + wide[:, 2 * rank:] + dot_nn(spread_lo, act_hi)
        start = step * batch
        for u in range(half):
            value = jnp.where(
                first_lanes,
                rotated[u * batch:(u + 1) * batch],
                rotated[(u + half) * batch:(u + half + 1) * batch],
            ) * inverse[u:u + 1]
            feat[u, pl.ds(start, batch)] = value

    each = steps // halves
    for index in range(halves + 1):
        beside = list(range(max(index - 1, 0) * each, index * each))
        if index < halves:
            project(index, beside)
        else:
            for step in beside:
                rotate(step)
    depth = half // slices
    me = lax.axis_index("mem") // cores
    for index in range(slices):
        start = (me ^ index) * depth
        piece = feat[pl.ds(start, depth)].astype(jnp.bfloat16)
        out_refs[index][pl.ds(0, depth * examples)] = piece.reshape(depth * examples, 2 * rank)
        out_refs[index][pl.ds(depth * examples, id_rows)] = digits


def features(slices, activations, out_grads, proj_in, proj_out, basis_in, basis_out, eigen, doc_ids):
    examples, tokens, width = activations.shape
    rank = proj_in.shape[1]
    rows = examples * tokens
    half = rank // 2
    hbm = pl.BlockSpec(memory_space=pl.ANY)
    vmem = pl.BlockSpec(memory_space=pltpu.VMEM)
    return pl.pallas_call(
        functools.partial(feature_kernel, tokens, slices),
        out_shape=[
            pltpu.VMEM((half // slices * examples + id_rows, 2 * rank), jnp.bfloat16)
        ] * slices,
        in_specs=[hbm] * 8,
        out_specs=[vmem] * slices,
        scratch_shapes=[
            pltpu.VMEM((rows, width), jnp.bfloat16),
            pltpu.VMEM((rows, width), jnp.bfloat16),
            pltpu.VMEM((rank, width), jnp.bfloat16),
            pltpu.VMEM((rank, width), jnp.bfloat16),
            pltpu.VMEM((rank, rank), jnp.float32),
            pltpu.VMEM((rank, rank), jnp.float32),
            pltpu.VMEM((rank, rank), jnp.float32),
            pltpu.VMEM((1, examples), jnp.int32),
            pltpu.VMEM((rows, rank), jnp.bfloat16),
            pltpu.VMEM((rank, rows), jnp.bfloat16),
            pltpu.VMEM((examples // batch, 2, rank, batch * tokens), jnp.float32),
            pltpu.VMEM((half, examples, 2 * rank), jnp.float32),
            pltpu.SemaphoreType.DMA((halves,)),
            pltpu.SemaphoreType.DMA((halves,)),
            pltpu.SemaphoreType.DMA((2,)),
            pltpu.SemaphoreType.DMA((4,)),
        ],
        compiler_params=pltpu.CompilerParams(vmem_limit_bytes=60 * 2**20),
        cost_estimate=pl.CostEstimate(
            flops=4 * rows * width * rank, bytes_accessed=4 * rows * width, transcendentals=0),
        name="features",
    )(
        activations.reshape(rows, width), out_grads.reshape(rows, width),
        proj_in.T, proj_out.T, basis_in, basis_out, eigen, doc_ids.reshape(1, examples),
    )


def slice_order(slices):
    return list(range(slices))


def product_kernel(slices, pieces, examples, row_groups, column_groups, *refs):
    runs = slices // pieces
    slabs = row_groups - 1 + 2 * column_groups
    ins, outs = refs[:runs * slabs], refs[runs * slabs:runs * slabs + slices]
    column_stack, row_stack, masked = refs[runs * slabs + slices:]
    piece_rows, lanes = ins[0].shape
    piece_rows = piece_rows // pieces
    depth = (piece_rows - id_rows) // examples
    mem = lax.axis_index("mem")
    pair, core = mem // cores, mem % cores

    def place(stack, digits, row, ref, piece):
        start = pl.multiple_of(row * examples, examples)
        for part in range(depth):
            stack[pl.ds(start, examples), pl.ds(part * lanes, lanes)] = (
                ref[pl.ds(piece * piece_rows + part * examples, examples)])
        some = ref[pl.ds((piece + 1) * piece_rows - id_rows, id_rows)].astype(jnp.float32)
        some = jnp.concatenate([some] * (digits.shape[1] // lanes), axis=1)
        block = lax.broadcasted_iota(jnp.int32, digits.shape, 1) // examples
        return jnp.where(block == row, some, digits)

    column_digits = jnp.zeros((id_rows, column_stack.shape[0]), jnp.float32)
    row_digits = jnp.zeros((id_rows, row_stack.shape[0]), jnp.float32)
    for run in range(runs):
        part = ins[run * slabs:(run + 1) * slabs]
        columns, others = part[:column_groups], part[column_groups:2 * column_groups]
        rows = (columns[0],) + tuple(part[2 * column_groups:])
        for piece in range(pieces):
            place_of = pair ^ slice_order(slices)[run * pieces + piece]
            for group in range(column_groups):
                for ref, side in ((columns[group], core), (others[group], core ^ 1)):
                    column = (group * slices + place_of) * cores + side
                    column_digits = place(column_stack, column_digits, column, ref, piece)
            for group in range(row_groups):
                row = place_of * row_groups + group
                row_digits = place(row_stack, row_digits, row, rows[group], piece)

    def halves(digits):
        return (digits[0:1] + digits[1:2] * 256.0, digits[2:3] + digits[3:4] * 256.0)

    column_low, column_high = halves(column_digits)
    row_low, row_high = halves(row_digits)
    result = dot_nt(row_stack[...], column_stack[...])
    for start in range(0, row_stack.shape[0], 128):
        low, high = (
            jnp.broadcast_to(row[:, start:start + 128], (128, 128)).T[:, 0:1] for row in (row_low, row_high))
        value = result[start:start + 128]
        value = jnp.where((low == column_low) & (high == column_high), 0.0, value)
        masked[pl.ds(start, 128)] = value.astype(jnp.bfloat16)
    count = row_groups * examples
    for index in range(slices):
        start = pl.multiple_of((pair ^ index) * count, count)
        outs[index][...] = masked[pl.ds(start, count)]


def products(slabs, slices, pieces, examples, row_groups, column_groups):
    piece_rows, lanes = slabs[0].shape
    depth = (piece_rows // pieces - id_rows) // examples
    vmem = pl.BlockSpec(memory_space=pltpu.VMEM)
    rows, cols = row_groups * slices * examples, column_groups * slices * cores * examples
    return pl.pallas_call(
        functools.partial(product_kernel, slices, pieces, examples, row_groups, column_groups),
        out_shape=[jax.ShapeDtypeStruct((row_groups * examples, cols), jnp.bfloat16)] * slices,
        in_specs=[vmem] * len(slabs),
        out_specs=[vmem] * slices,
        scratch_shapes=[
            pltpu.VMEM((cols, depth * lanes), jnp.bfloat16),
            pltpu.VMEM((rows, depth * lanes), jnp.bfloat16),
            pltpu.VMEM((rows, cols), jnp.bfloat16),
        ],
        compiler_params=pltpu.CompilerParams(vmem_limit_bytes=40 * 2**20),
        cost_estimate=pl.CostEstimate(
            flops=2 * rows * cols * depth * lanes, bytes_accessed=4 * rows * cols, transcendentals=0),
        name="products",
    )(*slabs)


def total_kernel(slices, *refs):
    parts, outs = refs[:slices], refs[slices:]
    examples = outs[0].shape[0]
    for group, out in enumerate(outs):
        rng = pl.ds(group * examples, examples)
        out[...] = sum(part[rng].astype(jnp.float32) for part in parts).astype(out.dtype)


def totals(parts, examples):
    rows, cols = parts[0].shape
    groups = rows // examples
    vmem = pl.BlockSpec(memory_space=pltpu.VMEM)
    return pl.pallas_call(
        functools.partial(total_kernel, len(parts)),
        out_shape=[
            jax.ShapeDtypeStruct((examples, cols), jnp.bfloat16 if group else jnp.float32)
            for group in range(groups)
        ],
        in_specs=[vmem] * len(parts),
        out_specs=[vmem] * groups,
        compiler_params=pltpu.CompilerParams(vmem_limit_bytes=40 * 2**20),
        cost_estimate=pl.CostEstimate(
            flops=rows * cols * len(parts), bytes_accessed=8 * rows * cols, transcendentals=0),
        name="totals",
    )(*parts)


def finish_kernel(factor, column_groups, *refs):
    parts, out_ref = refs[:-1], refs[-1]
    cols = parts[0].shape[1]
    width = cols // column_groups
    grp = lax.axis_index("grp")
    for row_step, part in enumerate(parts):
        value = part[...].astype(jnp.float32) * factor
        for column_step in range(column_groups):
            start = (grp ^ row_step ^ (column_step * len(parts))) * width
            out_ref[:, pl.ds(pl.multiple_of(start, width), width)] = (
                value[:, column_step * width:(column_step + 1) * width])


def finish(parts, column_groups, factor):
    examples, cols = parts[0].shape
    vmem = pl.BlockSpec(memory_space=pltpu.VMEM)
    return pl.pallas_call(
        functools.partial(finish_kernel, factor, column_groups),
        out_shape=jax.ShapeDtypeStruct((examples, len(parts) * cols), jnp.float32),
        in_specs=[vmem] * len(parts),
        out_specs=vmem,
        compiler_params=pltpu.CompilerParams(vmem_limit_bytes=40 * 2**20),
        cost_estimate=pl.CostEstimate(
            flops=8 * examples * cols, bytes_accessed=16 * examples * cols, transcendentals=0),
        name="finish",
    )(*parts)


def swap(value, axis, size, distance):
    if distance == 0:
        return value
    return lax.ppermute(value, axis, [(place, place ^ distance) for place in range(size)])


def on_device(members, groups, activations, out_grads, proj_in, proj_out, basis_in, basis_out, eigen, doc_ids):
    examples, tokens, width = activations.shape
    rank = proj_in.shape[1]
    factor = 1.0 / (tokens * rank)
    slices = members // cores
    runs = 2
    pieces = slices // runs
    row_groups = 1 << ((groups.bit_length() - 1) // 2)
    column_groups = groups // row_groups
    feat = features(slices, activations, out_grads, proj_in, proj_out, basis_in, basis_out, eigen, doc_ids)
    got = [swap(feat[index], "mem", members, cores * index) for index in slice_order(slices)]
    slabs = []
    for run in range(runs):
        slab = jnp.concatenate(got[run * pieces:(run + 1) * pieces], axis=0)
        if run:
            slab, slabs[column_groups] = lax.optimization_barrier((slab, slabs[column_groups]))
        columns = [swap(slab, "grp", groups, row_groups * step) for step in range(column_groups)]
        rows = [swap(slab, "grp", groups, step) for step in range(1, row_groups)]
        held = columns[1:]
        if run + 1 < runs:
            held = lax.optimization_barrier((*held, *rows))[:column_groups - 1]
        others = [swap(column, "mem", members, 1) for column in (slab, *held)]
        slabs += columns + others + rows
    partial = products(slabs, slices, pieces, examples, row_groups, column_groups)
    parts = [partial[0]] + [
        swap(partial[index], "mem", members, cores * index) for index in reversed(range(1, slices))]
    sums = totals(parts, examples)
    sums = [swap(value, "grp", groups, step) for step, value in enumerate(sums)]
    return finish(sums, column_groups, factor)


def solution(mesh):
    return jax.shard_map(
        functools.partial(on_device, mesh.shape["mem"], mesh.shape["grp"]),
        mesh=mesh,
        in_specs=(
            P(("grp", "mem"), None, None),
            P(("grp", "mem"), None, None),
            P(),
            P(),
            P(),
            P(),
            P(),
            P(("grp", "mem")),
        ),
        out_specs=P(("grp", "mem"), None),
        check_vma=False,
    )
```

```python
import functools
import jax
import jax.numpy as jnp
from jax import lax
from jax.experimental import pallas as pl
from jax.experimental.pallas import tpu as pltpu
from jax.sharding import PartitionSpec as P

damping = 0.1
halves = 2
batch = 8
id_rows = 16
cores = 2


def dot_nn(a, b):
    return lax.dot_general(a, b, (((1,), (0,)), ((), ())), preferred_element_type=jnp.float32)


def dot_nt(a, b):
    return lax.dot_general(a, b, (((1,), (1,)), ((), ())), preferred_element_type=jnp.float32)


def split_two(value):
    high = value.astype(jnp.bfloat16)
    low = (value - high.astype(jnp.float32)).astype(jnp.bfloat16)
    return high, low


def feature_kernel(
    tokens, slices, act_hbm, grad_hbm, pin_hbm, pout_hbm, bin_hbm, bout_hbm, eigen_hbm, ids_hbm, *refs
):
    out_refs = refs[:slices]
    (act, grad, pin, pout, bin_ref, bout_ref, eigen_ref, ids_ref, act_proj, grad_proj, gt_ref, feat,
     act_sem, grad_sem, w_sem, s_sem) = refs[slices:]
    rows, width = act.shape
    rank = bin_ref.shape[0]
    half = rank // 2
    step_rows = batch * tokens
    steps = rows // step_rows
    examples = feat.shape[1]

    half_rows = rows // halves

    def half_copies(index):
        rng = pl.ds(index * half_rows, half_rows)
        return (
            pltpu.make_async_copy(act_hbm.at[rng], act.at[rng], act_sem.at[index]),
            pltpu.make_async_copy(grad_hbm.at[rng], grad.at[rng], grad_sem.at[index]),
        )

    weights = [
        pltpu.make_async_copy(pin_hbm, pin, w_sem.at[0]),
        pltpu.make_async_copy(pout_hbm, pout, w_sem.at[1]),
    ]
    def start_half(index):
        for priority, copy in enumerate(half_copies(index)):
            copy.start(priority=priority)

    small = [
        pltpu.make_async_copy(source, target, s_sem.at[index])
        for index, (source, target) in enumerate((
            (bin_hbm, bin_ref), (bout_hbm, bout_ref), (eigen_hbm, eigen_ref), (ids_hbm, ids_ref)))
    ]
    for priority, copy in enumerate(weights):
        copy.start(priority=priority)
    start_half(0)
    for copy in small:
        copy.start()
    for index in range(1, halves):
        start_half(index)
    for copy in small:
        copy.wait()

    bin_hi, bin_lo = split_two(jnp.concatenate([bin_ref[...], bin_ref[...]], axis=1))
    bout_hi, bout_lo = split_two(bout_ref[...].T)
    inverse = 1.0 / jnp.sqrt(eigen_ref[...] + damping)
    inverse = jnp.concatenate([inverse[:half], inverse[half:]], axis=1)
    own_token = (
        lax.broadcasted_iota(jnp.int32, (batch, step_rows), 1) // tokens
        == lax.broadcasted_iota(jnp.int32, (batch, step_rows), 0)
    )
    first_lanes = lax.broadcasted_iota(jnp.int32, (batch, 2 * rank), 1) < rank
    ids = jnp.concatenate([ids_ref[...]] * (2 * rank // examples), axis=1)
    place = lax.broadcasted_iota(jnp.int32, (id_rows, 2 * rank), 0) % 4
    digits = (jnp.broadcast_to(ids, (id_rows, 2 * rank)) >> (place * 8)) & 255
    digits = digits.astype(jnp.float32).astype(jnp.bfloat16)
    for copy in weights:
        copy.wait()

    def project(index, beside):
        rng = pl.ds(index * half_rows, half_rows)
        act_copy, grad_copy = half_copies(index)
        act_copy.wait()
        act_part = dot_nt(pin[...], act[rng]).T.astype(jnp.bfloat16)
        act_hi, act_lo = split_two(dot_nn(act_part, bin_hi) + dot_nn(act_part, bin_lo))
        act_proj[rng] = jnp.concatenate([act_hi, act_lo], axis=1)
        for step in beside[0::2]:
            rotate(step)
        grad_copy.wait()
        grad_proj[:, rng] = dot_nt(pout[...], grad[rng]).astype(jnp.bfloat16)
        for step in beside[1::2]:
            rotate(step)

    def rotate(step):
        rng = pl.ds(step * step_rows, step_rows)
        act_part, grad_part = act_proj[rng], grad_proj[:, rng]
        grad_hi, grad_lo = split_two(dot_nn(bout_hi, grad_part) + dot_nn(bout_lo, grad_part))
        gt_ref[step, 0] = grad_hi.astype(jnp.float32)
        gt_ref[step, 1] = grad_lo.astype(jnp.float32)
        spread_hi, spread_lo = [
            jnp.concatenate([
                jnp.where(own_token, jnp.broadcast_to(gt_ref[step, part, pl.ds(u, 1)], (batch, step_rows)), 0.0)
                for u in range(rank)
            ], axis=0).astype(jnp.bfloat16)
            for part in range(2)
        ]
        wide = dot_nn(spread_hi, act_part)
        rotated = wide[:, :2 * rank] + wide[:, 2 * rank:] + dot_nn(spread_lo, act_part[:, :2 * rank])
        start = step * batch
        for u in range(half):
            value = jnp.where(
                first_lanes,
                rotated[u * batch:(u + 1) * batch],
                rotated[(u + half) * batch:(u + half + 1) * batch],
            ) * inverse[u:u + 1]
            feat[u, pl.ds(start, batch)] = value

    each = steps // halves
    for index in range(halves + 1):
        beside = list(range(max(index - 1, 0) * each, index * each))
        if index < halves:
            project(index, beside)
        else:
            for step in beside:
                rotate(step)
    depth = half // slices
    me = lax.axis_index("mem") // cores
    for index in range(slices):
        start = (me ^ index) * depth
        piece = feat[pl.ds(start, depth)].astype(jnp.bfloat16)
        out_refs[index][pl.ds(0, depth * examples)] = piece.reshape(depth * examples, 2 * rank)
        out_refs[index][pl.ds(depth * examples, id_rows)] = digits


def features(slices, activations, out_grads, proj_in, proj_out, basis_in, basis_out, eigen, doc_ids):
    examples, tokens, width = activations.shape
    rank = proj_in.shape[1]
    rows = examples * tokens
    half = rank // 2
    hbm = pl.BlockSpec(memory_space=pl.ANY)
    vmem = pl.BlockSpec(memory_space=pltpu.VMEM)
    return pl.pallas_call(
        functools.partial(feature_kernel, tokens, slices),
        out_shape=[
            pltpu.VMEM((half // slices * examples + id_rows, 2 * rank), jnp.bfloat16)
        ] * slices,
        in_specs=[hbm] * 8,
        out_specs=[vmem] * slices,
        scratch_shapes=[
            pltpu.VMEM((rows, width), jnp.bfloat16),
            pltpu.VMEM((rows, width), jnp.bfloat16),
            pltpu.VMEM((rank, width), jnp.bfloat16),
            pltpu.VMEM((rank, width), jnp.bfloat16),
            pltpu.VMEM((rank, rank), jnp.float32),
            pltpu.VMEM((rank, rank), jnp.float32),
            pltpu.VMEM((rank, rank), jnp.float32),
            pltpu.VMEM((1, examples), jnp.int32),
            pltpu.VMEM((rows, 4 * rank), jnp.bfloat16),
            pltpu.VMEM((rank, rows), jnp.bfloat16),
            pltpu.VMEM((examples // batch, 2, rank, batch * tokens), jnp.float32),
            pltpu.VMEM((half, examples, 2 * rank), jnp.float32),
            pltpu.SemaphoreType.DMA((halves,)),
            pltpu.SemaphoreType.DMA((halves,)),
            pltpu.SemaphoreType.DMA((2,)),
            pltpu.SemaphoreType.DMA((4,)),
        ],
        compiler_params=pltpu.CompilerParams(vmem_limit_bytes=60 * 2**20),
        cost_estimate=pl.CostEstimate(
            flops=4 * rows * width * rank, bytes_accessed=4 * rows * width, transcendentals=0),
        name="features",
    )(
        activations.reshape(rows, width), out_grads.reshape(rows, width),
        proj_in.T, proj_out.T, basis_in, basis_out, eigen, doc_ids.reshape(1, examples),
    )


def slice_order(slices):
    return list(range(slices))


def product_kernel(slices, pieces, examples, row_groups, column_groups, *refs):
    runs = slices // pieces
    slabs = row_groups - 1 + 2 * column_groups
    ins, outs = refs[:runs * slabs], refs[runs * slabs:runs * slabs + slices]
    column_stack, row_stack, masked = refs[runs * slabs + slices:]
    piece_rows, lanes = ins[0].shape
    piece_rows = piece_rows // pieces
    depth = (piece_rows - id_rows) // examples
    mem = lax.axis_index("mem")
    pair, core = mem // cores, mem % cores

    def place(stack, digits, row, ref, piece):
        start = pl.multiple_of(row * examples, examples)
        for part in range(depth):
            stack[pl.ds(start, examples), pl.ds(part * lanes, lanes)] = (
                ref[pl.ds(piece * piece_rows + part * examples, examples)])
        some = ref[pl.ds((piece + 1) * piece_rows - id_rows, id_rows)].astype(jnp.float32)
        some = jnp.concatenate([some] * (digits.shape[1] // lanes), axis=1)
        block = lax.broadcasted_iota(jnp.int32, digits.shape, 1) // examples
        return jnp.where(block == row, some, digits)

    column_digits = jnp.zeros((id_rows, column_stack.shape[0]), jnp.float32)
    row_digits = jnp.zeros((id_rows, row_stack.shape[0]), jnp.float32)
    for run in range(runs):
        part = ins[run * slabs:(run + 1) * slabs]
        columns, others = part[:column_groups], part[column_groups:2 * column_groups]
        rows = (columns[0],) + tuple(part[2 * column_groups:])
        for piece in range(pieces):
            place_of = pair ^ slice_order(slices)[run * pieces + piece]
            for group in range(column_groups):
                for ref, side in ((columns[group], core), (others[group], core ^ 1)):
                    column = (group * slices + place_of) * cores + side
                    column_digits = place(column_stack, column_digits, column, ref, piece)
            for group in range(row_groups):
                row = place_of * row_groups + group
                row_digits = place(row_stack, row_digits, row, rows[group], piece)

    def halves(digits):
        return (digits[0:1] + digits[1:2] * 256.0, digits[2:3] + digits[3:4] * 256.0)

    column_low, column_high = halves(column_digits)
    row_low, row_high = halves(row_digits)
    result = dot_nt(row_stack[...], column_stack[...])
    for start in range(0, row_stack.shape[0], 128):
        low, high = (
            jnp.broadcast_to(row[:, start:start + 128], (128, 128)).T[:, 0:1] for row in (row_low, row_high))
        value = result[start:start + 128]
        value = jnp.where((low == column_low) & (high == column_high), 0.0, value)
        masked[pl.ds(start, 128)] = value.astype(jnp.bfloat16)
    count = row_groups * examples
    for index in range(slices):
        start = pl.multiple_of((pair ^ index) * count, count)
        outs[index][...] = masked[pl.ds(start, count)]


def products(slabs, slices, pieces, examples, row_groups, column_groups):
    piece_rows, lanes = slabs[0].shape
    depth = (piece_rows // pieces - id_rows) // examples
    vmem = pl.BlockSpec(memory_space=pltpu.VMEM)
    rows, cols = row_groups * slices * examples, column_groups * slices * cores * examples
    return pl.pallas_call(
        functools.partial(product_kernel, slices, pieces, examples, row_groups, column_groups),
        out_shape=[jax.ShapeDtypeStruct((row_groups * examples, cols), jnp.bfloat16)] * slices,
        in_specs=[vmem] * len(slabs),
        out_specs=[vmem] * slices,
        scratch_shapes=[
            pltpu.VMEM((cols, depth * lanes), jnp.bfloat16),
            pltpu.VMEM((rows, depth * lanes), jnp.bfloat16),
            pltpu.VMEM((rows, cols), jnp.bfloat16),
        ],
        compiler_params=pltpu.CompilerParams(vmem_limit_bytes=40 * 2**20),
        cost_estimate=pl.CostEstimate(
            flops=2 * rows * cols * depth * lanes, bytes_accessed=4 * rows * cols, transcendentals=0),
        name="products",
    )(*slabs)


def total_kernel(slices, *refs):
    parts, outs = refs[:slices], refs[slices:]
    examples = outs[0].shape[0]
    for group, out in enumerate(outs):
        rng = pl.ds(group * examples, examples)
        out[...] = sum(part[rng].astype(jnp.float32) for part in parts).astype(out.dtype)


def totals(parts, examples):
    rows, cols = parts[0].shape
    groups = rows // examples
    vmem = pl.BlockSpec(memory_space=pltpu.VMEM)
    return pl.pallas_call(
        functools.partial(total_kernel, len(parts)),
        out_shape=[
            jax.ShapeDtypeStruct((examples, cols), jnp.bfloat16 if group else jnp.float32)
            for group in range(groups)
        ],
        in_specs=[vmem] * len(parts),
        out_specs=[vmem] * groups,
        compiler_params=pltpu.CompilerParams(vmem_limit_bytes=40 * 2**20),
        cost_estimate=pl.CostEstimate(
            flops=rows * cols * len(parts), bytes_accessed=8 * rows * cols, transcendentals=0),
        name="totals",
    )(*parts)


def finish_kernel(factor, column_groups, *refs):
    parts, out_ref = refs[:-1], refs[-1]
    cols = parts[0].shape[1]
    width = cols // column_groups
    grp = lax.axis_index("grp")
    for row_step, part in enumerate(parts):
        value = part[...].astype(jnp.float32) * factor
        for column_step in range(column_groups):
            start = (grp ^ row_step ^ (column_step * len(parts))) * width
            out_ref[:, pl.ds(pl.multiple_of(start, width), width)] = (
                value[:, column_step * width:(column_step + 1) * width])


def finish(parts, column_groups, factor):
    examples, cols = parts[0].shape
    vmem = pl.BlockSpec(memory_space=pltpu.VMEM)
    return pl.pallas_call(
        functools.partial(finish_kernel, factor, column_groups),
        out_shape=jax.ShapeDtypeStruct((examples, len(parts) * cols), jnp.float32),
        in_specs=[vmem] * len(parts),
        out_specs=vmem,
        compiler_params=pltpu.CompilerParams(vmem_limit_bytes=40 * 2**20),
        cost_estimate=pl.CostEstimate(
            flops=8 * examples * cols, bytes_accessed=16 * examples * cols, transcendentals=0),
        name="finish",
    )(*parts)


def swap(value, axis, size, distance):
    if distance == 0:
        return value
    return lax.ppermute(value, axis, [(place, place ^ distance) for place in range(size)])


def on_device(members, groups, activations, out_grads, proj_in, proj_out, basis_in, basis_out, eigen, doc_ids):
    examples, tokens, width = activations.shape
    rank = proj_in.shape[1]
    factor = 1.0 / (tokens * rank)
    slices = members // cores
    runs = 2
    pieces = slices // runs
    row_groups = 1 << ((groups.bit_length() - 1) // 2)
    column_groups = groups // row_groups
    feat = features(slices, activations, out_grads, proj_in, proj_out, basis_in, basis_out, eigen, doc_ids)
    got = [swap(feat[index], "mem", members, cores * index) for index in slice_order(slices)]
    slabs = []
    for run in range(runs):
        slab = jnp.concatenate(got[run * pieces:(run + 1) * pieces], axis=0)
        if run:
            slab, slabs[column_groups] = lax.optimization_barrier((slab, slabs[column_groups]))
        columns = [swap(slab, "grp", groups, row_groups * step) for step in range(column_groups)]
        rows = [swap(slab, "grp", groups, step) for step in range(1, row_groups)]
        held = columns[1:]
        if run + 1 < runs:
            held = lax.optimization_barrier((*held, *rows))[:column_groups - 1]
        others = [swap(column, "mem", members, 1) for column in (slab, *held)]
        slabs += columns + others + rows
    partial = products(slabs, slices, pieces, examples, row_groups, column_groups)
    parts = [partial[0]] + [
        swap(partial[index], "mem", members, cores * index) for index in reversed(range(1, slices))]
    sums = totals(parts, examples)
    sums = [swap(value, "grp", groups, step) for step, value in enumerate(sums)]
    return finish(sums, column_groups, factor)


def solution(mesh):
    return jax.shard_map(
        functools.partial(on_device, mesh.shape["mem"], mesh.shape["grp"]),
        mesh=mesh,
        in_specs=(
            P(("grp", "mem"), None, None),
            P(("grp", "mem"), None, None),
            P(),
            P(),
            P(),
            P(),
            P(),
            P(("grp", "mem")),
        ),
        out_specs=P(("grp", "mem"), None),
        check_vma=False,
    )
```

```python
import functools
import jax
import jax.numpy as jnp
from jax import lax
from jax.experimental import pallas as pl
from jax.experimental.pallas import tpu as pltpu
from jax.sharding import PartitionSpec as P

damping = 0.1
halves = 2
batch = 8
id_rows = 16
cores = 2


def dot_nn(a, b):
    return lax.dot_general(a, b, (((1,), (0,)), ((), ())), preferred_element_type=jnp.float32)


def dot_nt(a, b):
    return lax.dot_general(a, b, (((1,), (1,)), ((), ())), preferred_element_type=jnp.float32)


def split_two(value):
    high = value.astype(jnp.bfloat16)
    low = (value - high.astype(jnp.float32)).astype(jnp.bfloat16)
    return high, low


def feature_kernel(
    tokens, slices, act_hbm, grad_hbm, pin_hbm, pout_hbm, bin_hbm, bout_hbm, eigen_hbm, ids_hbm, *refs
):
    out_refs = refs[:slices]
    (act, grad, pin, pout, bin_ref, bout_ref, eigen_ref, ids_ref, act_proj, grad_proj, gt_ref, feat,
     act_sem, grad_sem, w_sem, s_sem) = refs[slices:]
    rows, width = act.shape
    rank = bin_ref.shape[0]
    half = rank // 2
    step_rows = batch * tokens
    steps = rows // step_rows
    examples = feat.shape[1]

    half_rows = rows // halves

    def half_copies(index):
        rng = pl.ds(index * half_rows, half_rows)
        return (
            pltpu.make_async_copy(act_hbm.at[rng], act.at[rng], act_sem.at[index]),
            pltpu.make_async_copy(grad_hbm.at[rng], grad.at[rng], grad_sem.at[index]),
        )

    weights = [
        pltpu.make_async_copy(pin_hbm, pin, w_sem.at[0]),
        pltpu.make_async_copy(pout_hbm, pout, w_sem.at[1]),
    ]
    def start_half(index):
        for priority, copy in enumerate(half_copies(index)):
            copy.start(priority=priority)

    small = [
        pltpu.make_async_copy(source, target, s_sem.at[index])
        for index, (source, target) in enumerate((
            (bin_hbm, bin_ref), (bout_hbm, bout_ref), (eigen_hbm, eigen_ref), (ids_hbm, ids_ref)))
    ]
    for copy in weights:
        copy.start()
    start_half(0)
    for copy in small:
        copy.start()
    for index in range(1, halves):
        start_half(index)
    for copy in small:
        copy.wait()

    bin_hi, bin_lo = split_two(jnp.concatenate([bin_ref[...], bin_ref[...]], axis=1))
    bout_hi, bout_lo = split_two(bout_ref[...].T)
    inverse = 1.0 / jnp.sqrt(eigen_ref[...] + damping)
    inverse = jnp.concatenate([inverse[:half], inverse[half:]], axis=1)
    own_token = (
        lax.broadcasted_iota(jnp.int32, (batch, step_rows), 1) // tokens
        == lax.broadcasted_iota(jnp.int32, (batch, step_rows), 0)
    )
    first_lanes = lax.broadcasted_iota(jnp.int32, (batch, 2 * rank), 1) < rank
    ids = jnp.concatenate([ids_ref[...]] * (2 * rank // examples), axis=1)
    place = lax.broadcasted_iota(jnp.int32, (id_rows, 2 * rank), 0) % 4
    digits = (jnp.broadcast_to(ids, (id_rows, 2 * rank)) >> (place * 8)) & 255
    digits = digits.astype(jnp.float32).astype(jnp.bfloat16)
    for copy in weights:
        copy.wait()

    def project(index, beside):
        rng = pl.ds(index * half_rows, half_rows)
        act_copy, grad_copy = half_copies(index)
        act_copy.wait()
        act_proj[rng] = dot_nt(pin[...], act[rng]).T.astype(jnp.bfloat16)
        for step in beside[0::2]:
            rotate(step)
        grad_copy.wait()
        grad_proj[:, rng] = dot_nt(pout[...], grad[rng]).astype(jnp.bfloat16)
        for step in beside[1::2]:
            rotate(step)

    def rotate(step):
        rng = pl.ds(step * step_rows, step_rows)
        act_part, grad_part = act_proj[rng], grad_proj[:, rng]
        act_hi, act_lo = split_two(dot_nn(act_part, bin_hi) + dot_nn(act_part, bin_lo))
        grad_hi, grad_lo = split_two(dot_nn(bout_hi, grad_part) + dot_nn(bout_lo, grad_part))
        gt_ref[step, 0] = grad_hi.astype(jnp.float32)
        gt_ref[step, 1] = grad_lo.astype(jnp.float32)
        spread_hi, spread_lo = [
            jnp.concatenate([
                jnp.where(own_token, jnp.broadcast_to(gt_ref[step, part, pl.ds(u, 1)], (batch, step_rows)), 0.0)
                for u in range(rank)
            ], axis=0).astype(jnp.bfloat16)
            for part in range(2)
        ]
        wide = dot_nn(spread_hi, jnp.concatenate([act_hi, act_lo], axis=1))
        rotated = wide[:, :2 * rank] + wide[:, 2 * rank:] + dot_nn(spread_lo, act_hi)
        start = step * batch
        for u in range(half):
            value = jnp.where(
                first_lanes,
                rotated[u * batch:(u + 1) * batch],
                rotated[(u + half) * batch:(u + half + 1) * batch],
            ) * inverse[u:u + 1]
            feat[u, pl.ds(start, batch)] = value

    each = steps // halves
    for index in range(halves + 1):
        beside = list(range(max(index - 1, 0) * each, index * each))
        if index < halves:
            project(index, beside)
        else:
            for step in beside:
                rotate(step)
    depth = half // slices
    me = lax.axis_index("mem") // cores
    for index in range(slices):
        start = (me ^ index) * depth
        piece = feat[pl.ds(start, depth)].astype(jnp.bfloat16)
        out_refs[index][pl.ds(0, depth * examples)] = piece.reshape(depth * examples, 2 * rank)
        out_refs[index][pl.ds(depth * examples, id_rows)] = digits


def features(slices, activations, out_grads, proj_in, proj_out, basis_in, basis_out, eigen, doc_ids):
    examples, tokens, width = activations.shape
    rank = proj_in.shape[1]
    rows = examples * tokens
    half = rank // 2
    hbm = pl.BlockSpec(memory_space=pl.ANY)
    vmem = pl.BlockSpec(memory_space=pltpu.VMEM)
    return pl.pallas_call(
        functools.partial(feature_kernel, tokens, slices),
        out_shape=[
            pltpu.VMEM((half // slices * examples + id_rows, 2 * rank), jnp.bfloat16)
        ] * slices,
        in_specs=[hbm] * 8,
        out_specs=[vmem] * slices,
        scratch_shapes=[
            pltpu.VMEM((rows, width), jnp.bfloat16),
            pltpu.VMEM((rows, width), jnp.bfloat16),
            pltpu.VMEM((rank, width), jnp.bfloat16),
            pltpu.VMEM((rank, width), jnp.bfloat16),
            pltpu.VMEM((rank, rank), jnp.float32),
            pltpu.VMEM((rank, rank), jnp.float32),
            pltpu.VMEM((rank, rank), jnp.float32),
            pltpu.VMEM((1, examples), jnp.int32),
            pltpu.VMEM((rows, rank), jnp.bfloat16),
            pltpu.VMEM((rank, rows), jnp.bfloat16),
            pltpu.VMEM((examples // batch, 2, rank, batch * tokens), jnp.float32),
            pltpu.VMEM((half, examples, 2 * rank), jnp.float32),
            pltpu.SemaphoreType.DMA((halves,)),
            pltpu.SemaphoreType.DMA((halves,)),
            pltpu.SemaphoreType.DMA((2,)),
            pltpu.SemaphoreType.DMA((4,)),
        ],
        compiler_params=pltpu.CompilerParams(vmem_limit_bytes=60 * 2**20),
        cost_estimate=pl.CostEstimate(
            flops=4 * rows * width * rank, bytes_accessed=4 * rows * width, transcendentals=0),
        name="features",
    )(
        activations.reshape(rows, width), out_grads.reshape(rows, width),
        proj_in.T, proj_out.T, basis_in, basis_out, eigen, doc_ids.reshape(1, examples),
    )


def slice_order(slices):
    return list(range(slices))


def product_kernel(slices, pieces, examples, row_groups, column_groups, *refs):
    runs = slices // pieces
    slabs = row_groups - 1 + 2 * column_groups
    ins, outs = refs[:runs * slabs], refs[runs * slabs:runs * slabs + slices]
    column_stack, row_stack, masked = refs[runs * slabs + slices:]
    piece_rows, lanes = ins[0].shape
    piece_rows = piece_rows // pieces
    depth = (piece_rows - id_rows) // examples
    mem = lax.axis_index("mem")
    pair, core = mem // cores, mem % cores

    def place(stack, digits, row, ref, piece):
        start = pl.multiple_of(row * examples, examples)
        for part in range(depth):
            stack[pl.ds(start, examples), pl.ds(part * lanes, lanes)] = (
                ref[pl.ds(piece * piece_rows + part * examples, examples)])
        some = ref[pl.ds((piece + 1) * piece_rows - id_rows, id_rows)].astype(jnp.float32)
        some = jnp.concatenate([some] * (digits.shape[1] // lanes), axis=1)
        block = lax.broadcasted_iota(jnp.int32, digits.shape, 1) // examples
        return jnp.where(block == row, some, digits)

    column_digits = jnp.zeros((id_rows, column_stack.shape[0]), jnp.float32)
    row_digits = jnp.zeros((id_rows, row_stack.shape[0]), jnp.float32)
    for run in range(runs):
        part = ins[run * slabs:(run + 1) * slabs]
        columns, others = part[:column_groups], part[column_groups:2 * column_groups]
        rows = (columns[0],) + tuple(part[2 * column_groups:])
        for piece in range(pieces):
            place_of = pair ^ slice_order(slices)[run * pieces + piece]
            for group in range(column_groups):
                for ref, side in ((columns[group], core), (others[group], core ^ 1)):
                    column = (group * slices + place_of) * cores + side
                    column_digits = place(column_stack, column_digits, column, ref, piece)
            for group in range(row_groups):
                row = place_of * row_groups + group
                row_digits = place(row_stack, row_digits, row, rows[group], piece)

    def halves(digits):
        return (digits[0:1] + digits[1:2] * 256.0, digits[2:3] + digits[3:4] * 256.0)

    column_low, column_high = halves(column_digits)
    row_low, row_high = halves(row_digits)
    result = dot_nt(row_stack[...], column_stack[...])
    for start in range(0, row_stack.shape[0], 128):
        low, high = (
            jnp.broadcast_to(row[:, start:start + 128], (128, 128)).T[:, 0:1] for row in (row_low, row_high))
        value = result[start:start + 128]
        value = jnp.where((low == column_low) & (high == column_high), 0.0, value)
        masked[pl.ds(start, 128)] = value.astype(jnp.bfloat16)
    count = row_groups * examples
    for index in range(slices):
        start = pl.multiple_of((pair ^ index) * count, count)
        outs[index][...] = masked[pl.ds(start, count)]


def products(slabs, slices, pieces, examples, row_groups, column_groups):
    piece_rows, lanes = slabs[0].shape
    depth = (piece_rows // pieces - id_rows) // examples
    vmem = pl.BlockSpec(memory_space=pltpu.VMEM)
    rows, cols = row_groups * slices * examples, column_groups * slices * cores * examples
    return pl.pallas_call(
        functools.partial(product_kernel, slices, pieces, examples, row_groups, column_groups),
        out_shape=[jax.ShapeDtypeStruct((row_groups * examples, cols), jnp.bfloat16)] * slices,
        in_specs=[vmem] * len(slabs),
        out_specs=[vmem] * slices,
        scratch_shapes=[
            pltpu.VMEM((cols, depth * lanes), jnp.bfloat16),
            pltpu.VMEM((rows, depth * lanes), jnp.bfloat16),
            pltpu.VMEM((rows, cols), jnp.bfloat16),
        ],
        compiler_params=pltpu.CompilerParams(vmem_limit_bytes=40 * 2**20),
        cost_estimate=pl.CostEstimate(
            flops=2 * rows * cols * depth * lanes, bytes_accessed=4 * rows * cols, transcendentals=0),
        name="products",
    )(*slabs)


def total_kernel(slices, *refs):
    parts, outs = refs[:slices], refs[slices:]
    examples = outs[0].shape[0]
    for group, out in enumerate(outs):
        rng = pl.ds(group * examples, examples)
        out[...] = sum(part[rng].astype(jnp.float32) for part in parts).astype(out.dtype)


def totals(parts, examples):
    rows, cols = parts[0].shape
    groups = rows // examples
    vmem = pl.BlockSpec(memory_space=pltpu.VMEM)
    return pl.pallas_call(
        functools.partial(total_kernel, len(parts)),
        out_shape=[
            jax.ShapeDtypeStruct((examples, cols), jnp.bfloat16 if group else jnp.float32)
            for group in range(groups)
        ],
        in_specs=[vmem] * len(parts),
        out_specs=[vmem] * groups,
        compiler_params=pltpu.CompilerParams(vmem_limit_bytes=40 * 2**20),
        cost_estimate=pl.CostEstimate(
            flops=rows * cols * len(parts), bytes_accessed=8 * rows * cols, transcendentals=0),
        name="totals",
    )(*parts)


def finish_kernel(factor, column_groups, *refs):
    parts, out_ref = refs[:-1], refs[-1]
    cols = parts[0].shape[1]
    width = cols // column_groups
    grp = lax.axis_index("grp")
    for row_step, part in enumerate(parts):
        value = part[...].astype(jnp.float32) * factor
        for column_step in range(column_groups):
            start = (grp ^ row_step ^ (column_step * len(parts))) * width
            out_ref[:, pl.ds(pl.multiple_of(start, width), width)] = (
                value[:, column_step * width:(column_step + 1) * width])


def finish(parts, column_groups, factor):
    examples, cols = parts[0].shape
    vmem = pl.BlockSpec(memory_space=pltpu.VMEM)
    return pl.pallas_call(
        functools.partial(finish_kernel, factor, column_groups),
        out_shape=jax.ShapeDtypeStruct((examples, len(parts) * cols), jnp.float32),
        in_specs=[vmem] * len(parts),
        out_specs=vmem,
        compiler_params=pltpu.CompilerParams(vmem_limit_bytes=40 * 2**20),
        cost_estimate=pl.CostEstimate(
            flops=8 * examples * cols, bytes_accessed=16 * examples * cols, transcendentals=0),
        name="finish",
    )(*parts)


def swap(value, axis, size, distance):
    if distance == 0:
        return value
    return lax.ppermute(value, axis, [(place, place ^ distance) for place in range(size)])


def on_device(members, groups, activations, out_grads, proj_in, proj_out, basis_in, basis_out, eigen, doc_ids):
    examples, tokens, width = activations.shape
    rank = proj_in.shape[1]
    factor = 1.0 / (tokens * rank)
    slices = members // cores
    runs = 2
    pieces = slices // runs
    row_groups = 1 << ((groups.bit_length() - 1) // 2)
    column_groups = groups // row_groups
    feat = features(slices, activations, out_grads, proj_in, proj_out, basis_in, basis_out, eigen, doc_ids)
    got = [swap(feat[index], "mem", members, cores * index) for index in slice_order(slices)]
    slabs = []
    for run in range(runs):
        slab = jnp.concatenate(got[run * pieces:(run + 1) * pieces], axis=0)
        if run:
            slab, slabs[column_groups] = lax.optimization_barrier((slab, slabs[column_groups]))
        columns = [swap(slab, "grp", groups, row_groups * step) for step in range(column_groups)]
        rows = [swap(slab, "grp", groups, step) for step in range(1, row_groups)]
        held = columns[1:]
        if run + 1 < runs:
            held = lax.optimization_barrier((*held, *rows))[:column_groups - 1]
        others = [swap(column, "mem", members, 1) for column in (slab, *held)]
        slabs += columns + others + rows
    partial = products(slabs, slices, pieces, examples, row_groups, column_groups)
    parts = [partial[0]] + [
        swap(partial[index], "mem", members, cores * index)
        for index in (*range(slices // 2, slices), *reversed(range(1, slices // 2)))]
    sums = totals(parts, examples)
    sums = [swap(value, "grp", groups, step) for step, value in enumerate(sums)]
    return finish(sums, column_groups, factor)


def solution(mesh):
    return jax.shard_map(
        functools.partial(on_device, mesh.shape["mem"], mesh.shape["grp"]),
        mesh=mesh,
        in_specs=(
            P(("grp", "mem"), None, None),
            P(("grp", "mem"), None, None),
            P(),
            P(),
            P(),
            P(),
            P(),
            P(("grp", "mem")),
        ),
        out_specs=P(("grp", "mem"), None),
        check_vma=False,
    )
```

```python
import functools
import jax
import jax.numpy as jnp
from jax import lax
from jax.experimental import pallas as pl
from jax.experimental.pallas import tpu as pltpu
from jax.sharding import PartitionSpec as P

damping = 0.1
halves = 2
batch = 8
id_rows = 16
cores = 2


def dot_nn(a, b):
    return lax.dot_general(a, b, (((1,), (0,)), ((), ())), preferred_element_type=jnp.float32)


def dot_nt(a, b):
    return lax.dot_general(a, b, (((1,), (1,)), ((), ())), preferred_element_type=jnp.float32)


def split_two(value):
    high = value.astype(jnp.bfloat16)
    low = (value - high.astype(jnp.float32)).astype(jnp.bfloat16)
    return high, low


def feature_kernel(
    tokens, slices, act_hbm, grad_hbm, pin_hbm, pout_hbm, bin_hbm, bout_hbm, eigen_hbm, ids_hbm, *refs
):
    out_refs = refs[:slices]
    (act, grad, pin, pout, bin_ref, bout_ref, eigen_ref, ids_ref, act_proj, grad_proj, gt_ref, feat,
     act_sem, grad_sem, w_sem, s_sem) = refs[slices:]
    rows, width = act.shape
    rank = bin_ref.shape[0]
    half = rank // 2
    step_rows = batch * tokens
    steps = rows // step_rows
    examples = feat.shape[1]

    half_rows = rows // halves

    def half_copies(index):
        rng = pl.ds(index * half_rows, half_rows)
        return (
            pltpu.make_async_copy(act_hbm.at[rng], act.at[rng], act_sem.at[index]),
            pltpu.make_async_copy(grad_hbm.at[rng], grad.at[rng], grad_sem.at[index]),
        )

    weights = [
        pltpu.make_async_copy(pin_hbm, pin, w_sem.at[0]),
        pltpu.make_async_copy(pout_hbm, pout, w_sem.at[1]),
    ]
    def start_half(index):
        for priority, copy in enumerate(half_copies(index)):
            copy.start(priority=priority)

    small = [
        pltpu.make_async_copy(source, target, s_sem.at[index])
        for index, (source, target) in enumerate((
            (bin_hbm, bin_ref), (bout_hbm, bout_ref), (eigen_hbm, eigen_ref), (ids_hbm, ids_ref)))
    ]
    weights[0].start()
    half_copies(0)[0].start(priority=0)
    weights[1].start()
    half_copies(0)[1].start(priority=1)
    for copy in small:
        copy.start()
    for index in range(1, halves):
        start_half(index)
    for copy in small:
        copy.wait()

    bin_hi, bin_lo = split_two(jnp.concatenate([bin_ref[...], bin_ref[...]], axis=1))
    bout_hi, bout_lo = split_two(bout_ref[...].T)
    inverse = 1.0 / jnp.sqrt(eigen_ref[...] + damping)
    inverse = jnp.concatenate([inverse[:half], inverse[half:]], axis=1)
    own_token = (
        lax.broadcasted_iota(jnp.int32, (batch, step_rows), 1) // tokens
        == lax.broadcasted_iota(jnp.int32, (batch, step_rows), 0)
    )
    first_lanes = lax.broadcasted_iota(jnp.int32, (batch, 2 * rank), 1) < rank
    ids = jnp.concatenate([ids_ref[...]] * (2 * rank // examples), axis=1)
    place = lax.broadcasted_iota(jnp.int32, (id_rows, 2 * rank), 0) % 4
    digits = (jnp.broadcast_to(ids, (id_rows, 2 * rank)) >> (place * 8)) & 255
    digits = digits.astype(jnp.float32).astype(jnp.bfloat16)
    weights[0].wait()

    def project(index, beside):
        rng = pl.ds(index * half_rows, half_rows)
        act_copy, grad_copy = half_copies(index)
        act_copy.wait()
        act_proj[rng] = dot_nt(pin[...], act[rng]).T.astype(jnp.bfloat16)
        for step in beside[0::2]:
            rotate(step)
        if index == 0:
            weights[1].wait()
        grad_copy.wait()
        grad_proj[:, rng] = dot_nt(pout[...], grad[rng]).astype(jnp.bfloat16)
        for step in beside[1::2]:
            rotate(step)

    def rotate(step):
        rng = pl.ds(step * step_rows, step_rows)
        act_part, grad_part = act_proj[rng], grad_proj[:, rng]
        act_hi, act_lo = split_two(dot_nn(act_part, bin_hi) + dot_nn(act_part, bin_lo))
        grad_hi, grad_lo = split_two(dot_nn(bout_hi, grad_part) + dot_nn(bout_lo, grad_part))
        gt_ref[step, 0] = grad_hi.astype(jnp.float32)
        gt_ref[step, 1] = grad_lo.astype(jnp.float32)
        spread_hi, spread_lo = [
            jnp.concatenate([
                jnp.where(own_token, jnp.broadcast_to(gt_ref[step, part, pl.ds(u, 1)], (batch, step_rows)), 0.0)
                for u in range(rank)
            ], axis=0).astype(jnp.bfloat16)
            for part in range(2)
        ]
        wide = dot_nn(spread_hi, jnp.concatenate([act_hi, act_lo], axis=1))
        rotated = wide[:, :2 * rank] + wide[:, 2 * rank:] + dot_nn(spread_lo, act_hi)
        start = step * batch
        for u in range(half):
            value = jnp.where(
                first_lanes,
                rotated[u * batch:(u + 1) * batch],
                rotated[(u + half) * batch:(u + half + 1) * batch],
            ) * inverse[u:u + 1]
            feat[u, pl.ds(start, batch)] = value

    each = steps // halves
    for index in range(halves + 1):
        beside = list(range(max(index - 1, 0) * each, index * each))
        if index < halves:
            project(index, beside)
        else:
            for step in beside:
                rotate(step)
    depth = half // slices
    me = lax.axis_index("mem") // cores
    for index in range(slices):
        start = (me ^ index) * depth
        piece = feat[pl.ds(start, depth)].astype(jnp.bfloat16)
        out_refs[index][pl.ds(0, depth * examples)] = piece.reshape(depth * examples, 2 * rank)
        out_refs[index][pl.ds(depth * examples, id_rows)] = digits


def features(slices, activations, out_grads, proj_in, proj_out, basis_in, basis_out, eigen, doc_ids):
    examples, tokens, width = activations.shape
    rank = proj_in.shape[1]
    rows = examples * tokens
    half = rank // 2
    hbm = pl.BlockSpec(memory_space=pl.ANY)
    vmem = pl.BlockSpec(memory_space=pltpu.VMEM)
    return pl.pallas_call(
        functools.partial(feature_kernel, tokens, slices),
        out_shape=[
            pltpu.VMEM((half // slices * examples + id_rows, 2 * rank), jnp.bfloat16)
        ] * slices,
        in_specs=[hbm] * 8,
        out_specs=[vmem] * slices,
        scratch_shapes=[
            pltpu.VMEM((rows, width), jnp.bfloat16),
            pltpu.VMEM((rows, width), jnp.bfloat16),
            pltpu.VMEM((rank, width), jnp.bfloat16),
            pltpu.VMEM((rank, width), jnp.bfloat16),
            pltpu.VMEM((rank, rank), jnp.float32),
            pltpu.VMEM((rank, rank), jnp.float32),
            pltpu.VMEM((rank, rank), jnp.float32),
            pltpu.VMEM((1, examples), jnp.int32),
            pltpu.VMEM((rows, rank), jnp.bfloat16),
            pltpu.VMEM((rank, rows), jnp.bfloat16),
            pltpu.VMEM((examples // batch, 2, rank, batch * tokens), jnp.float32),
            pltpu.VMEM((half, examples, 2 * rank), jnp.float32),
            pltpu.SemaphoreType.DMA((halves,)),
            pltpu.SemaphoreType.DMA((halves,)),
            pltpu.SemaphoreType.DMA((2,)),
            pltpu.SemaphoreType.DMA((4,)),
        ],
        compiler_params=pltpu.CompilerParams(vmem_limit_bytes=60 * 2**20),
        cost_estimate=pl.CostEstimate(
            flops=4 * rows * width * rank, bytes_accessed=4 * rows * width, transcendentals=0),
        name="features",
    )(
        activations.reshape(rows, width), out_grads.reshape(rows, width),
        proj_in.T, proj_out.T, basis_in, basis_out, eigen, doc_ids.reshape(1, examples),
    )


def slice_order(slices):
    return list(range(slices))


def product_kernel(slices, pieces, examples, row_groups, column_groups, *refs):
    runs = slices // pieces
    slabs = row_groups - 1 + 2 * column_groups
    ins, outs = refs[:runs * slabs], refs[runs * slabs:runs * slabs + slices]
    column_stack, row_stack, masked = refs[runs * slabs + slices:]
    piece_rows, lanes = ins[0].shape
    piece_rows = piece_rows // pieces
    depth = (piece_rows - id_rows) // examples
    mem = lax.axis_index("mem")
    pair, core = mem // cores, mem % cores

    def place(stack, digits, row, ref, piece):
        start = pl.multiple_of(row * examples, examples)
        for part in range(depth):
            stack[pl.ds(start, examples), pl.ds(part * lanes, lanes)] = (
                ref[pl.ds(piece * piece_rows + part * examples, examples)])
        some = ref[pl.ds((piece + 1) * piece_rows - id_rows, id_rows)].astype(jnp.float32)
        some = jnp.concatenate([some] * (digits.shape[1] // lanes), axis=1)
        block = lax.broadcasted_iota(jnp.int32, digits.shape, 1) // examples
        return jnp.where(block == row, some, digits)

    column_digits = jnp.zeros((id_rows, column_stack.shape[0]), jnp.float32)
    row_digits = jnp.zeros((id_rows, row_stack.shape[0]), jnp.float32)
    for run in range(runs):
        part = ins[run * slabs:(run + 1) * slabs]
        columns, others = part[:column_groups], part[column_groups:2 * column_groups]
        rows = (columns[0],) + tuple(part[2 * column_groups:])
        for piece in range(pieces):
            place_of = pair ^ slice_order(slices)[run * pieces + piece]
            for group in range(column_groups):
                for ref, side in ((columns[group], core), (others[group], core ^ 1)):
                    column = (group * slices + place_of) * cores + side
                    column_digits = place(column_stack, column_digits, column, ref, piece)
            for group in range(row_groups):
                row = place_of * row_groups + group
                row_digits = place(row_stack, row_digits, row, rows[group], piece)

    def halves(digits):
        return (digits[0:1] + digits[1:2] * 256.0, digits[2:3] + digits[3:4] * 256.0)

    column_low, column_high = halves(column_digits)
    row_low, row_high = halves(row_digits)
    result = dot_nt(row_stack[...], column_stack[...])
    for start in range(0, row_stack.shape[0], 128):
        low, high = (
            jnp.broadcast_to(row[:, start:start + 128], (128, 128)).T[:, 0:1] for row in (row_low, row_high))
        value = result[start:start + 128]
        value = jnp.where((low == column_low) & (high == column_high), 0.0, value)
        masked[pl.ds(start, 128)] = value.astype(jnp.bfloat16)
    count = row_groups * examples
    for index in range(slices):
        start = pl.multiple_of((pair ^ index) * count, count)
        outs[index][...] = masked[pl.ds(start, count)]


def products(slabs, slices, pieces, examples, row_groups, column_groups):
    piece_rows, lanes = slabs[0].shape
    depth = (piece_rows // pieces - id_rows) // examples
    vmem = pl.BlockSpec(memory_space=pltpu.VMEM)
    rows, cols = row_groups * slices * examples, column_groups * slices * cores * examples
    return pl.pallas_call(
        functools.partial(product_kernel, slices, pieces, examples, row_groups, column_groups),
        out_shape=[jax.ShapeDtypeStruct((row_groups * examples, cols), jnp.bfloat16)] * slices,
        in_specs=[vmem] * len(slabs),
        out_specs=[vmem] * slices,
        scratch_shapes=[
            pltpu.VMEM((cols, depth * lanes), jnp.bfloat16),
            pltpu.VMEM((rows, depth * lanes), jnp.bfloat16),
            pltpu.VMEM((rows, cols), jnp.bfloat16),
        ],
        compiler_params=pltpu.CompilerParams(vmem_limit_bytes=40 * 2**20),
        cost_estimate=pl.CostEstimate(
            flops=2 * rows * cols * depth * lanes, bytes_accessed=4 * rows * cols, transcendentals=0),
        name="products",
    )(*slabs)


def total_kernel(slices, *refs):
    parts, outs = refs[:slices], refs[slices:]
    examples = outs[0].shape[0]
    for group, out in enumerate(outs):
        rng = pl.ds(group * examples, examples)
        out[...] = sum(part[rng].astype(jnp.float32) for part in parts).astype(out.dtype)


def totals(parts, examples):
    rows, cols = parts[0].shape
    groups = rows // examples
    vmem = pl.BlockSpec(memory_space=pltpu.VMEM)
    return pl.pallas_call(
        functools.partial(total_kernel, len(parts)),
        out_shape=[
            jax.ShapeDtypeStruct((examples, cols), jnp.bfloat16 if group else jnp.float32)
            for group in range(groups)
        ],
        in_specs=[vmem] * len(parts),
        out_specs=[vmem] * groups,
        compiler_params=pltpu.CompilerParams(vmem_limit_bytes=40 * 2**20),
        cost_estimate=pl.CostEstimate(
            flops=rows * cols * len(parts), bytes_accessed=8 * rows * cols, transcendentals=0),
        name="totals",
    )(*parts)


def finish_kernel(factor, column_groups, *refs):
    parts, out_ref = refs[:-1], refs[-1]
    cols = parts[0].shape[1]
    width = cols // column_groups
    grp = lax.axis_index("grp")
    for row_step, part in enumerate(parts):
        value = part[...].astype(jnp.float32) * factor
        for column_step in range(column_groups):
            start = (grp ^ row_step ^ (column_step * len(parts))) * width
            out_ref[:, pl.ds(pl.multiple_of(start, width), width)] = (
                value[:, column_step * width:(column_step + 1) * width])


def finish(parts, column_groups, factor):
    examples, cols = parts[0].shape
    vmem = pl.BlockSpec(memory_space=pltpu.VMEM)
    return pl.pallas_call(
        functools.partial(finish_kernel, factor, column_groups),
        out_shape=jax.ShapeDtypeStruct((examples, len(parts) * cols), jnp.float32),
        in_specs=[vmem] * len(parts),
        out_specs=vmem,
        compiler_params=pltpu.CompilerParams(vmem_limit_bytes=40 * 2**20),
        cost_estimate=pl.CostEstimate(
            flops=8 * examples * cols, bytes_accessed=16 * examples * cols, transcendentals=0),
        name="finish",
    )(*parts)


def swap(value, axis, size, distance):
    if distance == 0:
        return value
    return lax.ppermute(value, axis, [(place, place ^ distance) for place in range(size)])


def on_device(members, groups, activations, out_grads, proj_in, proj_out, basis_in, basis_out, eigen, doc_ids):
    examples, tokens, width = activations.shape
    rank = proj_in.shape[1]
    factor = 1.0 / (tokens * rank)
    slices = members // cores
    runs = 2
    pieces = slices // runs
    row_groups = 1 << ((groups.bit_length() - 1) // 2)
    column_groups = groups // row_groups
    feat = features(slices, activations, out_grads, proj_in, proj_out, basis_in, basis_out, eigen, doc_ids)
    got = [swap(feat[index], "mem", members, cores * index) for index in slice_order(slices)]
    slabs = []
    for run in range(runs):
        slab = jnp.concatenate(got[run * pieces:(run + 1) * pieces], axis=0)
        if run:
            slab, slabs[column_groups] = lax.optimization_barrier((slab, slabs[column_groups]))
        columns = [swap(slab, "grp", groups, row_groups * step) for step in range(column_groups)]
        rows = [swap(slab, "grp", groups, step) for step in range(1, row_groups)]
        held = columns[1:]
        if run + 1 < runs:
            held = lax.optimization_barrier((*held, *rows))[:column_groups - 1]
        others = [swap(column, "mem", members, 1) for column in (slab, *held)]
        slabs += columns + others + rows
    partial = products(slabs, slices, pieces, examples, row_groups, column_groups)
    parts = [partial[0]] + [
        swap(partial[index], "mem", members, cores * index) for index in reversed(range(1, slices))]
    sums = totals(parts, examples)
    sums = [swap(value, "grp", groups, step) for step, value in enumerate(sums)]
    return finish(sums, column_groups, factor)


def solution(mesh):
    return jax.shard_map(
        functools.partial(on_device, mesh.shape["mem"], mesh.shape["grp"]),
        mesh=mesh,
        in_specs=(
            P(("grp", "mem"), None, None),
            P(("grp", "mem"), None, None),
            P(),
            P(),
            P(),
            P(),
            P(),
            P(("grp", "mem")),
        ),
        out_specs=P(("grp", "mem"), None),
        check_vma=False,
    )
```
